32 devices in a mesh: seq: 2 (over y), fsdp: 16 (over z, x, core).
Axes of the slice: x: 2, y: 2, z: 4, core: 2. Of those that a mesh axis runs over, the one named last changes fastest.
Arguments:
- hidden: bfloat16 [16, 1024, 768], P('fsdp', 'seq'), may hold values from -6 to 6
- query_in: bfloat16 [16, 256, 768], P('fsdp', 'seq'), may hold values from -6 to 6
- memory: bfloat16 [16, 384, 768], P('fsdp', 'seq'), may hold values from -6 to 6
- segment_ids: int32 [16, 1408], P('fsdp'), may hold values from 0 to 2, never falling along the last dimension, each value on 1 to 704 neighbouring positions
- block_order: int32 [16, 4], P('fsdp'), may hold values from 0 to 3, each once within a row
- memory_valid: int32 [16, 384], P('fsdp'), may hold values 0 or 1
- w_query: bfloat16 [768, 768], P('fsdp'), may hold values from -0.21875 to 0.21875
- w_key: bfloat16 [768, 768], P('fsdp'), may hold values from -0.21875 to 0.21875
- w_value: bfloat16 [768, 768], P('fsdp'), may hold values from -0.21875 to 0.21875
- w_out: bfloat16 [768, 768], P('fsdp'), may hold values from -1.75 to 1.75
- w_rel: bfloat16 [768, 768], P('fsdp', 'seq'), may hold values from -0.21875 to 0.21875
- rel_biases: bfloat16 [3, 768], P(None, ('seq', 'fsdp')), may hold values from -3 to 3
- seg_embed: bfloat16 [2, 768], P(None, ('seq', 'fsdp')), may hold values from -3 to 3
- w_inner: bfloat16 [768, 3072], P('fsdp'), may hold values from -0.21875 to 0.21875
- b_inner: bfloat16 [3072], P('fsdp'), may hold values from -3 to 3
- w_outer: bfloat16 [3072, 768], P('fsdp'), may hold values from -0.109375 to 0.109375
- b_outer: bfloat16 [768], P('fsdp'), may hold values from -2 to 2
- norm_gains: bfloat16 [2, 768], P(None, 'fsdp'), may hold values from 0.5 to 1.5
- norm_biases: bfloat16 [2, 768], P(None, 'fsdp'), may hold values from -2 to 2
- grad_hidden_out: bfloat16 [16, 1024, 768], P('fsdp', 'seq'), may hold values from -6 to 6
- grad_query_out: bfloat16 [16, 256, 768], P('fsdp', 'seq'), may hold values from -6 to 6
Outputs:
- hidden_out: bfloat16 [16, 1024, 768], P('fsdp', 'seq')
- query_out: bfloat16 [16, 256, 768], P('fsdp', 'seq')
- grad_hidden: float32 [16, 1024, 768], P('fsdp', 'seq')
- grad_query: float32 [16, 256, 768], P('fsdp', 'seq')
- grad_w_query: float32 [768, 768], P(('seq', 'fsdp'))
- grad_w_key: float32 [768, 768], P(('seq', 'fsdp'))
- grad_w_value: float32 [768, 768], P(('seq', 'fsdp'))
- grad_w_out: float32 [768, 768], P(('seq', 'fsdp'))
- grad_w_rel: float32 [768, 768], P('fsdp', 'seq')
- grad_rel_biases: float32 [3, 768], P(None, ('seq', 'fsdp'))
- grad_seg_embed: float32 [2, 768], P(None, ('seq', 'fsdp'))
- grad_w_inner: float32 [768, 3072], P(('seq', 'fsdp'))
- grad_b_inner: float32 [3072], P(('seq', 'fsdp'))
- grad_w_outer: float32 [3072, 768], P(('seq', 'fsdp'))
- grad_b_outer: float32 [768], P(('seq', 'fsdp'))
- grad_norm_gains: float32 [2, 768], P(None, ('seq', 'fsdp'))
- grad_norm_biases: float32 [2, 768], P(None, ('seq', 'fsdp'))
The draws below stay inside these ranges and needn't reach their ends.
Inputs may be any that keep to these rules, and one draw needn't show every extreme that they name: `segment_ids`: each row holds the segments of 384 memory slots, then of 1024 tokens, never falling. `block_order`: each row names each of the 4 blocks once.
All inputs are finite; a program needn't handle non-finite values. No bound on the sum of `memory_valid` on one device may be relied on, other than what follows from the above.
Results may differ from the reference program's by a relative error of at most 0.017.
Values may be sent and summed in bfloat16 or wider, within the bound.
No kernel may reach another device: no remote copies, remote signals or barrier semaphores. Data moves between devices by JAX's collectives and lax.ppermute only.
A program may use at most 256 MiB of HBM per device.

```python
import math
import jax
import jax.numpy as jnp
import numpy as np
from jax import lax

D = 768
DH = 64
F = 3072
BLOCK = 256
NBLK = 4
MEM = 384
L = 1024
SEQS = 16


def plant(values, rng, smallest, largest):
    index_at = [jax.random.randint(jax.random.fold_in(rng, axis), (), 0, length) for axis, length in enumerate(values.shape)]
    longest = values.shape.index(max(values.shape))
    beside = index_at[:longest] + [(index_at[longest] + 1) % values.shape[longest]] + index_at[longest + 1:]
    return values.at[tuple(index_at)].set(smallest).at[tuple(beside)].set(largest)


def steps_of(rng, extent, cuts, smallest, largest):
    factor_of, own = 1.0, jax.random.fold_in(rng, 6)
    for dim, shards_of in cuts:
        heights = jnp.exp(jax.random.uniform(jax.random.fold_in(own, dim), (shards_of,), jnp.float32, smallest / len(cuts), largest / len(cuts)))
        factor_of = factor_of * jnp.repeat(heights, extent[dim] // shards_of).reshape([-1 if axis == dim else 1 for axis in range(len(extent))])
    return factor_of


def profile(number_of, total, most, slope):
    weights = [(1 << 20) // math.isqrt(rank ** slope) + 1 for rank in range(2, number_of + 1)]
    spare, holding = total - most - (number_of - 1), [1] * (number_of - 1)
    while spare > 0:
        candidates = [i for i in range(number_of - 1) if holding[i] < most]
        pool, left = sum([weights[i] for i in candidates]), spare
        for i in candidates:
            addition = min(most - holding[i], max(1, left * weights[i] // pool), spare)
            holding[i] = holding[i] + addition
            spare = spare - addition
    return np.array([most] + holding)


def uneven(own_key, number_of, total, bound, skew):
    if number_of == 2:
        one = jax.random.randint(own_key, (), max(1, total - bound), min(bound, total - 1) + 1)
        return jnp.stack([one, total - one])
    lengths = jnp.asarray(profile(number_of, total, bound, skew), jnp.int32)
    pairs = (number_of - 1) // 2
    source_of, sink = lengths[1:1 + 2 * pairs:2], lengths[2:2 + 2 * pairs:2]
    slack = jnp.minimum(source_of - 1, bound - sink)
    moved = jax.random.randint(jax.random.fold_in(own_key, 1), (pairs,), 0, 1 << 20) % (slack + 1)
    lengths = lengths.at[1:1 + 2 * pairs:2].set(source_of - moved).at[2:2 + 2 * pairs:2].set(sink + moved)
    return lengths[jax.random.permutation(jax.random.fold_in(own_key, 2), number_of)]


def normal_values(own_key, extent, width, reach, cuts=(), dtype=jnp.bfloat16):
    drawn = width * jax.random.normal(own_key, extent, jnp.float32)
    if cuts:
        drawn = drawn * steps_of(own_key, extent, cuts, -0.22, 0.18)
    return jnp.clip(drawn, -reach, reach).astype(dtype)


def setup_inputs(seed: int = 0) -> dict:
    streams_of = jax.random.split(jax.random.key(seed), 22)
    return {
        "hidden": normal_values(streams_of[0], (SEQS, L, D), 1.0, 6.0, ((0, 16), (1, 2))),
        "query_in": normal_values(streams_of[1], (SEQS, BLOCK, D), 1.0, 6.0, ((0, 16), (1, 2))),
        "memory": normal_values(streams_of[2], (SEQS, MEM, D), 1.0, 6.0, ((0, 16), (1, 2))),
        "segment_ids": jax.vmap(lambda own: jnp.searchsorted(jnp.cumsum(uneven(own, 3, MEM + L, (MEM + L) // 2, 0)), jnp.arange(MEM + L), side="right"))(jax.random.split(streams_of[3], SEQS)).reshape((SEQS, MEM + L)).astype(jnp.int32),
        "block_order": jax.vmap(lambda own: jax.random.permutation(own, NBLK))(jax.random.split(streams_of[4], SEQS)).reshape((SEQS, NBLK)).astype(jnp.int32),
        "memory_valid": plant((jax.random.randint(streams_of[5], (SEQS, MEM), 0, 4) < 3).astype(jnp.int32), jax.random.fold_in(streams_of[5], 1), 0, 1),
        "w_query": normal_values(streams_of[6], (D, D), D ** -0.5, 0.21875, ((0, 16),)),
        "w_key": normal_values(streams_of[7], (D, D), D ** -0.5, 0.21875, ((0, 16),)),
        "w_value": normal_values(streams_of[8], (D, D), D ** -0.5, 0.21875, ((0, 16),)),
        "w_out": normal_values(streams_of[9], (D, D), (D // 64) ** -0.5, 1.75, ((0, 16),)),
        "w_rel": normal_values(streams_of[10], (D, D), D ** -0.5, 0.21875, ((0, 16), (1, 2))),
        "rel_biases": normal_values(streams_of[11], (3, D), 0.5, 3.0, ((1, 32),)),
        "seg_embed": normal_values(streams_of[12], (2, D), 0.5, 3.0, ((1, 32),)),
        "w_inner": normal_values(streams_of[13], (D, F), D ** -0.5, 0.21875, ((0, 16),)),
        "b_inner": normal_values(streams_of[14], (F,), 0.5, 3.0, ((0, 16),)),
        "w_outer": normal_values(streams_of[15], (F, D), F ** -0.5, 0.109375, ((0, 16),)),
        "b_outer": normal_values(streams_of[16], (D,), 0.3, 2.0, ((0, 16),)),
        "norm_gains": jnp.clip(1.0 + 0.1 * jax.random.normal(streams_of[17], (2, D), jnp.float32), 0.5, 1.5).astype(jnp.bfloat16),
        "norm_biases": normal_values(streams_of[18], (2, D), 0.3, 2.0, ((1, 16),)),
        "grad_hidden_out": normal_values(streams_of[19], (SEQS, L, D), 1.0, 6.0, ((0, 16), (1, 2))),
        "grad_query_out": normal_values(streams_of[20], (SEQS, BLOCK, D), 1.0, 6.0, ((0, 16), (1, 2))),
    }


EPSILON = 1e-05
NEGATIVE = -1e+30
SCORE_SCALE = 0.125
HIGHEST = lax.Precision.HIGHEST

@jax.custom_vjp
def low(v):
    return lax.optimization_barrier(v.astype(jnp.bfloat16)).astype(jnp.float32)

@jax.custom_vjp
def low_back(v):
    return v

def low_keep(v):
    return (low(v), None)

def low_pass(kept, grad):
    return (grad,)

def back_keep(v):
    return (v, None)

def back_low(kept, grad):
    return (low(grad),)
low.defvjp(low_keep, low_pass)
low_back.defvjp(back_keep, back_low)

def rounded(values):
    return low(low_back(values))

def product(left, right):
    return jnp.dot(left, right, precision=HIGHEST)

def layer_norm(values, gain, shift):
    center = values - lax.optimization_barrier(jnp.mean(values, -1, keepdims=True))
    spread = lax.optimization_barrier(jnp.mean(center * center, -1, keepdims=True))
    return center * lax.rsqrt(spread + EPSILON) * gain + shift

def gelu_tanh(values):
    return 0.5 * values * (1.0 + jnp.tanh(0.7978845608028654 * (values + 0.044715 * values * values * values)))

def sinusoid(row_count, width_all, farthest):
    distance = farthest - jnp.arange(row_count).astype(jnp.float32)
    frequency = 10000.0 ** (-jnp.arange(0, width_all, 2).astype(jnp.float32) / width_all)
    angles = distance[:, None] * frequency[None, :]
    return jnp.concatenate([jnp.sin(angles), jnp.cos(angles)], 1)

def seq_masks(seg_ids, order_row, mem_valid):
    block_ids = jnp.arange(NBLK).astype(jnp.int32)
    rank_of = lax.optimization_barrier(jnp.sum(block_ids[None, :] * (order_row[None, :] == block_ids[:, None]).astype(jnp.int32), 1))
    token_rank = jnp.repeat(rank_of, BLOCK)
    valid_row = (mem_valid == 1)[None, :]
    allow_content = jnp.concatenate([jnp.broadcast_to(valid_row, (L, MEM)), token_rank[None, :] <= token_rank[:, None]], 1)
    same_content = seg_ids[MEM:][:, None] == seg_ids[None, :]
    target_base = (order_row[NBLK - 1] * BLOCK).astype(jnp.int32)
    target_seg = lax.dynamic_slice_in_dim(seg_ids, (MEM + target_base).astype(jnp.int32), BLOCK)
    same_query = target_seg[:, None] == seg_ids[None, :]
    positions = target_base + jnp.arange(BLOCK).astype(jnp.int32)
    allow_query = jnp.concatenate([jnp.broadcast_to(valid_row, (BLOCK, MEM)), jnp.arange(L).astype(jnp.int32)[None, :] != positions[:, None]], 1)
    return (allow_content, same_content, allow_query, same_query, target_base)

def skew_rows(table_in, row_count, key_count):
    span_width = table_in.shape[1]
    flat_table = table_in.reshape(row_count * span_width)
    picked = flat_table[row_count - 1:row_count - 1 + row_count * (span_width - 1)]
    return picked.reshape(row_count, span_width - 1)[:, :key_count]

def attend_head(query_rows, key_rows, value_rows, rel_rows, bias_three, seg_pair, same_seg, allowed):
    row_count = query_rows.shape[0]
    key_count = key_rows.shape[0]
    query_w = low(query_rows + bias_three[0])
    query_r = low(query_rows + bias_three[1])
    query_s = query_rows + bias_three[2]
    content = product(query_w, key_rows.T)
    position = skew_rows(product(query_r, rel_rows.T), row_count, key_count)
    seg_scores = product(query_s, seg_pair.T)
    segment = jnp.where(same_seg, seg_scores[:, 0:1], seg_scores[:, 1:2])
    scores = low_back((content + position + segment) * SCORE_SCALE)
    scores = jnp.where(allowed, scores, NEGATIVE)
    row_max = lax.optimization_barrier(jnp.max(scores, -1, keepdims=True))
    exp_terms = jnp.exp(scores - row_max)
    attn_prob = exp_terms / lax.optimization_barrier(jnp.sum(exp_terms, -1, keepdims=True))
    return product(low(attn_prob), value_rows)

def attend_rows(query_three, first_row, same_seg, allowed, keys_three, values_three, rel_three, bias_three, seg_three):
    row_count = query_three.shape[0]
    key_count = keys_three.shape[0]
    rel_rows = lax.dynamic_slice_in_dim(rel_three, L - row_count - first_row, key_count + row_count - 1, 0)
    per_head = jax.vmap(attend_head, in_axes=(1, 1, 1, 1, 1, 1, None, None), out_axes=1)
    return per_head(query_three, keys_three, values_three, rel_rows, bias_three, seg_three, same_seg, allowed)

def one_sequence(params, hidden_seq, query_seq, memory_seq, seg_ids, order_row, mem_valid):
    w_query, w_key, w_value, w_out, w_rel, rel_biases, seg_embed, w_inner, b_inner, w_outer, b_outer, norm_gains, norm_biases = params
    heads_all = D // DH
    query_h = rounded(product(hidden_seq, w_query))
    key_h = rounded(product(hidden_seq, w_key))
    value_h = rounded(product(hidden_seq, w_value))
    query_g = rounded(product(query_seq, w_query))
    key_m = rounded(product(memory_seq, w_key))
    value_m = rounded(product(memory_seq, w_value))
    keys_three = jnp.concatenate([key_m, key_h], 0).reshape(MEM + L, heads_all, DH)
    values_three = jnp.concatenate([value_m, value_h], 0).reshape(MEM + L, heads_all, DH)
    pos_table = low(sinusoid(MEM + 2 * L - 1, D, MEM + L - 1))
    rel_three = rounded(product(pos_table, w_rel)).reshape(MEM + 2 * L - 1, heads_all, DH)
    bias_three = rel_biases.reshape(3, heads_all, DH)
    seg_three = seg_embed.reshape(2, heads_all, DH)
    allow_content, same_content, allow_query, same_query, target_base = seq_masks(seg_ids, order_row, mem_valid)
    block_rows = min(512, L)
    query_three = query_h.reshape(L, heads_all, DH)

    def content_block(block_index):
        first_row = (block_index * block_rows).astype(jnp.int32)
        return attend_rows(lax.dynamic_slice_in_dim(query_three, first_row, block_rows, 0), first_row, lax.dynamic_slice_in_dim(same_content, first_row, block_rows, 0), lax.dynamic_slice_in_dim(allow_content, first_row, block_rows, 0), keys_three, values_three, rel_three, bias_three, seg_three)
    content_att = lax.map(jax.checkpoint(content_block), jnp.arange(L // block_rows).astype(jnp.int32)).reshape(L, D)

    def query_block(target_three):
        return attend_rows(target_three, target_base, same_query, allow_query, keys_three, values_three, rel_three, bias_three, seg_three)
    query_att = jax.checkpoint(query_block)(query_g.reshape(BLOCK, heads_all, DH)).reshape(BLOCK, D)
    attn_h = rounded(content_att)
    attn_g = rounded(query_att)

    def finish(attn_rows, resid_rows):
        mixed_rows = low_back(product(attn_rows, w_out))
        first_norm = layer_norm(mixed_rows + resid_rows, norm_gains[0], norm_biases[0])
        hidden_pre = low_back(product(low(first_norm), w_inner) + b_inner)
        outer_rows = low_back(product(low(gelu_tanh(hidden_pre)), w_outer) + b_outer)
        return layer_norm(outer_rows + first_norm, norm_gains[1], norm_biases[1])
    return (finish(attn_h, hidden_seq), finish(attn_g, query_seq))

def reference(hidden, query_in, memory, segment_ids, block_order, memory_valid, w_query, w_key, w_value, w_out, w_rel, rel_biases, seg_embed, w_inner, b_inner, w_outer, b_outer, norm_gains, norm_biases, grad_hidden_out, grad_query_out):
    params = tuple((weight.astype(jnp.float32) for weight in (w_query, w_key, w_value, w_out, w_rel, rel_biases, seg_embed, w_inner, b_inner, w_outer, b_outer, norm_gains, norm_biases)))

    def per_sequence(running, seq_items):
        hidden_seq, query_seq, memory_seq, seg_ids, order_row, mem_valid, grad_h, grad_g = seq_items
        memory_f = memory_seq.astype(jnp.float32)

        def forward(weights, hidden_f, query_f):
            return one_sequence(weights, hidden_f, query_f, memory_f, seg_ids, order_row, mem_valid)
        outputs, pull_back = jax.vjp(forward, params, hidden_seq.astype(jnp.float32), query_seq.astype(jnp.float32))
        grad_params, grad_hid, grad_qry = pull_back((grad_h.astype(jnp.float32), grad_g.astype(jnp.float32)))
        running = jax.tree.map(lambda left, right: left + right, running, grad_params)
        return (running, (outputs[0].astype(jnp.bfloat16), outputs[1].astype(jnp.bfloat16), grad_hid, grad_qry))
    zero_grads = jax.tree.map(jnp.zeros_like, params)
    totals, per_seq = lax.scan(per_sequence, zero_grads, (hidden, query_in, memory, segment_ids, block_order, memory_valid, grad_hidden_out, grad_query_out))
    return (per_seq[0], per_seq[1], per_seq[2], per_seq[3], totals[0], totals[1], totals[2], totals[3], totals[4], totals[5], totals[6], totals[7], totals[8], totals[9], totals[10], totals[11], totals[12])
```

```python
import jax
import jax.numpy as jnp
from jax import lax
from jax.experimental import pallas as pl
from jax.experimental.pallas import tpu as pltpu
from jax.sharding import PartitionSpec as P

DH = 64
BLOCK = 256
NBLK = 4
MEM = 384
L = 1024
LANES = 128

QROW = L
MROW = L + BLOCK
ROWS = L + BLOCK + MEM
KEYS = MEM + L
SPAN_M = MEM + BLOCK
SPAN_T = 2 * BLOCK
REL_M = L - BLOCK
REL_T = MEM + L - BLOCK
REL_ROWS = MEM + 2 * L

EPSILON = 1e-05
NEGATIVE = -1e30
SCORE_SCALE = 0.125
EXP2_SCALE = SCORE_SCALE * 1.4426950408889634
STEPS = NBLK + 1
BF = jnp.bfloat16
F32 = jnp.float32


def product(left, right):
    return jnp.dot(left, right, preferred_element_type=F32)


def inner_rows(left, right):
    return lax.dot_general(left, right, (((1,), (1,)), ((), ())), preferred_element_type=F32)


def inner_cols(left, right):
    return lax.dot_general(left, right, (((0,), (0,)), ((), ())), preferred_element_type=F32)


def layer_norm(values, gain, shift):
    center = values - jnp.mean(values, -1, keepdims=True)
    spread = jnp.mean(center * center, -1, keepdims=True)
    return center * lax.rsqrt(spread + EPSILON) * gain + shift


def gelu_tanh(values):
    return (
        0.5
        * values
        * (1.0 + jnp.tanh(0.7978845608028654 * (values + 0.044715 * values * values * values)))
    )


def sinusoid(row_count, width_all, farthest):
    distance = farthest - jnp.arange(row_count).astype(F32)
    frequency = 10000.0 ** (-jnp.arange(0, width_all, 2).astype(F32) / width_all)
    angles = distance[:, None] * frequency[None, :]
    return jnp.concatenate([jnp.sin(angles), jnp.cos(angles)], 1)


def split_low(values):
    high = values.astype(BF).astype(F32)
    return high, values - high


def place(step, order_ref):
    last = jnp.minimum(step, NBLK - 1)
    block = order_ref[last]
    row = jnp.where(step < NBLK, block, NBLK) * BLOCK
    return block, pl.multiple_of(row, BLOCK), last


def row_terms(q_ref, kx_ref, par_ref, row):
    query = q_ref[pl.ds(row, BLOCK), :].astype(F32)
    marks = kx_ref[pl.ds(row, BLOCK), :].astype(F32)
    return query + par_ref[0:1, :], query + par_ref[1:2, :], query + par_ref[2:3, :], marks


def forward_kernel(
    order_ref,
    q_ref,
    k_ref,
    v_ref,
    rel_ref,
    kx_ref,
    par_ref,
    att_ref,
    exp_ref,
    inv_ref,
    kcat_ref,
    vcat_ref,
    score_ref,
    lhs_ref,
    qr_ref,
):
    step = pl.program_id(1)

    @pl.when(step == 0)
    def _():
        kcat_ref[:, :LANES] = k_ref[...]
        kcat_ref[:, LANES:] = kx_ref[...]
        vcat_ref[:, :LANES] = v_ref[...]
        vcat_ref[:, LANES:] = jnp.ones((ROWS, LANES), BF)

    block, row, last = place(step, order_ref)
    lane = lax.broadcasted_iota(jnp.int32, (BLOCK, LANES), 1)
    query_w, query_r, query_s, marks = row_terms(q_ref, kx_ref, par_ref, row)
    same, other = query_s * par_ref[3:4, :], query_s * par_ref[4:5, :]
    for head in range(2):
        mine = (lane < DH) == (head == 0)
        other_sum = jnp.sum(jnp.where(mine, other, 0.0), -1, keepdims=True)
        diff = jnp.sum(jnp.where(mine, same, 0.0), -1, keepdims=True) - other_sum
        diff_high, diff_low = split_low(diff)
        other_high, other_low = split_low(other_sum)
        extra = jnp.where(lane < 3, marks * diff_high, jnp.where(lane < 6, marks * diff_low, 0.0))
        extra = jnp.where(lane == 6, other_high, jnp.where(lane == 7, other_low, extra))
        extra = jnp.where(lane == 8, NEGATIVE, extra)
        lhs_ref[head, :, :LANES] = jnp.where(mine, query_w, 0.0).astype(BF)
        lhs_ref[head, :, LANES:] = extra.astype(BF)
        qr_ref[head] = jnp.where(mine, query_r, 0.0).astype(BF)

    def scores(head, key_row, key_count, rel_row):
        content = inner_rows(lhs_ref[head], kcat_ref[pl.ds(key_row, key_count), :])
        span = key_count + BLOCK
        position = inner_rows(qr_ref[head], rel_ref[pl.ds(rel_row, span), :])
        position = pltpu.roll(position, span - BLOCK + 1, 1, stride=1, stride_axis=0)
        return content + position[:, :key_count]

    def widest(running, tile):
        for at in range(0, tile.shape[1], LANES):
            piece = tile[:, at : at + LANES]
            running = piece if running is None else jnp.maximum(running, piece)
        return running

    tops = []
    rel_row = pl.multiple_of(REL_M - BLOCK * block, BLOCK)
    for head in range(2):
        tile = scores(head, MROW, MEM, rel_row)
        score_ref[head, :, :MEM] = tile
        tops.append(widest(None, tile))

    def column(at):
        return pl.multiple_of(MEM + BLOCK * at, LANES)

    def token_tile(at, tops):
        key_block = order_ref[at]
        key_row = pl.multiple_of(BLOCK * key_block, BLOCK)
        rel_row = pl.multiple_of(REL_T + BLOCK * (key_block - block), LANES)
        fresh = []
        for head in range(2):
            tile = scores(head, key_row, BLOCK, rel_row)
            score_ref[head, :, pl.ds(column(at), BLOCK)] = tile
            fresh.append(widest(tops[head], tile))
        return tuple(fresh)

    tops = lax.fori_loop(0, last, token_tile, tuple(tops))
    across = lax.broadcasted_iota(jnp.int32, (BLOCK, BLOCK), 0) - lax.broadcasted_iota(
        jnp.int32, (BLOCK, BLOCK), 1
    )
    hidden_at = jnp.where(step < NBLK, BLOCK, 0)
    own_row = pl.multiple_of(BLOCK * block, BLOCK)
    peaks = []
    for head in range(2):
        tile = scores(head, own_row, BLOCK, REL_T)
        tile = jnp.where(across == hidden_at, NEGATIVE, tile)
        score_ref[head, :, pl.ds(column(last), BLOCK)] = tile
        peaks.append(jnp.max(widest(tops[head], tile), -1, keepdims=True))

    def weigh(head, at, key_row, key_count):
        tile = score_ref[head, :, pl.ds(at, key_count)]
        low = jnp.exp2((tile - peaks[head]) * EXP2_SCALE).astype(BF)
        exp_ref[head, :, pl.ds(at, key_count)] = low
        return product(low, vcat_ref[pl.ds(key_row, key_count), :])

    sums = tuple(weigh(head, 0, MROW, MEM) for head in range(2))

    def token_sum(at, sums):
        key_row = pl.multiple_of(BLOCK * order_ref[at], BLOCK)
        return tuple(sums[head] + weigh(head, column(at), key_row, BLOCK) for head in range(2))

    sums = lax.fori_loop(0, last + 1, token_sum, sums)
    first = lane < DH
    inverse = 1.0 / jnp.where(first, sums[0][:, LANES:], sums[1][:, LANES:])
    total = jnp.where(first, sums[0][:, :LANES], sums[1][:, :LANES])
    att_ref[pl.ds(row, BLOCK), :] = (total * inverse).astype(BF)
    inv_ref[pl.ds(row, BLOCK), :] = inverse


def backward_kernel(
    order_ref,
    q_ref,
    k_ref,
    v_ref,
    rel_ref,
    kx_ref,
    par_ref,
    grad_ref,
    att_ref,
    inv_ref,
    exp_ref,
    dq_ref,
    dk_ref,
    dv_ref,
    drel_ref,
    dpar_ref,
    kcat_ref,
    vcat_ref,
    flip_ref,
    lhs_ref,
    qwt_ref,
    qrt_ref,
    gt_ref,
    dkt_ref,
    dvt_ref,
    drelt_ref,
    accw_ref,
    accr_ref,
):
    step = pl.program_id(1)

    @pl.when(step == 0)
    def _():
        kcat_ref[:, :LANES] = k_ref[...]
        kcat_ref[:, LANES:] = kx_ref[...]
        vcat_ref[:, :LANES] = (v_ref[...].astype(F32) * SCORE_SCALE).astype(BF)
        vcat_ref[:, LANES:] = jnp.full((ROWS, LANES), SCORE_SCALE, BF)
        up = lax.broadcasted_iota(jnp.int32, (BLOCK, BLOCK), 0)
        down = lax.broadcasted_iota(jnp.int32, (BLOCK, BLOCK), 1)
        flip_ref[...] = jnp.where(up + down == BLOCK - 1, 1.0, 0.0).astype(BF)
        dkt_ref[...] = jnp.zeros_like(dkt_ref)
        dvt_ref[...] = jnp.zeros_like(dvt_ref)
        drelt_ref[...] = jnp.zeros_like(drelt_ref)
        dpar_ref[...] = jnp.zeros_like(dpar_ref)

    block, row, last = place(step, order_ref)
    lane = lax.broadcasted_iota(jnp.int32, (BLOCK, LANES), 1)
    query_w, query_r, query_s, marks = row_terms(q_ref, kx_ref, par_ref, row)
    grad_low = (grad_ref[pl.ds(row, BLOCK), :].astype(F32) * inv_ref[pl.ds(row, BLOCK), :]).astype(
        BF
    )
    grad = grad_low.astype(F32)
    dots = grad * att_ref[pl.ds(row, BLOCK), :].astype(F32)
    for head in range(2):
        mine = (lane < DH) == (head == 0)
        high, low = split_low(-jnp.sum(jnp.where(mine, dots, 0.0), -1, keepdims=True))
        extra = jnp.where(lane == 0, high, jnp.where(lane == 1, low, 0.0))
        lhs_ref[head, :, :LANES] = jnp.where(mine, grad, 0.0).astype(BF)
        lhs_ref[head, :, LANES:] = extra.astype(BF)
    flip = flip_ref[...]
    qwt_ref[...] = query_w.astype(BF).astype(F32).T.astype(BF)
    qrt_ref[...] = product(flip, query_r.astype(BF)).T.astype(BF)
    gt_ref[...] = grad.T.astype(BF)
    accw_ref[...] = jnp.zeros_like(accw_ref)
    accr_ref[...] = jnp.zeros_like(accr_ref)

    def tile(head, at, key_row, key_count, rel_row):
        span = key_count + BLOCK
        own = slice(DH * head, DH * head + DH)
        keys = pl.ds(key_row, key_count)
        span_at = pl.ds(rel_row, span)
        probs = exp_ref[head, :, pl.ds(at, key_count)]
        slope = inner_rows(lhs_ref[head], vcat_ref[keys, :])
        scaled = (probs.astype(F32) * slope).astype(BF)
        accw_ref[head] += product(scaled, kcat_ref[keys, :])
        dkt_ref[own, keys] += product(qwt_ref[own, :], scaled)
        dvt_ref[own, keys] += product(gt_ref[own, :], probs)
        turned = product(flip, scaled).astype(BF)
        turned = jnp.concatenate([turned, jnp.zeros((BLOCK, BLOCK), BF)], 1)
        turned = pltpu.roll(turned, 0, 1, stride=1, stride_axis=0)
        accr_ref[head] += product(turned, rel_ref[span_at, :])
        drelt_ref[own, span_at] += product(qrt_ref[own, :], turned)

    rel_row = pl.multiple_of(REL_M - BLOCK * block, BLOCK)
    for head in range(2):
        tile(head, 0, MROW, MEM, rel_row)

    def token_tile(at, carry):
        key_block = order_ref[at]
        key_row = pl.multiple_of(BLOCK * key_block, BLOCK)
        rel_row = pl.multiple_of(REL_T + BLOCK * (key_block - block), LANES)
        for head in range(2):
            tile(head, pl.multiple_of(MEM + BLOCK * at, LANES), key_row, BLOCK, rel_row)
        return carry

    lax.fori_loop(0, last + 1, token_tile, 0)

    first = lane < DH
    grad_w = jnp.where(first, accw_ref[0, :, :LANES], accw_ref[1, :, :LANES])
    high, low = split_low(jnp.where(first, accr_ref[0], accr_ref[1]))
    grad_r = product(flip, high.astype(BF)) + product(flip, low.astype(BF))
    same_sums, other_sums = [], []
    for head in range(2):
        sums = accw_ref[head, :, LANES:]
        same_sums.append(jnp.sum(jnp.where(lane < 3, marks * sums, 0.0), -1, keepdims=True))
        total = jnp.sum(jnp.where(lane == 6, sums, 0.0), -1, keepdims=True)
        other_sums.append(total - same_sums[head])
    same = jnp.where(first, same_sums[0], same_sums[1])
    other = jnp.where(first, other_sums[0], other_sums[1])
    grad_s = same * par_ref[3:4, :] + other * par_ref[4:5, :]
    dq_ref[pl.ds(row, BLOCK), :] = (grad_w + grad_r + grad_s).astype(BF)
    for at, rows in enumerate((grad_w, grad_r, grad_s, same * query_s, other * query_s)):
        dpar_ref[at : at + 1, :] += jnp.sum(rows, 0, keepdims=True)

    @pl.when(step == STEPS - 1)
    def _():
        dk_ref[...] = dkt_ref[...].T.astype(BF)
        dv_ref[...] = dvt_ref[...].T.astype(BF)
        drel_ref[...] = drelt_ref[...].T.astype(BF)


def attention_specs(pairs):
    def column(rows, first):
        return pl.BlockSpec((rows, LANES), lambda pair, step, order: (0, first + pair))

    shared = pl.BlockSpec((ROWS, LANES), lambda pair, step, order: (0, 0))
    ins = [
        column(ROWS, 0),
        column(ROWS, pairs),
        column(ROWS, 2 * pairs),
        column(REL_ROWS, 0),
        shared,
        column(8, 0),
    ]
    exps = pl.BlockSpec(
        (None, None, 2, BLOCK, KEYS), lambda pair, step, order: (pair, step, 0, 0, 0)
    )
    return column, ins, exps


PARAMS = dict(
    dimension_semantics=("arbitrary", "arbitrary"), vmem_limit_bytes=48 * 1024 * 1024
)


def attention_forward(order, qkv, rel, marks, par):
    pairs = rel.shape[1] // LANES
    column, ins, exps = attention_specs(pairs)
    width = pairs * LANES
    return pl.pallas_call(
        forward_kernel,
        grid_spec=pltpu.PrefetchScalarGridSpec(
            num_scalar_prefetch=1,
            grid=(pairs, STEPS),
            in_specs=ins,
            out_specs=[column(MROW, 0), exps, column(MROW, 0)],
            scratch_shapes=[
                pltpu.VMEM((ROWS, 2 * LANES), BF),
                pltpu.VMEM((ROWS, 2 * LANES), BF),
                pltpu.VMEM((2, BLOCK, KEYS), F32),
                pltpu.VMEM((2, BLOCK, 2 * LANES), BF),
                pltpu.VMEM((2, BLOCK, LANES), BF),
            ],
        ),
        out_shape=[
            jax.ShapeDtypeStruct((MROW, width), BF),
            jax.ShapeDtypeStruct((pairs, STEPS, 2, BLOCK, KEYS), BF),
            jax.ShapeDtypeStruct((MROW, width), F32),
        ],
        compiler_params=pltpu.CompilerParams(**PARAMS),
    )(order, qkv, qkv, qkv, rel, marks, par)


def attention_backward(order, qkv, rel, marks, par, grad, att, inverse, exps_in):
    pairs = rel.shape[1] // LANES
    column, ins, exps = attention_specs(pairs)
    width = pairs * LANES
    return pl.pallas_call(
        backward_kernel,
        grid_spec=pltpu.PrefetchScalarGridSpec(
            num_scalar_prefetch=1,
            grid=(pairs, STEPS),
            in_specs=ins + [column(MROW, 0)] * 3 + [exps],
            out_specs=[
                column(MROW, 0),
                column(ROWS, 0),
                column(ROWS, 0),
                column(REL_ROWS, 0),
                column(8, 0),
            ],
            scratch_shapes=[
                pltpu.VMEM((ROWS, 2 * LANES), BF),
                pltpu.VMEM((ROWS, 2 * LANES), BF),
                pltpu.VMEM((BLOCK, BLOCK), BF),
                pltpu.VMEM((2, BLOCK, 2 * LANES), BF),
                pltpu.VMEM((LANES, BLOCK), BF),
                pltpu.VMEM((LANES, BLOCK), BF),
                pltpu.VMEM((LANES, BLOCK), BF),
                pltpu.VMEM((LANES, ROWS), F32),
                pltpu.VMEM((LANES, ROWS), F32),
                pltpu.VMEM((LANES, REL_ROWS), F32),
                pltpu.VMEM((2, BLOCK, 2 * LANES), F32),
                pltpu.VMEM((2, BLOCK, LANES), F32),
            ],
        ),
        out_shape=[
            jax.ShapeDtypeStruct((MROW, width), BF),
            jax.ShapeDtypeStruct((ROWS, width), BF),
            jax.ShapeDtypeStruct((ROWS, width), BF),
            jax.ShapeDtypeStruct((REL_ROWS, width), BF),
            jax.ShapeDtypeStruct((8, width), F32),
        ],
        compiler_params=pltpu.CompilerParams(**PARAMS),
    )(order, qkv, qkv, qkv, rel, marks, par, grad, att, inverse, exps_in)


def swap(values):
    return lax.ppermute(values, "seq", [(0, 1), (1, 0)])


def pad_to(values, count):
    return jnp.pad(values, (0, count - values.shape[0]))


def shards(
    hidden,
    query_in,
    memory,
    segment_ids,
    block_order,
    memory_valid,
    w_query,
    w_key,
    w_value,
    w_out,
    w_rel,
    rel_biases,
    seg_embed,
    w_inner,
    b_inner,
    w_outer,
    b_outer,
    norm_gains,
    norm_biases,
    grad_hidden_out,
    grad_query_out,
):
    side = lax.axis_index("seq")
    groups = lax.axis_size("fsdp")
    half, width = hidden.shape[1:]
    target_half = query_in.shape[1]
    memory_half = memory.shape[1]
    head_width = w_rel.shape[1]
    shard_rows = w_query.shape[0]
    ffn_width = w_inner.shape[1]
    own_rows = half + target_half

    def own_columns(weight):
        return lax.dynamic_slice_in_dim(weight, side * head_width, head_width, 1)

    smalls = (rel_biases, seg_embed, b_inner, b_outer, norm_gains, norm_biases)
    small_flat = pad_to(jnp.concatenate([s.reshape(-1) for s in smalls]), shard_rows * LANES)
    packed = jnp.concatenate(
        [
            own_columns(w_query),
            own_columns(w_key),
            own_columns(w_value),
            w_rel,
            small_flat.reshape(shard_rows, LANES),
        ],
        1,
    )
    packed = lax.all_gather(packed, "fsdp", axis=0, tiled=True)
    mixed = lax.all_gather(
        jnp.concatenate([w_out, w_inner], 1), "fsdp", axis=0, tiled=True
    )
    full_outer = lax.all_gather(w_outer, "fsdp", axis=0, tiled=True)
    full_out, full_inner = mixed[:, :width], mixed[:, width:]
    head_weights = packed[:, : 3 * head_width]
    rel_weight = packed[:, 3 * head_width : 4 * head_width]
    small_all = packed[:, 4 * head_width :].reshape(groups, shard_rows * LANES).astype(F32)

    def unpack():
        found, at = [], 0
        for small in smalls:
            piece = small_all[:, at : at + small.size].reshape((groups,) + small.shape)
            found.append(jnp.moveaxis(piece, 0, -2).reshape(small.shape[:-1] + (-1,)))
            at += small.size
        return found

    all_biases, all_seg, inner_bias, outer_bias, gains, shifts = unpack()

    mine = jnp.concatenate([hidden[0], query_in[0], memory[0]], 0)
    theirs = swap(mine)
    low = jnp.where(side == 0, mine, theirs)
    high = jnp.where(side == 0, theirs, mine)
    cuts = ((0, half), (half, own_rows), (own_rows, own_rows + memory_half))
    stacked = jnp.concatenate([part[a:b] for a, b in cuts for part in (low, high)], 0)

    qkv = product(stacked, head_weights).astype(BF)
    pos_table = sinusoid(REL_ROWS, width, MEM + L - 1).astype(BF)
    rel = product(pos_table, rel_weight).astype(BF)
    par = jnp.concatenate([all_biases, all_seg, jnp.zeros((3, head_width), F32)], 0)
    order = block_order[0]
    segs = segment_ids[0]
    target_seg = lax.dynamic_slice_in_dim(segs, MEM + order[NBLK - 1] * BLOCK, BLOCK)
    seg_rows = jnp.concatenate([segs[MEM:], target_seg, segs[:MEM]])
    invalid = jnp.concatenate([jnp.zeros((MROW,), jnp.int32), (memory_valid[0] != 1).astype(jnp.int32)])
    lane = jnp.arange(LANES)[None, :]
    marks = jnp.where(lane < 6, seg_rows[:, None] == lane % 3, (lane == 6) | (lane == 7))
    marks = jnp.where(lane == 8, invalid[:, None] == 1, marks).astype(BF)

    att, exps, inverse = attention_forward(order, qkv, rel, marks, par)

    def rows_of(values, which):
        return jnp.concatenate(
            [
                lax.dynamic_slice_in_dim(values, which * half, half, 0),
                lax.dynamic_slice_in_dim(values, L + which * target_half, target_half, 0),
            ],
            0,
        )

    def by_side(own, other, axis):
        return jnp.where(
            side == 0,
            jnp.concatenate([own, other], axis),
            jnp.concatenate([other, own], axis),
        )

    attn_rows = by_side(rows_of(att, side), swap(rows_of(att, 1 - side)), 1)
    first_sum = product(attn_rows, full_out) + mine[:own_rows].astype(F32)
    first_norm = layer_norm(first_sum, gains[0], shifts[0])
    first_low = first_norm.astype(BF)
    hidden_pre = product(first_low, full_inner) + inner_bias
    activation = gelu_tanh(hidden_pre).astype(BF)
    second_sum = product(activation, full_outer) + outer_bias + first_norm
    result = layer_norm(second_sum, gains[1], shifts[1]).astype(BF)
    grad_rows = jnp.concatenate([grad_hidden_out[0], grad_query_out[0]], 0).astype(F32)
    second_pull = jax.vjp(layer_norm, second_sum, gains[1], shifts[1])[1]
    grad_second, grad_gain_two, grad_shift_two = second_pull(grad_rows)
    grad_outer_low = grad_second.astype(BF)
    grad_b_outer = jnp.sum(grad_outer_low.astype(F32), 0)
    grad_w_outer = inner_cols(activation, grad_outer_low)
    gelu_pull = jax.vjp(gelu_tanh, hidden_pre)[1]
    grad_pre = gelu_pull(inner_rows(grad_outer_low, full_outer))[0].astype(BF)
    grad_b_inner = jnp.sum(grad_pre.astype(F32), 0)
    grad_w_inner = inner_cols(first_low, grad_pre)
    grad_first = grad_second + inner_rows(grad_pre, full_inner)
    first_pull = jax.vjp(layer_norm, first_sum, gains[0], shifts[0])[1]
    grad_sum_one, grad_gain_one, grad_shift_one = first_pull(grad_first)
    grad_mixed = grad_sum_one.astype(BF)
    grad_w_out = inner_cols(attn_rows, grad_mixed)
    grad_attn = inner_rows(grad_mixed, full_out).astype(BF)

    devices = 2 * groups
    out_rows = width // devices
    token_smalls = (
        grad_b_inner.reshape(devices, -1),
        grad_b_outer.reshape(devices, -1),
        jnp.stack([grad_gain_one, grad_gain_two]).reshape(2, devices, -1),
        jnp.stack([grad_shift_one, grad_shift_two]).reshape(2, devices, -1),
    )
    token_flat = jnp.concatenate(
        [s if s.ndim == 2 else s.transpose(1, 0, 2).reshape(devices, -1) for s in token_smalls], 1
    )
    token_count = token_flat.shape[1]
    token_flat = jnp.pad(token_flat, ((0, 0), (0, out_rows * LANES - token_count)))
    token_packed = jnp.concatenate(
        [grad_w_out, grad_w_inner, token_flat.reshape(width, LANES)], 1
    ).astype(BF)
    everywhere = ("seq", "fsdp")
    token_sums = lax.psum_scatter(token_packed, everywhere, scatter_dimension=0, tiled=True)
    out_outer = lax.psum_scatter(
        grad_w_outer.astype(BF), everywhere, scatter_dimension=0, tiled=True
    ).astype(F32)
    token_sums = token_sums.astype(F32)
    out_out = token_sums[:, :width]
    out_inner = token_sums[:, width : width + ffn_width]
    small_sums = token_sums[:, width + ffn_width :].reshape(-1)
    inner_count, row_count = ffn_width // devices, width // devices
    out_b_inner = small_sums[:inner_count]
    at = inner_count
    out_b_outer = small_sums[at : at + row_count]
    at += row_count
    out_gains = small_sums[at : at + 2 * row_count].reshape(2, row_count)
    at += 2 * row_count
    out_shifts = small_sums[at : at + 2 * row_count].reshape(2, row_count)

    own_grad = lax.dynamic_slice_in_dim(grad_attn, side * head_width, head_width, 1)
    far_grad = swap(lax.dynamic_slice_in_dim(grad_attn, (1 - side) * head_width, head_width, 1))
    head_grad = jnp.concatenate(
        [by_side(own_grad[a:b], far_grad[a:b], 0) for a, b in cuts[:2]], 0
    )
    dq, dk, dv, drel, dpar = attention_backward(
        order, qkv, rel, marks, par, head_grad, att, inverse, exps
    )

    weight_q = head_weights[:, :head_width]
    weight_k = head_weights[:, head_width : 2 * head_width]
    weight_v = head_weights[:, 2 * head_width :]

    def back_rows(which):
        return (
            inner_rows(rows_of(dq, which), weight_q)
            + jnp.pad(
                inner_rows(
                    lax.dynamic_slice_in_dim(dk, which * half, half, 0), weight_k
                )
                + inner_rows(
                    lax.dynamic_slice_in_dim(dv, which * half, half, 0), weight_v
                ),
                ((0, target_half), (0, 0)),
            )
        )

    far_rows = swap(back_rows(1 - side).astype(BF)).astype(F32)
    grad_own = grad_sum_one + back_rows(side) + far_rows

    grad_head = jnp.concatenate(
        [inner_cols(stacked[:MROW], dq), inner_cols(stacked, dk), inner_cols(stacked, dv)], 1
    ).astype(BF)
    grad_head = grad_head.reshape(2, groups, out_rows, 3 * head_width)
    grad_head = grad_head.transpose(1, 0, 2, 3).reshape(width, 3 * head_width)
    grad_rel = inner_cols(pos_table, drel).astype(BF)
    bias_count = head_width // groups
    head_flat = dpar[:5].reshape(5, groups, bias_count).transpose(1, 0, 2).reshape(groups, -1)
    head_flat = jnp.pad(head_flat, ((0, 0), (0, shard_rows * LANES - 5 * bias_count)))
    head_packed = jnp.concatenate(
        [grad_head, grad_rel, head_flat.reshape(width, LANES).astype(BF)], 1
    )
    head_sums = lax.psum_scatter(head_packed, "fsdp", scatter_dimension=0, tiled=True)
    own_sum = lax.dynamic_slice_in_dim(head_sums, side * out_rows, out_rows, 0)
    far_sum = lax.dynamic_slice_in_dim(head_sums, (1 - side) * out_rows, out_rows, 0)
    own_sum = own_sum[:, : 3 * head_width].astype(F32)
    far_sum = swap(far_sum[:, : 3 * head_width]).astype(F32)
    out_query, out_key, out_value = (
        by_side(
            own_sum[:, at * head_width : (at + 1) * head_width],
            far_sum[:, at * head_width : (at + 1) * head_width],
            1,
        )
        for at in range(3)
    )
    out_rel = head_sums[:, 3 * head_width : 4 * head_width].astype(F32)
    small_head = head_sums[:, 4 * head_width :].reshape(-1).astype(F32)
    out_biases = small_head[: 3 * bias_count].reshape(3, bias_count)
    out_seg = small_head[3 * bias_count : 5 * bias_count].reshape(2, bias_count)
    return (
        result[None, :half],
        result[None, half:],
        grad_own[None, :half],
        grad_own[None, half:],
        out_query,
        out_key,
        out_value,
        out_out,
        out_rel,
        out_biases,
        out_seg,
        out_inner,
        out_b_inner,
        out_outer,
        out_b_outer,
        out_gains,
        out_shifts,
    )


def solution(mesh):
    rows = P("fsdp", "seq", None)
    both = ("seq", "fsdp")
    in_specs = (
        (rows,) * 3
        + (P("fsdp", None),) * 7
        + (P("fsdp", "seq"), P(None, both), P(None, both))
        + (P("fsdp", None), P("fsdp"), P("fsdp", None), P("fsdp"))
        + (P(None, "fsdp"), P(None, "fsdp"))
        + (rows,) * 2
    )
    out_specs = (
        (rows,) * 4
        + (P(both, None),) * 4
        + (P("fsdp", "seq"), P(None, both), P(None, both))
        + (P(both, None), P(both), P(both, None), P(both))
        + (P(None, both), P(None, both))
    )
    return jax.shard_map(shards, mesh=mesh, in_specs=in_specs, out_specs=out_specs, check_vma=False)
```

```python
import jax
import jax.numpy as jnp
from jax import lax
from jax.experimental import pallas as pl
from jax.experimental.pallas import tpu as pltpu
from jax.sharding import PartitionSpec as P

DH = 64
BLOCK = 256
NBLK = 4
MEM = 384
L = 1024
LANES = 128

QROW = L
MROW = L + BLOCK
ROWS = L + BLOCK + MEM
KEYS = MEM + L
SPAN_M = MEM + BLOCK
SPAN_T = 2 * BLOCK
REL_M = L - BLOCK
REL_T = MEM + L - BLOCK
REL_ROWS = MEM + 2 * L

EPSILON = 1e-05
NEGATIVE = -1e30
SCORE_SCALE = 0.125
EXP2_SCALE = SCORE_SCALE * 1.4426950408889634
STEPS = NBLK + 1
VMEM_LIMIT = 60 * 1024 * 1024
BF = jnp.bfloat16
F32 = jnp.float32


def product(left, right):
    return jnp.dot(left, right, preferred_element_type=F32)


def inner_rows(left, right):
    return lax.dot_general(left, right, (((1,), (1,)), ((), ())), preferred_element_type=F32)


def inner_cols(left, right):
    return lax.dot_general(left, right, (((0,), (0,)), ((), ())), preferred_element_type=F32)


def sinusoid(row_count, width_all, farthest):
    fine = DH
    frequency = 10000.0 ** (-jnp.arange(0, width_all, 2).astype(F32) / width_all)
    starts = (farthest - fine * jnp.arange(row_count // fine)).astype(F32)
    far = starts[:, None, None] * frequency
    near = jnp.arange(fine).astype(F32)[None, :, None] * frequency
    sines = jnp.sin(far) * jnp.cos(near) - jnp.cos(far) * jnp.sin(near)
    cosines = jnp.cos(far) * jnp.cos(near) + jnp.sin(far) * jnp.sin(near)
    return jnp.concatenate([sines, cosines], 2).reshape(row_count, width_all)


def split_low(values):
    high = values.astype(BF).astype(F32)
    return high, values - high


def place(step, order_ref):
    last = jnp.minimum(step, NBLK - 1)
    block = order_ref[last]
    row = jnp.where(step < NBLK, block, NBLK) * BLOCK
    return block, pl.multiple_of(row, BLOCK), last


def row_terms(q_ref, kx_ref, par_ref, row):
    query = q_ref[pl.ds(row, BLOCK), :].astype(F32)
    marks = kx_ref[pl.ds(row, BLOCK), :].astype(F32)
    return query + par_ref[0:1, :], query + par_ref[1:2, :], query + par_ref[2:3, :], marks


def forward_kernel(
    order_ref,
    q_ref,
    k_ref,
    v_ref,
    rel_ref,
    kx_ref,
    par_ref,
    att_ref,
    exp_ref,
    inv_ref,
    kcat_ref,
    vcat_ref,
    score_ref,
    lhs_ref,
    qr_ref,
):
    step = pl.program_id(0)

    @pl.when(step == 0)
    def _():
        kcat_ref[:, :LANES] = k_ref[...]
        kcat_ref[:, LANES:] = kx_ref[...]
        vcat_ref[:, :LANES] = v_ref[...]
        vcat_ref[:, LANES:] = jnp.ones((ROWS, LANES), BF)

    block, row, last = place(step, order_ref)
    lane = lax.broadcasted_iota(jnp.int32, (BLOCK, LANES), 1)
    query_w, query_r, query_s, marks = row_terms(q_ref, kx_ref, par_ref, row)
    same, other = query_s * par_ref[3:4, :], query_s * par_ref[4:5, :]
    for head in range(2):
        mine = (lane < DH) == (head == 0)
        other_sum = jnp.sum(jnp.where(mine, other, 0.0), -1, keepdims=True)
        diff = jnp.sum(jnp.where(mine, same, 0.0), -1, keepdims=True) - other_sum
        diff_high, diff_low = split_low(diff)
        other_high, other_low = split_low(other_sum)
        extra = jnp.where(lane < 3, marks * diff_high, jnp.where(lane < 6, marks * diff_low, 0.0))
        extra = jnp.where(lane == 6, other_high, jnp.where(lane == 7, other_low, extra))
        extra = jnp.where(lane == 8, NEGATIVE, extra)
        lhs_ref[head, :, :LANES] = jnp.where(mine, query_w, 0.0).astype(BF)
        lhs_ref[head, :, LANES:] = extra.astype(BF)
        qr_ref[head] = jnp.where(mine, query_r, 0.0).astype(BF)

    def scores(head, key_row, key_count, rel_row):
        content = inner_rows(lhs_ref[head], kcat_ref[pl.ds(key_row, key_count), :])
        span = key_count + BLOCK
        position = inner_rows(qr_ref[head], rel_ref[pl.ds(rel_row, span), :])
        position = pltpu.roll(position, span - BLOCK + 1, 1, stride=1, stride_axis=0)
        return content + position[:, :key_count]

    def widest(running, tile):
        for at in range(0, tile.shape[1], LANES):
            piece = tile[:, at : at + LANES]
            running = piece if running is None else jnp.maximum(running, piece)
        return running

    tops = []
    rel_row = pl.multiple_of(REL_M - BLOCK * block, BLOCK)
    for head in range(2):
        tile = scores(head, MROW, MEM, rel_row)
        score_ref[head, :, :MEM] = tile
        tops.append(widest(None, tile))

    def column(at):
        return pl.multiple_of(MEM + BLOCK * at, LANES)

    def token_tile(at, tops):
        key_block = order_ref[at]
        key_row = pl.multiple_of(BLOCK * key_block, BLOCK)
        rel_row = pl.multiple_of(REL_T + BLOCK * (key_block - block), LANES)
        fresh = []
        for head in range(2):
            tile = scores(head, key_row, BLOCK, rel_row)
            score_ref[head, :, pl.ds(column(at), BLOCK)] = tile
            fresh.append(widest(tops[head], tile))
        return tuple(fresh)

    tops = lax.fori_loop(0, last, token_tile, tuple(tops))
    across = lax.broadcasted_iota(jnp.int32, (BLOCK, BLOCK), 0) - lax.broadcasted_iota(
        jnp.int32, (BLOCK, BLOCK), 1
    )
    hidden_at = jnp.where(step < NBLK, BLOCK, 0)
    own_row = pl.multiple_of(BLOCK * block, BLOCK)
    peaks = []
    for head in range(2):
        tile = scores(head, own_row, BLOCK, REL_T)
        tile = jnp.where(across == hidden_at, NEGATIVE, tile)
        score_ref[head, :, pl.ds(column(last), BLOCK)] = tile
        peaks.append(jnp.max(widest(tops[head], tile), -1, keepdims=True))

    def weigh(head, at, key_row, key_count):
        tile = score_ref[head, :, pl.ds(at, key_count)]
        low = jnp.exp2((tile - peaks[head]) * EXP2_SCALE).astype(BF)
        exp_ref[head, :, pl.ds(at, key_count)] = low
        return product(low, vcat_ref[pl.ds(key_row, key_count), :])

    sums = tuple(weigh(head, 0, MROW, MEM) for head in range(2))

    def token_sum(at, sums):
        key_row = pl.multiple_of(BLOCK * order_ref[at], BLOCK)
        return tuple(sums[head] + weigh(head, column(at), key_row, BLOCK) for head in range(2))

    sums = lax.fori_loop(0, last + 1, token_sum, sums)
    first = lane < DH
    inverse = 1.0 / jnp.where(first, sums[0][:, LANES:], sums[1][:, LANES:])
    total = jnp.where(first, sums[0][:, :LANES], sums[1][:, :LANES])
    att_ref[pl.ds(row, BLOCK), :] = (total * inverse).astype(BF)
    inv_ref[pl.ds(row, BLOCK), :] = inverse


def backward_kernel(
    order_ref,
    q_ref,
    k_ref,
    v_ref,
    rel_ref,
    kx_ref,
    par_ref,
    grad_ref,
    att_ref,
    inv_ref,
    exp_ref,
    dqkv_ref,
    drel_ref,
    dpar_ref,
    kcat_ref,
    vcat_ref,
    flip_ref,
    lhs_ref,
    qwt_ref,
    qrt_ref,
    gt_ref,
    dkt_ref,
    dvt_ref,
    drelt_ref,
    accw_ref,
    accr_ref,
):
    step = pl.program_id(0)

    @pl.when(step == 0)
    def _():
        kcat_ref[:, :LANES] = k_ref[...]
        kcat_ref[:, LANES:] = kx_ref[...]
        vcat_ref[:, :LANES] = (v_ref[...].astype(F32) * SCORE_SCALE).astype(BF)
        vcat_ref[:, LANES:] = jnp.full((ROWS, LANES), SCORE_SCALE, BF)
        up = lax.broadcasted_iota(jnp.int32, (BLOCK, BLOCK), 0)
        down = lax.broadcasted_iota(jnp.int32, (BLOCK, BLOCK), 1)
        flip_ref[...] = jnp.where(up + down == BLOCK - 1, 1.0, 0.0).astype(BF)
        dkt_ref[...] = jnp.zeros_like(dkt_ref)
        dvt_ref[...] = jnp.zeros_like(dvt_ref)
        drelt_ref[...] = jnp.zeros_like(drelt_ref)
        dpar_ref[...] = jnp.zeros_like(dpar_ref)

    block, row, last = place(step, order_ref)
    lane = lax.broadcasted_iota(jnp.int32, (BLOCK, LANES), 1)
    query_w, query_r, query_s, marks = row_terms(q_ref, kx_ref, par_ref, row)
    grad_low = (grad_ref[pl.ds(row, BLOCK), :].astype(F32) * inv_ref[pl.ds(row, BLOCK), :]).astype(
        BF
    )
    grad = grad_low.astype(F32)
    dots = grad * att_ref[pl.ds(row, BLOCK), :].astype(F32)
    for head in range(2):
        mine = (lane < DH) == (head == 0)
        high, low = split_low(-jnp.sum(jnp.where(mine, dots, 0.0), -1, keepdims=True))
        extra = jnp.where(lane == 0, high, jnp.where(lane == 1, low, 0.0))
        lhs_ref[head, :, :LANES] = jnp.where(mine, grad, 0.0).astype(BF)
        lhs_ref[head, :, LANES:] = extra.astype(BF)
    flip = flip_ref[...]
    qwt_ref[...] = query_w.astype(BF).astype(F32).T.astype(BF)
    qrt_ref[...] = product(flip, query_r.astype(BF)).T.astype(BF)
    gt_ref[...] = grad.T.astype(BF)
    accw_ref[...] = jnp.zeros_like(accw_ref)
    accr_ref[...] = jnp.zeros_like(accr_ref)

    def tile(head, at, key_row, key_count, rel_row):
        span = key_count + BLOCK
        own = slice(DH * head, DH * head + DH)
        keys = pl.ds(key_row, key_count)
        span_at = pl.ds(rel_row, span)
        probs = exp_ref[head, :, pl.ds(at, key_count)]
        slope = inner_rows(lhs_ref[head], vcat_ref[keys, :])
        scaled = (probs.astype(F32) * slope).astype(BF)
        accw_ref[head] += product(scaled, kcat_ref[keys, :])
        dkt_ref[own, keys] += product(qwt_ref[own, :], scaled)
        dvt_ref[own, keys] += product(gt_ref[own, :], probs)
        turned = product(flip, scaled).astype(BF)
        turned = jnp.concatenate([turned, jnp.zeros((BLOCK, BLOCK), BF)], 1)
        turned = pltpu.roll(turned, 0, 1, stride=1, stride_axis=0)
        accr_ref[head] += product(turned, rel_ref[span_at, :])
        drelt_ref[own, span_at] += product(qrt_ref[own, :], turned)

    rel_row = pl.multiple_of(REL_M - BLOCK * block, BLOCK)
    for head in range(2):
        tile(head, 0, MROW, MEM, rel_row)

    def token_tile(at, carry):
        key_block = order_ref[at]
        key_row = pl.multiple_of(BLOCK * key_block, BLOCK)
        rel_row = pl.multiple_of(REL_T + BLOCK * (key_block - block), LANES)
        for head in range(2):
            tile(head, pl.multiple_of(MEM + BLOCK * at, LANES), key_row, BLOCK, rel_row)
        return carry

    lax.fori_loop(0, last + 1, token_tile, 0)

    first = lane < DH
    grad_w = jnp.where(first, accw_ref[0, :, :LANES], accw_ref[1, :, :LANES])
    high, low = split_low(jnp.where(first, accr_ref[0], accr_ref[1]))
    grad_r = product(flip, high.astype(BF)) + product(flip, low.astype(BF))
    same_sums, other_sums = [], []
    for head in range(2):
        sums = accw_ref[head, :, LANES:]
        same_sums.append(jnp.sum(jnp.where(lane < 3, marks * sums, 0.0), -1, keepdims=True))
        total = jnp.sum(jnp.where(lane == 6, sums, 0.0), -1, keepdims=True)
        other_sums.append(total - same_sums[head])
    same = jnp.where(first, same_sums[0], same_sums[1])
    other = jnp.where(first, other_sums[0], other_sums[1])
    grad_s = same * par_ref[3:4, :] + other * par_ref[4:5, :]
    dqkv_ref[pl.ds(row, BLOCK), :LANES] = (grad_w + grad_r + grad_s).astype(BF)
    for at, rows in enumerate((grad_w, grad_r, grad_s, same * query_s, other * query_s)):
        dpar_ref[at : at + 1, :] += jnp.sum(rows, 0, keepdims=True)

    @pl.when(step == STEPS - 1)
    def _():
        dqkv_ref[MROW:, :LANES] = jnp.zeros((MEM, LANES), BF)
        dqkv_ref[:, LANES : 2 * LANES] = dkt_ref[...].T.astype(BF)
        dqkv_ref[:, 2 * LANES :] = dvt_ref[...].T.astype(BF)
        drel_ref[...] = drelt_ref[...].T.astype(BF)


def column(rows, at):
    return pl.BlockSpec((rows, LANES), lambda step, order: (0, at))


def attention_specs(pair, first):
    ins = [column(ROWS, first + at) for at in range(3)]
    ins += [column(REL_ROWS, pair), column(ROWS, 0), column(8, pair)]
    exps = pl.BlockSpec((None, 2, BLOCK, KEYS), lambda step, order: (step, 0, 0, 0))
    return ins, exps


def settings(passes):
    return dict(
        compiler_params=pltpu.CompilerParams(
            dimension_semantics=("arbitrary",), vmem_limit_bytes=40 * 1024 * 1024
        ),
        cost_estimate=pl.CostEstimate(
            flops=passes * 4 * MROW * KEYS * BLOCK,
            bytes_accessed=STEPS * 2 * BLOCK * KEYS * 2,
            transcendentals=2 * MROW * KEYS,
        ),
    )


def attention_forward(pair, first, order, qkv, rel, marks, par):
    ins, exps = attention_specs(pair, first)
    return pl.pallas_call(
        forward_kernel,
        grid_spec=pltpu.PrefetchScalarGridSpec(
            num_scalar_prefetch=1,
            grid=(STEPS,),
            in_specs=ins,
            out_specs=[column(MROW, 0), exps, column(MROW, 0)],
            scratch_shapes=[
                pltpu.VMEM((ROWS, 2 * LANES), BF),
                pltpu.VMEM((ROWS, 2 * LANES), BF),
                pltpu.VMEM((2, BLOCK, KEYS), F32),
                pltpu.VMEM((2, BLOCK, 2 * LANES), BF),
                pltpu.VMEM((2, BLOCK, LANES), BF),
            ],
        ),
        out_shape=[
            jax.ShapeDtypeStruct((MROW, LANES), BF),
            pltpu.HBM((STEPS, 2, BLOCK, KEYS), BF),
            jax.ShapeDtypeStruct((MROW, LANES), F32),
        ],
        **settings(16),
    )(order, qkv, qkv, qkv, rel, marks, par)


def attention_backward(pair, first, order, qkv, rel, marks, par, grad, att, inverse, exps_in):
    ins, exps = attention_specs(pair, first)
    return pl.pallas_call(
        backward_kernel,
        grid_spec=pltpu.PrefetchScalarGridSpec(
            num_scalar_prefetch=1,
            grid=(STEPS,),
            in_specs=ins + [column(MROW, 0)] * 3 + [exps],
            out_specs=[
                pl.BlockSpec((ROWS, 3 * LANES), lambda step, order: (0, 0)),
                column(REL_ROWS, 0),
                column(8, 0),
            ],
            scratch_shapes=[
                pltpu.VMEM((ROWS, 2 * LANES), BF),
                pltpu.VMEM((ROWS, 2 * LANES), BF),
                pltpu.VMEM((BLOCK, BLOCK), BF),
                pltpu.VMEM((2, BLOCK, 2 * LANES), BF),
                pltpu.VMEM((LANES, BLOCK), BF),
                pltpu.VMEM((LANES, BLOCK), BF),
                pltpu.VMEM((LANES, BLOCK), BF),
                pltpu.VMEM((LANES, ROWS), F32),
                pltpu.VMEM((LANES, ROWS), F32),
                pltpu.VMEM((LANES, REL_ROWS), F32),
                pltpu.VMEM((2, BLOCK, 2 * LANES), F32),
                pltpu.VMEM((2, BLOCK, LANES), F32),
            ],
        ),
        out_shape=[
            jax.ShapeDtypeStruct((ROWS, 3 * LANES), BF),
            jax.ShapeDtypeStruct((REL_ROWS, LANES), BF),
            jax.ShapeDtypeStruct((8, LANES), F32),
        ],
        **settings(24),
    )(order, qkv, qkv, qkv, rel, marks, par, grad, att, inverse, exps_in)


CHUNKS = 2


def norm_parts(values):
    center = values - jnp.mean(values, -1, keepdims=True)
    spread = jnp.mean(center * center, -1, keepdims=True)
    scale = lax.rsqrt(spread + EPSILON)
    return center * scale, scale


def norm_pull(grad, unit, scale, gain):
    grad = grad * gain
    mean = jnp.mean(grad, -1, keepdims=True)
    slope = jnp.mean(grad * unit, -1, keepdims=True)
    return (grad - mean - unit * slope) * scale


def middle_kernel(
    attn_ref,
    hidden_ref,
    query_ref,
    grad_hidden_ref,
    grad_query_ref,
    w_out_ref,
    w_inner_ref,
    w_outer_ref,
    inner_bias_ref,
    small_ref,
    result_ref,
    grad_sum_ref,
    grad_attn_ref,
    gw_ref,
    gb_inner_ref,
    g_small_ref,
    unit_ref,
    scale_ref,
    low_ref,
    low_t_ref,
    act_ref,
    slope_ref,
    sum_ref,
    grad_ref,
    grad_low_ref,
    back_ref,
):
    step = pl.program_id(0)
    rows, width = attn_ref.shape
    tiles = act_ref.shape[1] // width
    half = hidden_ref.shape[0]
    cut = rows // CHUNKS
    gain_one, shift_one = small_ref[0:1, :], small_ref[1:2, :]
    gain_two, shift_two = small_ref[2:3, :], small_ref[3:4, :]
    parts = [slice(at * cut, at * cut + cut) for at in range(CHUNKS)]

    @pl.when(step == 0)
    def _():
        sum_ref[...] = product(attn_ref[...], w_out_ref[...])
        sum_ref[:half, :] += hidden_ref[...].astype(F32)
        sum_ref[half:, :] += query_ref[...].astype(F32)
        for part in parts:
            unit, scale = norm_parts(sum_ref[part, :])
            unit_ref[part, :] = unit
            scale_ref[part, :] = jnp.broadcast_to(scale, (cut, LANES))
            first = unit * gain_one + shift_one
            low_ref[part, :] = first.astype(BF)
            sum_ref[part, :] = first + small_ref[4:5, :]

    place_of = jnp.where(step < tiles, step, lax.div(step - tiles, 2))
    columns = pl.ds(pl.multiple_of(place_of * width, width), width)

    @pl.when(step < tiles)
    def _():
        for part in parts:
            pre = product(low_ref[part, :], w_inner_ref[...]) + inner_bias_ref[...]
            square = pre * pre
            bend = jnp.tanh(0.7978845608028654 * (pre + 0.044715 * square * pre))
            half_bend = 0.5 + 0.5 * bend
            act = (pre * half_bend).astype(BF)
            act_ref[part, columns] = act
            turn = 0.7978845608028654 * (1.0 + 0.134145 * square)
            slope_ref[part, columns] = half_bend + 0.5 * pre * (1.0 - bend * bend) * turn
            sum_ref[part, :] += product(act, w_outer_ref[...])

    @pl.when(step == tiles - 1)
    def _():
        g_gain = g_shift = g_outer = 0.0
        grad_ref[:half, :] = grad_hidden_ref[...].astype(F32)
        grad_ref[half:, :] = grad_query_ref[...].astype(F32)
        for part in parts:
            unit, scale = norm_parts(sum_ref[part, :])
            result_ref[part, :] = (unit * gain_two + shift_two).astype(BF)
            grad = grad_ref[part, :]
            g_gain += jnp.sum(grad * unit, 0, keepdims=True)
            g_shift += jnp.sum(grad, 0, keepdims=True)
            grad = norm_pull(grad, unit, scale, gain_two)
            low = grad.astype(BF)
            grad_ref[part, :] = grad
            grad_low_ref[part, :] = low
            g_outer += jnp.sum(low.astype(F32), 0, keepdims=True)
        g_small_ref[...] = jnp.zeros_like(g_small_ref)
        g_small_ref[2:3, :] = g_gain
        g_small_ref[3:4, :] = g_shift
        g_small_ref[4:5, :] = g_outer
        low_t_ref[...] = low_ref[...].T

    turn_back = jnp.logical_and(step >= tiles, step < 3 * tiles)

    @pl.when(jnp.logical_and(turn_back, lax.rem(step - tiles, 2) == 0))
    def _():
        g_inner = 0.0
        for part in parts:
            back = inner_rows(grad_low_ref[part, :], w_outer_ref[...])
            low = (back * slope_ref[part, columns]).astype(BF)
            back_ref[part, :] = low
            g_inner += jnp.sum(low.astype(F32), 0, keepdims=True)
            grad_ref[part, :] += inner_rows(low, w_inner_ref[...])
        gb_inner_ref[...] = g_inner
        gw_ref[...] = product(low_t_ref[...], back_ref[...]).astype(BF)

    @pl.when(jnp.logical_and(turn_back, lax.rem(step - tiles, 2) == 1))
    def _():
        gw_ref[...] = inner_cols(act_ref[:, columns], grad_low_ref[...]).astype(BF)

    @pl.when(step == 3 * tiles)
    def _():
        g_gain = g_shift = 0.0
        for part in parts:
            unit, scale = unit_ref[part, :], scale_ref[part, 0:1]
            grad = grad_ref[part, :]
            g_gain += jnp.sum(grad * unit, 0, keepdims=True)
            g_shift += jnp.sum(grad, 0, keepdims=True)
            grad = norm_pull(grad, unit, scale, gain_one)
            grad_sum_ref[part, :] = grad
            grad_low_ref[part, :] = grad.astype(BF)
        g_small_ref[0:1, :] = g_gain
        g_small_ref[1:2, :] = g_shift
        gw_ref[...] = inner_cols(attn_ref[...], grad_low_ref[...]).astype(BF)
        grad_attn_ref[...] = inner_rows(grad_low_ref[...], w_out_ref[...]).astype(BF)


def middle(attn, hidden, query, grad_hidden, grad_query, weights, inner_bias, small):
    rows, width = attn.shape
    tiles = inner_bias.shape[1] // width

    def whole(array):
        return pl.BlockSpec(array.shape, lambda step: (0,) * array.ndim)

    def square(at):
        return pl.BlockSpec((width, width), lambda step: (0, at(step)))

    def back(step):
        return lax.min(lax.div(lax.max(step - tiles, 0), 2), tiles - 1)

    def tile(step):
        return lax.select(step < tiles, step, back(step))

    def written(step):
        odd = lax.rem(lax.max(step - tiles, 0), 2)
        return lax.select(step == 3 * tiles, 0, 1 + back(step) + tiles * odd)

    outs = [
        jax.ShapeDtypeStruct((rows, width), BF),
        jax.ShapeDtypeStruct((rows, width), F32),
        jax.ShapeDtypeStruct((rows, width), BF),
        jax.ShapeDtypeStruct((width, (1 + 2 * tiles) * width), BF),
        jax.ShapeDtypeStruct((1, tiles * width), F32),
        jax.ShapeDtypeStruct((8, width), F32),
    ]
    return pl.pallas_call(
        middle_kernel,
        grid=(1 + 3 * tiles,),
        in_specs=[whole(t) for t in (attn, hidden, query, grad_hidden, grad_query)]
        + [
            square(lambda step: 0),
            square(lambda step: 1 + tile(step)),
            square(lambda step: 1 + tiles + tile(step)),
            pl.BlockSpec((1, width), lambda step: (0, tile(step))),
            whole(small),
        ],
        out_specs=[whole(t) for t in outs[:3]]
        + [
            square(written),
            pl.BlockSpec((1, width), lambda step: (0, back(step))),
            whole(outs[5]),
        ],
        out_shape=outs,
        scratch_shapes=[
            pltpu.VMEM((rows, width), F32),
            pltpu.VMEM((rows, LANES), F32),
            pltpu.VMEM((rows, width), BF),
            pltpu.VMEM((width, rows), BF),
            pltpu.VMEM((rows, tiles * width), BF),
            pltpu.VMEM((rows, tiles * width), F32),
            pltpu.VMEM((rows, width), F32),
            pltpu.VMEM((rows, width), F32),
            pltpu.VMEM((rows, width), BF),
            pltpu.VMEM((rows, width), BF),
        ],
        compiler_params=pltpu.CompilerParams(
            dimension_semantics=("arbitrary",), vmem_limit_bytes=VMEM_LIMIT
        ),
        cost_estimate=pl.CostEstimate(
            flops=12 * rows * width * width * tiles,
            bytes_accessed=20 * width * width * tiles,
            transcendentals=rows * width * tiles,
        ),
    )(attn, hidden, query, grad_hidden, grad_query, weights, weights, weights, inner_bias, small)


def swap(values):
    return lax.ppermute(values, "seq", [(0, 1), (1, 0)])


def bit_orders(groups):
    high = list(range(groups.bit_length() - 2, 0, -1))
    return high, high[-1:] + high[:-1]


def across(values, groups, bit):
    return lax.ppermute(values, "fsdp", [(i, i ^ (1 << bit)) for i in range(groups)])


def merged(values, theirs, place, held, bit):
    axis = sum(1 for other in held if other > bit)
    return jnp.where(
        (place >> bit) & 1 == 0,
        jnp.stack([values, theirs], axis),
        jnp.stack([theirs, values], axis),
    )


def gather_beside(one, two, groups, chunks):
    place = lax.axis_index("fsdp")
    order_one, order_two = bit_orders(groups)
    order_one, order_two = order_one + [0], order_two + [0]
    swapped = []
    for at, (bit_one, bit_two) in enumerate(zip(order_one, order_two)):
        left = len(order_one) - at
        take = chunks[: -(-len(chunks) // left)] if len(chunks) >= left else []
        chunks = chunks[len(take) :]
        theirs = [across(one, groups, bit_one), across(two, groups, bit_two)]
        theirs += [swap(chunk) for chunk in take]
        theirs = lax.optimization_barrier(theirs)
        one = merged(one, theirs[0], place, order_one[:at], bit_one)
        two = merged(two, theirs[1], place, order_two[:at], bit_two)
        swapped += theirs[2:]
    bits = len(order_one)
    return (
        one.reshape((-1,) + one.shape[bits + 1 :]),
        two.reshape((-1,) + two.shape[bits + 1 :]),
        swapped,
    )


def shuffle(count, lanes):
    take = jnp.arange(count * lanes)[:, None]
    give = jnp.arange(count * lanes)[None, :]
    return ((take % lanes) * count + take // lanes == give).astype(BF)


def pad_to(values, count):
    return jnp.pad(values, (0, count - values.shape[0]))


def shards(
    hidden,
    query_in,
    memory,
    segment_ids,
    block_order,
    memory_valid,
    w_query,
    w_key,
    w_value,
    w_out,
    w_rel,
    rel_biases,
    seg_embed,
    w_inner,
    b_inner,
    w_outer,
    b_outer,
    norm_gains,
    norm_biases,
    grad_hidden_out,
    grad_query_out,
):
    side = lax.axis_index("seq")
    groups = lax.axis_size("fsdp")
    place_at = lax.axis_index("fsdp")
    half, width = hidden.shape[1:]
    target_half = query_in.shape[1]
    memory_half = memory.shape[1]
    head_width = w_rel.shape[1]
    shard_rows = w_query.shape[0]
    ffn_width = w_inner.shape[1]
    own_rows = half + target_half

    def by_side(own, other, axis):
        return jnp.where(
            side == 0,
            jnp.concatenate([own, other], axis),
            jnp.concatenate([other, own], axis),
        )

    pairs = head_width // LANES
    pair_width = 3 * LANES

    def head_columns(weight, pair):
        return lax.dynamic_slice_in_dim(weight, side * head_width + pair * LANES, LANES, 1)

    def pair_columns(pair):
        return [head_columns(weight, pair) for weight in (w_query, w_key, w_value)]

    few = jnp.concatenate([rel_biases, seg_embed], 0)
    few = jnp.pad(few, ((0, shard_rows - 5), (0, LANES - few.shape[1])))
    quarter = half // 2
    weights_one, weights_two, swapped = gather_beside(
        jnp.concatenate(sum([pair_columns(pair) for pair in range(pairs - 1)], []), 1),
        jnp.concatenate(pair_columns(pairs - 1) + [w_rel, few], 1),
        groups,
        [hidden[0, :quarter], hidden[0, quarter:], memory[0], query_in[0]],
    )
    rel_weight = weights_two[:, pair_width : pair_width + head_width]
    few_all = weights_two[:, pair_width + head_width :].reshape(groups, shard_rows, LANES)
    few_all = few_all[:, :5, : head_width // groups].astype(F32)
    few_all = few_all.transpose(1, 0, 2).reshape(5, head_width)

    blocks = ffn_width // width
    spots = shuffle(blocks, LANES)
    smalls = (b_inner, b_outer, norm_gains, norm_biases)
    small_flat = pad_to(jnp.concatenate([t.reshape(-1) for t in smalls]), shard_rows * LANES)
    inner_moved = lax.dot_general(
        w_inner.reshape(shard_rows, -1, blocks * LANES),
        spots,
        (((2,), (1,)), ((), ())),
        preferred_element_type=F32,
    ).astype(BF)
    inner_moved = inner_moved.reshape(shard_rows, -1, blocks, LANES).transpose(0, 2, 1, 3)
    mixed = jnp.concatenate(
        [
            w_out,
            inner_moved.reshape(shard_rows, ffn_width),
            w_outer.reshape(shard_rows, ffn_width),
            small_flat.reshape(shard_rows, LANES),
        ],
        1,
    )
    mixed, weights_one, swapped = lax.optimization_barrier((mixed, weights_one, swapped))
    mixed = lax.all_gather(mixed, "fsdp", axis=0, tiled=True)
    small_all = mixed[:, width + 2 * ffn_width :].reshape(groups, shard_rows * LANES).astype(F32)

    def unpack():
        found, at = [], 0
        for small in smalls:
            piece = small_all[:, at : at + small.size].reshape((groups,) + small.shape)
            found.append(jnp.moveaxis(piece, 0, -2).reshape(small.shape[:-1] + (-1,)))
            at += small.size
        return found

    inner_bias, outer_bias, gains, shifts = unpack()

    cuts = ((0, half), (half, own_rows))
    far_hidden = jnp.concatenate(swapped[:2], 0)
    stacked = jnp.concatenate(
        [
            by_side(hidden[0], far_hidden, 0),
            by_side(query_in[0], swapped[3], 0),
            by_side(memory[0], swapped[2], 0),
        ],
        0,
    )

    qkv_one = product(stacked, weights_one).astype(BF)
    qkv_two = product(stacked, weights_two[:, :pair_width]).astype(BF)
    pos_table = sinusoid(REL_ROWS, width, MEM + L - 1).astype(BF)
    rel = product(pos_table, rel_weight).astype(BF)
    par = jnp.concatenate([few_all, jnp.zeros((3, head_width), F32)], 0)
    order = block_order[0]
    segs = segment_ids[0]
    target_seg = lax.dynamic_slice_in_dim(segs, MEM + order[NBLK - 1] * BLOCK, BLOCK)
    seg_rows = jnp.concatenate([segs[MEM:], target_seg, segs[:MEM]])
    invalid = jnp.concatenate([jnp.zeros((MROW,), jnp.int32), (memory_valid[0] != 1).astype(jnp.int32)])
    lane = jnp.arange(LANES)[None, :]
    marks = jnp.where(lane < 6, seg_rows[:, None] == lane % 3, (lane == 6) | (lane == 7))
    marks = jnp.where(lane == 8, invalid[:, None] == 1, marks).astype(BF)

    def rows_of(values, which):
        return jnp.concatenate(
            [
                lax.dynamic_slice_in_dim(values, which * half, half, 0),
                lax.dynamic_slice_in_dim(values, L + which * target_half, target_half, 0),
            ],
            0,
        )

    def pair_args(pair):
        last = pair == pairs - 1
        at = (0, qkv_two) if last else (3 * pair, qkv_one)
        return (pair, at[0], order, at[1], rel, marks, par)

    kept = []
    own_att, far_att = [], []
    for pair in range(pairs):
        att, exps, inverse = attention_forward(*pair_args(pair))
        kept.append((att, inverse, exps))
        own_att.append(rows_of(att, side))
        far_att.append(swap(rows_of(att, 1 - side)))
    attn_rows = by_side(jnp.concatenate(own_att, 1), jnp.concatenate(far_att, 1), 1)
    small = jnp.stack([gains[0], shifts[0], gains[1], shifts[1], outer_bias] + [outer_bias] * 3)
    result, grad_sum_one, grad_attn, grad_weights, grad_b_inner, grad_small = middle(
        attn_rows,
        hidden[0],
        query_in[0],
        grad_hidden_out[0],
        grad_query_out[0],
        mixed,
        inner_bias.reshape(width, blocks).T.reshape(1, ffn_width),
        small,
    )

    devices = 2 * groups
    out_rows = width // devices
    token_sums = lax.psum_scatter(
        grad_weights, ("seq", "fsdp"), scatter_dimension=0, tiled=True
    )
    out_out = token_sums[:, :width].astype(F32)
    out_outer = token_sums[:, width + ffn_width :].reshape(blocks * out_rows, width).astype(F32)
    inner_sums = token_sums[:, width : width + ffn_width].reshape(out_rows, blocks, -1, LANES)
    out_inner = product(
        inner_sums.transpose(0, 2, 1, 3).reshape(out_rows, -1, blocks * LANES), spots
    ).reshape(out_rows, ffn_width)
    grad_b_inner = grad_b_inner.reshape(blocks, width).T.reshape(devices, -1)
    row_count = width // devices
    token_flat = jnp.concatenate(
        [
            grad_b_inner.reshape(devices, -1),
            grad_small[:5].reshape(5, devices, -1).transpose(1, 0, 2).reshape(devices, -1),
        ],
        1,
    )
    inner_count = ffn_width // devices

    weights_two = weights_two[:, :pair_width]
    weights_one, weights_two, attn_rows = lax.optimization_barrier(
        (weights_one, weights_two, attn_rows)
    )
    far_one, far_two = swap(weights_one), swap(weights_two)

    def pair_grad(pair, which):
        at = which * head_width + pair * LANES
        return lax.dynamic_slice_in_dim(grad_attn, at, LANES, 1)

    far_grads = [swap(pair_grad(pair, 1 - side)) for pair in range(pairs)]

    def sum_message(message):
        message = lax.all_to_all(message, "fsdp", split_axis=0, concat_axis=0, tiled=True)
        return jnp.sum(message.astype(F32), 0)

    own_rows_grads, far_rows_grads, sums, few_grads = [], [], [], []
    for pair in range(pairs):
        own, far = pair_grad(pair, side), far_grads[pair]
        if pair:
            own, message, sums = lax.optimization_barrier((own, message, sums))
            sums.append(sum_message(message))
        head_grad = jnp.concatenate([by_side(own[a:b], far[a:b], 0) for a, b in cuts], 0)
        dqkv, drel, dpar = attention_backward(*pair_args(pair), head_grad, *kept[pair])
        if pair == pairs - 1:
            dqkv, sums = lax.optimization_barrier((dqkv, sums))
        few_grads.append(dpar[:5])
        own_rows_grads.append(rows_of(dqkv, side))
        far_rows_grads.append(swap(rows_of(dqkv, 1 - side)))
        grad_pair = inner_cols(stacked, dqkv).astype(BF)
        grad_pair = grad_pair.reshape(2, groups, out_rows, pair_width).transpose(1, 0, 2, 3)
        message = jnp.concatenate(
            [
                grad_pair.reshape(groups, shard_rows, pair_width),
                inner_cols(pos_table, drel).astype(BF).reshape(groups, shard_rows, LANES),
            ],
            2,
        )
        if pair == 0:
            token_flat = token_flat.reshape(2, groups, -1).transpose(1, 0, 2).astype(BF)
            extra = ((0, 0), (0, 6), (0, pair_width + LANES - token_flat.shape[2]))
            message = jnp.concatenate([message, jnp.pad(token_flat, extra)], 1)
        if pair == pairs - 1:
            few = jnp.concatenate(few_grads, 1).reshape(5, groups, head_width // groups)
            few = few.transpose(1, 0, 2).reshape(groups, 1, -1).astype(BF)
            few = jnp.pad(few, ((0, 0), (0, 7), (0, pair_width + LANES - few.shape[2])))
            message = jnp.concatenate([message, few], 1)
    sums.append(sum_message(message))

    early = slice(0, pairs - 1)
    grad_own = grad_sum_one + inner_rows(
        jnp.concatenate(own_rows_grads + far_rows_grads[early], 1),
        jnp.concatenate([weights_one, weights_two, far_one], 1),
    )
    grad_own = grad_own + inner_rows(far_rows_grads[-1], far_two)

    both_sums = jnp.concatenate([t[:shard_rows, :pair_width] for t in sums], 1)
    own_sum = lax.dynamic_slice_in_dim(both_sums, side * out_rows, out_rows, 0)
    far_sum = lax.dynamic_slice_in_dim(both_sums, (1 - side) * out_rows, out_rows, 0)
    far_sum = swap(far_sum.astype(BF)).astype(F32)
    small_sums = lax.dynamic_index_in_dim(sums[0], shard_rows + side, 0, False)
    small_sums += swap(
        lax.dynamic_index_in_dim(sums[0], shard_rows + 1 - side, 0, False).astype(BF)
    ).astype(F32)
    out_b_inner = small_sums[:inner_count]
    out_rest = small_sums[inner_count : inner_count + 5 * row_count].reshape(5, row_count)
    out_gains, out_shifts, out_b_outer = out_rest[0:4:2], out_rest[1:4:2], out_rest[4]

    def weight_rows(values, which):
        return [
            values[:, pair * pair_width + which * LANES :][:, :LANES] for pair in range(pairs)
        ]

    out_query, out_key, out_value = (
        by_side(
            jnp.concatenate(weight_rows(own_sum, which), 1),
            jnp.concatenate(weight_rows(far_sum, which), 1),
            1,
        )
        for which in range(3)
    )
    out_rel = jnp.concatenate([t[:shard_rows, pair_width:] for t in sums], 1)
    few_sum = sums[-1][shard_rows, : 5 * (head_width // groups)].reshape(5, -1)
    out_biases, out_seg = few_sum[:3], few_sum[3:]
    return (
        result[None, :half],
        result[None, half:],
        grad_own[None, :half],
        grad_own[None, half:],
        out_query,
        out_key,
        out_value,
        out_out,
        out_rel,
        out_biases,
        out_seg,
        out_inner,
        out_b_inner,
        out_outer,
        out_b_outer,
        out_gains,
        out_shifts,
    )


def solution(mesh):
    rows = P("fsdp", "seq", None)
    both = ("seq", "fsdp")
    in_specs = (
        (rows,) * 3
        + (P("fsdp", None),) * 7
        + (P("fsdp", "seq"), P(None, both), P(None, both))
        + (P("fsdp", None), P("fsdp"), P("fsdp", None), P("fsdp"))
        + (P(None, "fsdp"), P(None, "fsdp"))
        + (rows,) * 2
    )
    out_specs = (
        (rows,) * 4
        + (P(both, None),) * 4
        + (P("fsdp", "seq"), P(None, both), P(None, both))
        + (P(both, None), P(both), P(both, None), P(both))
        + (P(None, both), P(None, both))
    )
    return jax.shard_map(shards, mesh=mesh, in_specs=in_specs, out_specs=out_specs, check_vma=False)
```

```python
import jax
import jax.numpy as jnp
from jax import lax
from jax.experimental import pallas as pl
from jax.experimental.pallas import tpu as pltpu
from jax.sharding import PartitionSpec as P

DH = 64
BLOCK = 256
NBLK = 4
MEM = 384
L = 1024
LANES = 128

QROW = L
MROW = L + BLOCK
ROWS = L + BLOCK + MEM
KEYS = MEM + L
SPAN_M = MEM + BLOCK
SPAN_T = 2 * BLOCK
REL_M = L - BLOCK
REL_T = MEM + L - BLOCK
REL_ROWS = MEM + 2 * L
SPANS = SPAN_M + NBLK * SPAN_T

EPSILON = 1e-05
NEGATIVE = -1e30
SCORE_SCALE = 0.125
EXP2_SCALE = SCORE_SCALE * 1.4426950408889634
STEPS = NBLK + 1
VMEM_LIMIT = 60 * 1024 * 1024
BF = jnp.bfloat16
F32 = jnp.float32


def product(left, right):
    return jnp.dot(left, right, preferred_element_type=F32)


def inner_rows(left, right):
    return lax.dot_general(left, right, (((1,), (1,)), ((), ())), preferred_element_type=F32)


def inner_cols(left, right):
    return lax.dot_general(left, right, (((0,), (0,)), ((), ())), preferred_element_type=F32)


def sinusoid(row_count, width_all, farthest):
    fine = DH
    frequency = 10000.0 ** (-jnp.arange(0, width_all, 2).astype(F32) / width_all)
    starts = (farthest - fine * jnp.arange(row_count // fine)).astype(F32)
    far = starts[:, None, None] * frequency
    near = jnp.arange(fine).astype(F32)[None, :, None] * frequency
    sines = jnp.sin(far) * jnp.cos(near) - jnp.cos(far) * jnp.sin(near)
    cosines = jnp.cos(far) * jnp.cos(near) + jnp.sin(far) * jnp.sin(near)
    return jnp.concatenate([sines, cosines], 2).reshape(row_count, width_all)


def split_low(values):
    high = values.astype(BF).astype(F32)
    return high, values - high


def place(step, order_ref):
    last = jnp.minimum(step, NBLK - 1)
    block = order_ref[last]
    row = jnp.where(step < NBLK, block, NBLK) * BLOCK
    return block, pl.multiple_of(row, BLOCK), last


def row_terms(q_ref, kx_ref, par_ref, row):
    query = q_ref[pl.ds(row, BLOCK), :].astype(F32)
    marks = kx_ref[pl.ds(row, BLOCK), :].astype(F32)
    return query + par_ref[0:1, :], query + par_ref[1:2, :], query + par_ref[2:3, :], marks


def gather_keys(order_ref, from_ref, to_ref, lanes):
    to_ref[:MEM, lanes] = from_ref[MROW:, :]
    for at in range(NBLK):
        rows = pl.ds(pl.multiple_of(BLOCK * order_ref[at], BLOCK), BLOCK)
        to_ref[MEM + BLOCK * at : MEM + BLOCK * (at + 1), lanes] = from_ref[rows, :]


def key_spots(order_ref, block, count):
    spots = [(0, MEM, pl.multiple_of(REL_M - BLOCK * block, BLOCK), 0)]
    for at in range(count):
        rel_row = pl.multiple_of(REL_T + BLOCK * (order_ref[at] - block), LANES)
        spots.append((MEM + BLOCK * at, BLOCK, rel_row, SPAN_M + SPAN_T * at))
    return spots


def gather_spans(spots, rel_ref, span_ref):
    for _, key_count, rel_row, put in spots:
        span = key_count + BLOCK
        span_ref[put : put + span, :] = rel_ref[pl.ds(rel_row, span), :]


def forward_kernel(
    order_ref,
    q_ref,
    k_ref,
    v_ref,
    rel_ref,
    kx_ref,
    par_ref,
    att_ref,
    exp_ref,
    inv_ref,
    kcat_ref,
    vcat_ref,
    score_ref,
    lhs_ref,
    qr_ref,
    span_ref,
    sum_ref,
):
    step = pl.program_id(0)

    @pl.when(step == 0)
    def _():
        gather_keys(order_ref, k_ref, kcat_ref, slice(0, LANES))
        gather_keys(order_ref, kx_ref, kcat_ref, slice(LANES, 2 * LANES))
        gather_keys(order_ref, v_ref, vcat_ref, slice(0, LANES))
        vcat_ref[:, LANES:] = jnp.ones((KEYS, LANES), BF)

    block, row, last = place(step, order_ref)
    lane = lax.broadcasted_iota(jnp.int32, (BLOCK, LANES), 1)
    query_w, query_r, query_s, marks = row_terms(q_ref, kx_ref, par_ref, row)
    same, other = query_s * par_ref[3:4, :], query_s * par_ref[4:5, :]
    for head in range(2):
        mine = (lane < DH) == (head == 0)
        other_sum = jnp.sum(jnp.where(mine, other, 0.0), -1, keepdims=True)
        diff = jnp.sum(jnp.where(mine, same, 0.0), -1, keepdims=True) - other_sum
        diff_high, diff_low = split_low(diff)
        other_high, other_low = split_low(other_sum)
        extra = jnp.where(lane < 3, marks * diff_high, jnp.where(lane < 6, marks * diff_low, 0.0))
        extra = jnp.where(lane == 6, other_high, jnp.where(lane == 7, other_low, extra))
        extra = jnp.where(lane == 8, NEGATIVE, extra)
        lhs_ref[head, :, :LANES] = jnp.where(mine, query_w, 0.0).astype(BF)
        lhs_ref[head, :, LANES:] = extra.astype(BF)
        qr_ref[head] = jnp.where(mine, query_r, 0.0).astype(BF)

    across = lax.broadcasted_iota(jnp.int32, (BLOCK, BLOCK), 0) - lax.broadcasted_iota(
        jnp.int32, (BLOCK, BLOCK), 1
    )
    hidden_at = jnp.where(step < NBLK, BLOCK, 0)

    for count in range(NBLK):

        @pl.when(last == count)
        def _():
            spots = key_spots(order_ref, block, count + 1)
            keys = MEM + BLOCK * (count + 1)
            spans = SPAN_M + SPAN_T * (count + 1)
            gather_spans(spots, rel_ref, span_ref)
            for head in range(2):
                content = inner_rows(lhs_ref[head], kcat_ref[:keys, :])
                position = inner_rows(qr_ref[head], span_ref[:spans, :])
                top = None
                for at, key_count, _, put in spots:
                    span = key_count + BLOCK
                    moved = position[:, put : put + span]
                    moved = pltpu.roll(moved, span - BLOCK + 1, 1, stride=1, stride_axis=0)
                    tile = content[:, at : at + key_count] + moved[:, :key_count]
                    if at + key_count == keys:
                        tile = jnp.where(across == hidden_at, NEGATIVE, tile)
                    score_ref[head, :, at : at + key_count] = tile
                    for piece in range(0, key_count, LANES):
                        part = tile[:, piece : piece + LANES]
                        top = part if top is None else jnp.maximum(top, part)
                peak = jnp.max(top, -1, keepdims=True)
                low = jnp.exp2((score_ref[head, :, :keys] - peak) * EXP2_SCALE).astype(BF)
                exp_ref[head, :, :keys] = low
                sum_ref[head] = product(low, vcat_ref[:keys, :])

    sums = sum_ref[0], sum_ref[1]
    first = lane < DH
    inverse = 1.0 / jnp.where(first, sums[0][:, LANES:], sums[1][:, LANES:])
    total = jnp.where(first, sums[0][:, :LANES], sums[1][:, :LANES])
    att_ref[pl.ds(row, BLOCK), :] = (total * inverse).astype(BF)
    inv_ref[pl.ds(row, BLOCK), :] = inverse


def backward_kernel(
    order_ref,
    q_ref,
    k_ref,
    v_ref,
    rel_ref,
    kx_ref,
    par_ref,
    grad_ref,
    att_ref,
    inv_ref,
    exp_ref,
    dqkv_ref,
    drel_ref,
    dpar_ref,
    kcat_ref,
    vcat_ref,
    flip_ref,
    lhs_ref,
    qwt_ref,
    qrt_ref,
    gt_ref,
    dkt_ref,
    dvt_ref,
    drelt_ref,
    accw_ref,
    accr_ref,
    span_ref,
    moved_ref,
):
    step = pl.program_id(0)

    @pl.when(step == 0)
    def _():
        gather_keys(order_ref, k_ref, kcat_ref, slice(0, LANES))
        gather_keys(order_ref, kx_ref, kcat_ref, slice(LANES, 2 * LANES))
        gather_keys(order_ref, v_ref, vcat_ref, slice(0, LANES))
        vcat_ref[:, :LANES] = (vcat_ref[:, :LANES].astype(F32) * SCORE_SCALE).astype(BF)
        vcat_ref[:, LANES:] = jnp.full((KEYS, LANES), SCORE_SCALE, BF)
        up = lax.broadcasted_iota(jnp.int32, (BLOCK, BLOCK), 0)
        down = lax.broadcasted_iota(jnp.int32, (BLOCK, BLOCK), 1)
        flip_ref[...] = jnp.where(up + down == BLOCK - 1, 1.0, 0.0).astype(BF)
        dkt_ref[...] = jnp.zeros_like(dkt_ref)
        dvt_ref[...] = jnp.zeros_like(dvt_ref)
        drelt_ref[...] = jnp.zeros_like(drelt_ref)
        dpar_ref[...] = jnp.zeros_like(dpar_ref)

    block, row, last = place(step, order_ref)
    lane = lax.broadcasted_iota(jnp.int32, (BLOCK, LANES), 1)
    first = lane < DH
    flip = flip_ref[...]
    rows = pl.ds(row, BLOCK)
    grad_low = (grad_ref[rows, :].astype(F32) * inv_ref[rows, :]).astype(BF)
    query, marks = product(flip, q_ref[rows, :]), product(flip, kx_ref[rows, :])
    grad, att = product(flip, grad_low), product(flip, att_ref[rows, :])
    query_w = query + par_ref[0:1, :]
    query_r = query + par_ref[1:2, :]
    query_s = query + par_ref[2:3, :]
    dots = grad * att
    for head in range(2):
        mine = first == (head == 0)
        high, low = split_low(-jnp.sum(jnp.where(mine, dots, 0.0), -1, keepdims=True))
        extra = jnp.where(lane == 0, high, jnp.where(lane == 1, low, 0.0))
        lhs_ref[head, :, :LANES] = jnp.where(mine, grad, 0.0).astype(BF)
        lhs_ref[head, :, LANES:] = extra.astype(BF)
    qwt_ref[...] = query_w.astype(BF).astype(F32).T.astype(BF)
    qrt_ref[...] = query_r.astype(BF).astype(F32).T.astype(BF)
    gt_ref[...] = grad_low.astype(F32).T.astype(BF)

    for count in range(NBLK):

        @pl.when(last == count)
        def _():
            spots = key_spots(order_ref, block, count + 1)
            keys = MEM + BLOCK * (count + 1)
            spans = SPAN_M + SPAN_T * (count + 1)
            gather_spans(spots, rel_ref, span_ref)
            for head in range(2):
                own = slice(DH * head, DH * head + DH)
                probs = exp_ref[head, :, :keys]
                slope = inner_rows(lhs_ref[head], vcat_ref[:keys, :])
                scaled = (product(flip, probs) * slope).astype(BF)
                for at, key_count, _, put in spots:
                    span = key_count + BLOCK
                    moved = jnp.concatenate(
                        [scaled[:, at : at + key_count], jnp.zeros((BLOCK, BLOCK), BF)], 1
                    )
                    moved_ref[head, :, put : put + span] = pltpu.roll(
                        moved, 0, 1, stride=1, stride_axis=0
                    )
                dkt_ref[own, :keys] += product(qwt_ref[own, :], scaled)
                dvt_ref[own, :keys] += product(gt_ref[own, :], probs)
                accw_ref[head] = product(scaled, kcat_ref[:keys, :])
                accr_ref[head] = product(moved_ref[head, :, :spans], span_ref[:spans, :])
                drel = product(qrt_ref[own, :], moved_ref[head, :, :spans])
                for _, key_count, rel_row, put in spots:
                    span = key_count + BLOCK
                    drelt_ref[own, pl.ds(rel_row, span)] += drel[:, put : put + span]

    grad_w = jnp.where(first, accw_ref[0, :, :LANES], accw_ref[1, :, :LANES])
    grad_r = jnp.where(first, accr_ref[0], accr_ref[1])
    same_sums, other_sums = [], []
    for head in range(2):
        sums = accw_ref[head, :, LANES:]
        same_sums.append(jnp.sum(jnp.where(lane < 3, marks * sums, 0.0), -1, keepdims=True))
        total = jnp.sum(jnp.where(lane == 6, sums, 0.0), -1, keepdims=True)
        other_sums.append(total - same_sums[head])
    same = jnp.where(first, same_sums[0], same_sums[1])
    other = jnp.where(first, other_sums[0], other_sums[1])
    grad_s = same * par_ref[3:4, :] + other * par_ref[4:5, :]
    high, low = split_low(grad_w + grad_r + grad_s)
    dqkv_ref[rows, :LANES] = (
        product(flip, high.astype(BF)) + product(flip, low.astype(BF))
    ).astype(BF)
    for at, terms in enumerate((grad_w, grad_r, grad_s, same * query_s, other * query_s)):
        dpar_ref[at : at + 1, :] += jnp.sum(terms, 0, keepdims=True)

    @pl.when(step == STEPS - 1)
    def _():
        dqkv_ref[MROW:, :LANES] = jnp.zeros((MEM, LANES), BF)
        dqkv_ref[L:MROW, LANES:] = jnp.zeros((BLOCK, 2 * LANES), BF)
        for lanes, from_ref in ((1, dkt_ref), (2, dvt_ref)):
            lanes = slice(lanes * LANES, (lanes + 1) * LANES)
            dqkv_ref[MROW:, lanes] = from_ref[:, :MEM].T.astype(BF)
            for at in range(NBLK):
                rows_at = pl.ds(pl.multiple_of(BLOCK * order_ref[at], BLOCK), BLOCK)
                start = MEM + BLOCK * at
                dqkv_ref[rows_at, lanes] = from_ref[:, start : start + BLOCK].T.astype(BF)
        drel_ref[...] = drelt_ref[...].T.astype(BF)


def column(rows, at):
    return pl.BlockSpec((rows, LANES), lambda step, order: (0, at))


def attention_specs(pair, first):
    ins = [column(ROWS, first + at) for at in range(3)]
    ins += [column(REL_ROWS, pair), column(ROWS, 0), column(8, pair)]
    exps = pl.BlockSpec((None, 2, BLOCK, KEYS), lambda step, order: (step, 0, 0, 0))
    return ins, exps


def settings(passes):
    return dict(
        compiler_params=pltpu.CompilerParams(
            dimension_semantics=("arbitrary",), vmem_limit_bytes=40 * 1024 * 1024
        ),
        cost_estimate=pl.CostEstimate(
            flops=passes * 4 * MROW * KEYS * BLOCK,
            bytes_accessed=STEPS * 2 * BLOCK * KEYS * 2,
            transcendentals=2 * MROW * KEYS,
        ),
    )


def attention_forward(pair, first, order, qkv, rel, marks, par):
    ins, exps = attention_specs(pair, first)
    return pl.pallas_call(
        forward_kernel,
        grid_spec=pltpu.PrefetchScalarGridSpec(
            num_scalar_prefetch=1,
            grid=(STEPS,),
            in_specs=ins,
            out_specs=[column(MROW, 0), exps, column(MROW, 0)],
            scratch_shapes=[
                pltpu.VMEM((KEYS, 2 * LANES), BF),
                pltpu.VMEM((KEYS, 2 * LANES), BF),
                pltpu.VMEM((2, BLOCK, KEYS), F32),
                pltpu.VMEM((2, BLOCK, 2 * LANES), BF),
                pltpu.VMEM((2, BLOCK, LANES), BF),
                pltpu.VMEM((SPANS, LANES), BF),
                pltpu.VMEM((2, BLOCK, 2 * LANES), F32),
            ],
        ),
        out_shape=[
            jax.ShapeDtypeStruct((MROW, LANES), BF),
            pltpu.HBM((STEPS, 2, BLOCK, KEYS), BF),
            jax.ShapeDtypeStruct((MROW, LANES), F32),
        ],
        **settings(16),
    )(order, qkv, qkv, qkv, rel, marks, par)


def attention_backward(pair, first, order, qkv, rel, marks, par, grad, att, inverse, exps_in):
    ins, exps = attention_specs(pair, first)
    return pl.pallas_call(
        backward_kernel,
        grid_spec=pltpu.PrefetchScalarGridSpec(
            num_scalar_prefetch=1,
            grid=(STEPS,),
            in_specs=ins + [column(MROW, 0)] * 3 + [exps],
            out_specs=[
                pl.BlockSpec((ROWS, 3 * LANES), lambda step, order: (0, 0)),
                column(REL_ROWS, 0),
                column(8, 0),
            ],
            scratch_shapes=[
                pltpu.VMEM((KEYS, 2 * LANES), BF),
                pltpu.VMEM((KEYS, 2 * LANES), BF),
                pltpu.VMEM((BLOCK, BLOCK), BF),
                pltpu.VMEM((2, BLOCK, 2 * LANES), BF),
                pltpu.VMEM((LANES, BLOCK), BF),
                pltpu.VMEM((LANES, BLOCK), BF),
                pltpu.VMEM((LANES, BLOCK), BF),
                pltpu.VMEM((LANES, KEYS), F32),
                pltpu.VMEM((LANES, KEYS), F32),
                pltpu.VMEM((LANES, REL_ROWS), F32),
                pltpu.VMEM((2, BLOCK, 2 * LANES), F32),
                pltpu.VMEM((2, BLOCK, LANES), F32),
                pltpu.VMEM((SPANS, LANES), BF),
                pltpu.VMEM((2, BLOCK, SPANS), BF),
            ],
        ),
        out_shape=[
            jax.ShapeDtypeStruct((ROWS, 3 * LANES), BF),
            jax.ShapeDtypeStruct((REL_ROWS, LANES), BF),
            jax.ShapeDtypeStruct((8, LANES), F32),
        ],
        **settings(24),
    )(order, qkv, qkv, qkv, rel, marks, par, grad, att, inverse, exps_in)


CHUNKS = 2


def norm_parts(values):
    center = values - jnp.mean(values, -1, keepdims=True)
    spread = jnp.mean(center * center, -1, keepdims=True)
    scale = lax.rsqrt(spread + EPSILON)
    return center * scale, scale


def norm_pull(grad, unit, scale, gain):
    grad = grad * gain
    mean = jnp.mean(grad, -1, keepdims=True)
    slope = jnp.mean(grad * unit, -1, keepdims=True)
    return (grad - mean - unit * slope) * scale


def middle_kernel(
    attn_ref,
    hidden_ref,
    query_ref,
    grad_hidden_ref,
    grad_query_ref,
    weights_ref,
    inner_bias_ref,
    small_ref,
    result_ref,
    grad_sum_ref,
    grad_attn_ref,
    gw_ref,
    gb_inner_ref,
    g_small_ref,
    unit_ref,
    scale_ref,
    low_ref,
    low_t_ref,
    act_ref,
    slope_ref,
    sum_ref,
    grad_ref,
    grad_low_ref,
    back_ref,
    held_ref,
    arrived,
):
    step = pl.program_id(0)
    rows, width = attn_ref.shape
    tiles = act_ref.shape[1] // width
    half = hidden_ref.shape[0]
    cut = rows // CHUNKS
    gain_one, shift_one = small_ref[0:1, :], small_ref[1:2, :]
    gain_two, shift_two = small_ref[2:3, :], small_ref[3:4, :]
    parts = [slice(at * cut, at * cut + cut) for at in range(CHUNKS)]

    def fetch(at):
        columns = pl.ds(pl.multiple_of(at * width, width), width)
        return pltpu.make_async_copy(weights_ref.at[:, columns], held_ref.at[at], arrived.at[at])

    @pl.when(step == 0)
    def _():
        fetch(0).start()
        for at in range(tiles):
            fetch(1 + at).start()
            fetch(1 + tiles + at).start()
        fetch(0).wait()
        sum_ref[...] = product(attn_ref[...], held_ref[0])
        sum_ref[:half, :] += hidden_ref[...].astype(F32)
        sum_ref[half:, :] += query_ref[...].astype(F32)
        for part in parts:
            unit, scale = norm_parts(sum_ref[part, :])
            unit_ref[part, :] = unit
            scale_ref[part, :] = jnp.broadcast_to(scale, (cut, LANES))
            first = unit * gain_one + shift_one
            low_ref[part, :] = first.astype(BF)
            sum_ref[part, :] = first + small_ref[4:5, :]

    place_of = jnp.where(step < tiles, step, jnp.minimum(lax.div(step - tiles, 2), tiles - 1))
    columns = pl.ds(pl.multiple_of(place_of * width, width), width)

    w_inner, w_outer = held_ref.at[1 + place_of], held_ref.at[1 + tiles + place_of]

    @pl.when(step < tiles)
    def _():
        fetch(1 + step).wait()
        fetch(1 + tiles + step).wait()
        for part in parts:
            pre = product(low_ref[part, :], w_inner[...]) + inner_bias_ref[...]
            square = pre * pre
            bend = jnp.tanh(0.7978845608028654 * (pre + 0.044715 * square * pre))
            half_bend = 0.5 + 0.5 * bend
            wide = pre * half_bend
            act = wide.astype(BF)
            act_ref[part, columns] = act
            turn = 1.5957691216057308 + 0.2140644488 * square
            slope_ref[part, columns] = half_bend + wide * (1.0 - half_bend) * turn
            sum_ref[part, :] += product(act, w_outer[...])

    @pl.when(step == tiles - 1)
    def _():
        g_gain = g_shift = g_outer = 0.0
        grad_ref[:half, :] = grad_hidden_ref[...].astype(F32)
        grad_ref[half:, :] = grad_query_ref[...].astype(F32)
        for part in parts:
            unit, scale = norm_parts(sum_ref[part, :])
            result_ref[part, :] = (unit * gain_two + shift_two).astype(BF)
            grad = grad_ref[part, :]
            g_gain += jnp.sum(grad * unit, 0, keepdims=True)
            g_shift += jnp.sum(grad, 0, keepdims=True)
            grad = norm_pull(grad, unit, scale, gain_two)
            low = grad.astype(BF)
            grad_ref[part, :] = grad
            grad_low_ref[part, :] = low
            g_outer += jnp.sum(low.astype(F32), 0, keepdims=True)
        g_small_ref[...] = jnp.zeros_like(g_small_ref)
        g_small_ref[2:3, :] = g_gain
        g_small_ref[3:4, :] = g_shift
        g_small_ref[4:5, :] = g_outer
        low_t_ref[...] = low_ref[...].T

    turn_back = jnp.logical_and(step >= tiles, step < 3 * tiles)

    @pl.when(jnp.logical_and(turn_back, lax.rem(step - tiles, 2) == 0))
    def _():
        g_inner = 0.0
        for part in parts:
            back = inner_rows(grad_low_ref[part, :], w_outer[...])
            low = (back * slope_ref[part, columns]).astype(BF)
            back_ref[part, :] = low
            g_inner += jnp.sum(low.astype(F32), 0, keepdims=True)
            grad_ref[part, :] += inner_rows(low, w_inner[...])
        gb_inner_ref[...] = g_inner
        gw_ref[...] = product(low_t_ref[...], back_ref[...]).astype(BF)

    @pl.when(jnp.logical_and(turn_back, lax.rem(step - tiles, 2) == 1))
    def _():
        gw_ref[...] = inner_cols(act_ref[:, columns], grad_low_ref[...]).astype(BF)

    @pl.when(step == 3 * tiles)
    def _():
        g_gain = g_shift = 0.0
        for part in parts:
            unit, scale = unit_ref[part, :], scale_ref[part, 0:1]
            grad = grad_ref[part, :]
            g_gain += jnp.sum(grad * unit, 0, keepdims=True)
            g_shift += jnp.sum(grad, 0, keepdims=True)
            grad = norm_pull(grad, unit, scale, gain_one)
            grad_sum_ref[part, :] = grad
            grad_low_ref[part, :] = grad.astype(BF)
        g_small_ref[0:1, :] = g_gain
        g_small_ref[1:2, :] = g_shift
        gw_ref[...] = inner_cols(attn_ref[...], grad_low_ref[...]).astype(BF)
        grad_attn_ref[...] = inner_rows(grad_low_ref[...], held_ref[0]).astype(BF)


def middle(attn, hidden, query, grad_hidden, grad_query, weights, inner_bias, small):
    rows, width = attn.shape
    tiles = inner_bias.shape[1] // width

    def whole(array):
        return pl.BlockSpec(array.shape, lambda step: (0,) * array.ndim)

    def square(at):
        return pl.BlockSpec((width, width), lambda step: (0, at(step)))

    def back(step):
        return lax.min(lax.div(lax.max(step - tiles, 0), 2), tiles - 1)

    def tile(step):
        return lax.select(step < tiles, step, back(step))

    def written(step):
        odd = lax.rem(lax.max(step - tiles, 0), 2)
        return lax.select(step == 3 * tiles, 0, 1 + back(step) + tiles * odd)

    outs = [
        jax.ShapeDtypeStruct((rows, width), BF),
        jax.ShapeDtypeStruct((rows, width), F32),
        jax.ShapeDtypeStruct((rows, width), BF),
        jax.ShapeDtypeStruct((width, (1 + 2 * tiles) * width), BF),
        jax.ShapeDtypeStruct((1, tiles * width), F32),
        jax.ShapeDtypeStruct((8, width), F32),
    ]
    return pl.pallas_call(
        middle_kernel,
        grid=(1 + 3 * tiles,),
        in_specs=[whole(t) for t in (attn, hidden, query, grad_hidden, grad_query)]
        + [
            pl.BlockSpec(memory_space=pl.ANY),
            pl.BlockSpec((1, width), lambda step: (0, tile(step))),
            whole(small),
        ],
        out_specs=[whole(t) for t in outs[:3]]
        + [
            square(written),
            pl.BlockSpec((1, width), lambda step: (0, back(step))),
            whole(outs[5]),
        ],
        out_shape=outs,
        scratch_shapes=[
            pltpu.VMEM((rows, width), F32),
            pltpu.VMEM((rows, LANES), F32),
            pltpu.VMEM((rows, width), BF),
            pltpu.VMEM((width, rows), BF),
            pltpu.VMEM((rows, tiles * width), BF),
            pltpu.VMEM((rows, tiles * width), F32),
            pltpu.VMEM((rows, width), F32),
            pltpu.VMEM((rows, width), F32),
            pltpu.VMEM((rows, width), BF),
            pltpu.VMEM((rows, width), BF),
            pltpu.VMEM((1 + 2 * tiles, width, width), BF),
            pltpu.SemaphoreType.DMA((1 + 2 * tiles,)),
        ],
        compiler_params=pltpu.CompilerParams(
            dimension_semantics=("arbitrary",), vmem_limit_bytes=VMEM_LIMIT
        ),
        cost_estimate=pl.CostEstimate(
            flops=12 * rows * width * width * tiles,
            bytes_accessed=20 * width * width * tiles,
            transcendentals=rows * width * tiles,
        ),
    )(attn, hidden, query, grad_hidden, grad_query, weights, inner_bias, small)


def swap(values):
    return lax.ppermute(values, "seq", [(0, 1), (1, 0)])


def bit_orders(groups):
    high = list(range(groups.bit_length() - 2, 0, -1))
    return high, high[-1:] + high[:-1]


def across(values, groups, bit):
    return lax.ppermute(values, "fsdp", [(i, i ^ (1 << bit)) for i in range(groups)])


def merged(values, theirs, place, held, bit):
    axis = sum(1 for other in held if other > bit)
    return jnp.where(
        (place >> bit) & 1 == 0,
        jnp.stack([values, theirs], axis),
        jnp.stack([theirs, values], axis),
    )


def gather_beside(one, two, groups, chunks):
    place = lax.axis_index("fsdp")
    order_one, order_two = bit_orders(groups)
    order_one, order_two = order_one + [0], order_two + [0]
    swapped = []
    for at, (bit_one, bit_two) in enumerate(zip(order_one, order_two)):
        left = len(order_one) - at
        take = chunks[: -(-len(chunks) // left)] if len(chunks) >= left else []
        chunks = chunks[len(take) :]
        theirs = [across(one, groups, bit_one), across(two, groups, bit_two)]
        theirs += [swap(chunk) for chunk in take]
        theirs = lax.optimization_barrier(theirs)
        one = merged(one, theirs[0], place, order_one[:at], bit_one)
        two = merged(two, theirs[1], place, order_two[:at], bit_two)
        swapped += theirs[2:]
    bits = len(order_one)
    return (
        one.reshape((-1,) + one.shape[bits + 1 :]),
        two.reshape((-1,) + two.shape[bits + 1 :]),
        swapped,
    )


def shuffle(count, lanes):
    take = jnp.arange(count * lanes)[:, None]
    give = jnp.arange(count * lanes)[None, :]
    return ((take % lanes) * count + take // lanes == give).astype(BF)


def pad_to(values, count):
    return jnp.pad(values, (0, count - values.shape[0]))


def shards(
    hidden,
    query_in,
    memory,
    segment_ids,
    block_order,
    memory_valid,
    w_query,
    w_key,
    w_value,
    w_out,
    w_rel,
    rel_biases,
    seg_embed,
    w_inner,
    b_inner,
    w_outer,
    b_outer,
    norm_gains,
    norm_biases,
    grad_hidden_out,
    grad_query_out,
):
    side = lax.axis_index("seq")
    groups = lax.axis_size("fsdp")
    place_at = lax.axis_index("fsdp")
    half, width = hidden.shape[1:]
    target_half = query_in.shape[1]
    memory_half = memory.shape[1]
    head_width = w_rel.shape[1]
    shard_rows = w_query.shape[0]
    ffn_width = w_inner.shape[1]
    own_rows = half + target_half

    def by_side(own, other, axis):
        return jnp.where(
            side == 0,
            jnp.concatenate([own, other], axis),
            jnp.concatenate([other, own], axis),
        )

    pairs = head_width // LANES
    pair_width = 3 * LANES

    def head_columns(weight, pair):
        return lax.dynamic_slice_in_dim(weight, side * head_width + pair * LANES, LANES, 1)

    def pair_columns(pair):
        return [head_columns(weight, pair) for weight in (w_query, w_key, w_value)]

    few = jnp.concatenate([rel_biases, seg_embed], 0)
    few = jnp.pad(few, ((0, shard_rows - 5), (0, LANES - few.shape[1])))
    quarter = half // 2
    weights_one, weights_two, swapped = gather_beside(
        jnp.concatenate(sum([pair_columns(pair) for pair in range(pairs - 1)], []), 1),
        jnp.concatenate(pair_columns(pairs - 1) + [w_rel, few], 1),
        groups,
        [hidden[0, :quarter], hidden[0, quarter:], memory[0], query_in[0]],
    )
    rel_weight = weights_two[:, pair_width : pair_width + head_width]
    few_all = weights_two[:, pair_width + head_width :].reshape(groups, shard_rows, LANES)
    few_all = few_all[:, :5, : head_width // groups].astype(F32)
    few_all = few_all.transpose(1, 0, 2).reshape(5, head_width)

    blocks = ffn_width // width
    spots = shuffle(blocks, LANES)
    smalls = (b_inner, b_outer, norm_gains, norm_biases)
    small_flat = pad_to(jnp.concatenate([t.reshape(-1) for t in smalls]), shard_rows * LANES)
    inner_moved = lax.dot_general(
        w_inner.reshape(shard_rows, -1, blocks * LANES),
        spots,
        (((2,), (1,)), ((), ())),
        preferred_element_type=F32,
    ).astype(BF)
    inner_moved = inner_moved.reshape(shard_rows, -1, blocks, LANES).transpose(0, 2, 1, 3)
    mixed = jnp.concatenate(
        [
            w_out,
            inner_moved.reshape(shard_rows, ffn_width),
            w_outer.reshape(shard_rows, ffn_width),
            small_flat.reshape(shard_rows, LANES),
        ],
        1,
    )
    mixed, weights_one, swapped = lax.optimization_barrier((mixed, weights_one, swapped))
    mixed = lax.all_gather(mixed, "fsdp", axis=0, tiled=True)
    small_all = mixed[:, width + 2 * ffn_width :].reshape(groups, shard_rows * LANES).astype(F32)

    def unpack():
        found, at = [], 0
        for small in smalls:
            piece = small_all[:, at : at + small.size].reshape((groups,) + small.shape)
            found.append(jnp.moveaxis(piece, 0, -2).reshape(small.shape[:-1] + (-1,)))
            at += small.size
        return found

    inner_bias, outer_bias, gains, shifts = unpack()

    cuts = ((0, half), (half, own_rows))
    far_hidden = jnp.concatenate(swapped[:2], 0)
    stacked = jnp.concatenate(
        [
            by_side(hidden[0], far_hidden, 0),
            by_side(query_in[0], swapped[3], 0),
            by_side(memory[0], swapped[2], 0),
        ],
        0,
    )

    qkv_one = product(stacked, weights_one).astype(BF)
    qkv_two = product(stacked, weights_two[:, :pair_width]).astype(BF)
    pos_table = sinusoid(REL_ROWS, width, MEM + L - 1).astype(BF)
    rel = product(pos_table, rel_weight).astype(BF)
    par = jnp.concatenate([few_all, jnp.zeros((3, head_width), F32)], 0)
    order = block_order[0]
    segs = segment_ids[0]
    target_seg = lax.dynamic_slice_in_dim(segs, MEM + order[NBLK - 1] * BLOCK, BLOCK)
    seg_rows = jnp.concatenate([segs[MEM:], target_seg, segs[:MEM]])
    invalid = jnp.concatenate([jnp.zeros((MROW,), jnp.int32), (memory_valid[0] != 1).astype(jnp.int32)])
    lane = jnp.arange(LANES)[None, :]
    marks = jnp.where(lane < 6, seg_rows[:, None] == lane % 3, (lane == 6) | (lane == 7))
    marks = jnp.where(lane == 8, invalid[:, None] == 1, marks).astype(BF)

    def rows_of(values, which):
        return jnp.concatenate(
            [
                lax.dynamic_slice_in_dim(values, which * half, half, 0),
                lax.dynamic_slice_in_dim(values, L + which * target_half, target_half, 0),
            ],
            0,
        )

    def pair_args(pair):
        last = pair == pairs - 1
        at = (0, qkv_two) if last else (3 * pair, qkv_one)
        return (pair, at[0], order, at[1], rel, marks, par)

    kept = []
    own_att, far_att = [], []
    for pair in range(pairs):
        att, exps, inverse = attention_forward(*pair_args(pair))
        kept.append((att, inverse, exps))
        own_att.append(rows_of(att, side))
        far_att.append(swap(rows_of(att, 1 - side)))
    attn_rows = by_side(jnp.concatenate(own_att, 1), jnp.concatenate(far_att, 1), 1)
    small = jnp.stack([gains[0], shifts[0], gains[1], shifts[1], outer_bias] + [outer_bias] * 3)
    result, grad_sum_one, grad_attn, grad_weights, grad_b_inner, grad_small = middle(
        attn_rows,
        hidden[0],
        query_in[0],
        grad_hidden_out[0],
        grad_query_out[0],
        mixed,
        inner_bias.reshape(width, blocks).T.reshape(1, ffn_width),
        small,
    )

    devices = 2 * groups
    out_rows = width // devices
    token_sums = lax.psum_scatter(
        grad_weights, ("seq", "fsdp"), scatter_dimension=0, tiled=True
    )
    out_out = token_sums[:, :width].astype(F32)
    out_outer = token_sums[:, width + ffn_width :].reshape(blocks * out_rows, width).astype(F32)
    inner_sums = token_sums[:, width : width + ffn_width].reshape(out_rows, blocks, -1, LANES)
    out_inner = product(
        inner_sums.transpose(0, 2, 1, 3).reshape(out_rows, -1, blocks * LANES), spots
    ).reshape(out_rows, ffn_width)
    grad_b_inner = grad_b_inner.reshape(blocks, width).T.reshape(devices, -1)
    row_count = width // devices
    token_flat = jnp.concatenate(
        [
            grad_b_inner.reshape(devices, -1),
            grad_small[:5].reshape(5, devices, -1).transpose(1, 0, 2).reshape(devices, -1),
        ],
        1,
    )
    inner_count = ffn_width // devices

    weights_two = weights_two[:, :pair_width]
    weights_one, weights_two, attn_rows = lax.optimization_barrier(
        (weights_one, weights_two, attn_rows)
    )
    far_one, far_two = swap(weights_one), swap(weights_two)

    def pair_grad(pair, which):
        at = which * head_width + pair * LANES
        return lax.dynamic_slice_in_dim(grad_attn, at, LANES, 1)

    far_grads = [swap(pair_grad(pair, 1 - side)) for pair in range(pairs)]

    def sum_message(message):
        message = lax.all_to_all(message, "fsdp", split_axis=0, concat_axis=0, tiled=True)
        return jnp.sum(message.astype(F32), 0)

    own_rows_grads, far_rows_grads, sums, few_grads = [], [], [], []
    for pair in range(pairs):
        own, far = pair_grad(pair, side), far_grads[pair]
        if pair:
            own, message, sums = lax.optimization_barrier((own, message, sums))
            sums.append(sum_message(message))
        head_grad = jnp.concatenate([by_side(own[a:b], far[a:b], 0) for a, b in cuts], 0)
        dqkv, drel, dpar = attention_backward(*pair_args(pair), head_grad, *kept[pair])
        if pair == pairs - 1:
            dqkv, sums = lax.optimization_barrier((dqkv, sums))
        few_grads.append(dpar[:5])
        own_rows_grads.append(rows_of(dqkv, side))
        far_rows_grads.append(swap(rows_of(dqkv, 1 - side)))
        grad_pair = inner_cols(stacked, dqkv).astype(BF)
        grad_pair = grad_pair.reshape(2, groups, out_rows, pair_width).transpose(1, 0, 2, 3)
        message = jnp.concatenate(
            [
                grad_pair.reshape(groups, shard_rows, pair_width),
                inner_cols(pos_table, drel).astype(BF).reshape(groups, shard_rows, LANES),
            ],
            2,
        )
        if pair == 0:
            token_flat = token_flat.reshape(2, groups, -1).transpose(1, 0, 2).astype(BF)
            extra = ((0, 0), (0, 6), (0, pair_width + LANES - token_flat.shape[2]))
            message = jnp.concatenate([message, jnp.pad(token_flat, extra)], 1)
        if pair == pairs - 1:
            few = jnp.concatenate(few_grads, 1).reshape(5, groups, head_width // groups)
            few = few.transpose(1, 0, 2).reshape(groups, 1, -1).astype(BF)
            few = jnp.pad(few, ((0, 0), (0, 7), (0, pair_width + LANES - few.shape[2])))
            message = jnp.concatenate([message, few], 1)
    sums.append(sum_message(message))

    early = slice(0, pairs - 1)
    grad_own = grad_sum_one + inner_rows(
        jnp.concatenate(own_rows_grads + far_rows_grads[early], 1),
        jnp.concatenate([weights_one, weights_two, far_one], 1),
    )
    grad_own = grad_own + inner_rows(far_rows_grads[-1], far_two)

    both_sums = jnp.concatenate([t[:shard_rows, :pair_width] for t in sums], 1)
    own_sum = lax.dynamic_slice_in_dim(both_sums, side * out_rows, out_rows, 0)
    far_sum = lax.dynamic_slice_in_dim(both_sums, (1 - side) * out_rows, out_rows, 0)
    far_sum = swap(far_sum.astype(BF)).astype(F32)
    small_sums = lax.dynamic_index_in_dim(sums[0], shard_rows + side, 0, False)
    small_sums += swap(
        lax.dynamic_index_in_dim(sums[0], shard_rows + 1 - side, 0, False).astype(BF)
    ).astype(F32)
    out_b_inner = small_sums[:inner_count]
    out_rest = small_sums[inner_count : inner_count + 5 * row_count].reshape(5, row_count)
    out_gains, out_shifts, out_b_outer = out_rest[0:4:2], out_rest[1:4:2], out_rest[4]

    def weight_rows(values, which):
        return [
            values[:, pair * pair_width + which * LANES :][:, :LANES] for pair in range(pairs)
        ]

    out_query, out_key, out_value = (
        by_side(
            jnp.concatenate(weight_rows(own_sum, which), 1),
            jnp.concatenate(weight_rows(far_sum, which), 1),
            1,
        )
        for which in range(3)
    )
    out_rel = jnp.concatenate([t[:shard_rows, pair_width:] for t in sums], 1)
    few_sum = sums[-1][shard_rows, : 5 * (head_width // groups)].reshape(5, -1)
    out_biases, out_seg = few_sum[:3], few_sum[3:]
    return (
        result[None, :half],
        result[None, half:],
        grad_own[None, :half],
        grad_own[None, half:],
        out_query,
        out_key,
        out_value,
        out_out,
        out_rel,
        out_biases,
        out_seg,
        out_inner,
        out_b_inner,
        out_outer,
        out_b_outer,
        out_gains,
        out_shifts,
    )


def solution(mesh):
    rows = P("fsdp", "seq", None)
    both = ("seq", "fsdp")
    in_specs = (
        (rows,) * 3
        + (P("fsdp", None),) * 7
        + (P("fsdp", "seq"), P(None, both), P(None, both))
        + (P("fsdp", None), P("fsdp"), P("fsdp", None), P("fsdp"))
        + (P(None, "fsdp"), P(None, "fsdp"))
        + (rows,) * 2
    )
    out_specs = (
        (rows,) * 4
        + (P(both, None),) * 4
        + (P("fsdp", "seq"), P(None, both), P(None, both))
        + (P(both, None), P(both), P(both, None), P(both))
        + (P(None, both), P(None, both))
    )
    return jax.shard_map(shards, mesh=mesh, in_specs=in_specs, out_specs=out_specs, check_vma=False)
```

```python
import functools

import jax
import jax.numpy as jnp
from jax import lax
from jax.experimental import pallas as pl
from jax.experimental.pallas import tpu as pltpu
from jax.sharding import PartitionSpec as P

DH = 64
BLOCK = 256
NBLK = 4
MEM = 384
L = 1024
LANES = 128

QROW = L
MROW = L + BLOCK
ROWS = L + BLOCK + MEM
KEYS = MEM + L
SPAN_M = MEM + BLOCK
SPAN_T = 2 * BLOCK
REL_M = L - BLOCK
REL_T = MEM + L - BLOCK
REL_ROWS = MEM + 2 * L
SPANS = SPAN_M + NBLK * SPAN_T

EPSILON = 1e-05
NEGATIVE = -1e30
SCORE_SCALE = 0.125
EXP2_SCALE = SCORE_SCALE * 1.4426950408889634
STEPS = NBLK + 1
VMEM_LIMIT = 60 * 1024 * 1024
BF = jnp.bfloat16
F32 = jnp.float32


def product(left, right):
    return jnp.dot(left, right, preferred_element_type=F32)


def inner_rows(left, right):
    return lax.dot_general(left, right, (((1,), (1,)), ((), ())), preferred_element_type=F32)


def inner_cols(left, right):
    return lax.dot_general(left, right, (((0,), (0,)), ((), ())), preferred_element_type=F32)


def sinusoid(row_count, width_all, farthest):
    fine = DH
    frequency = 10000.0 ** (-jnp.arange(0, width_all, 2).astype(F32) / width_all)
    starts = (farthest - fine * jnp.arange(row_count // fine)).astype(F32)
    far = starts[:, None, None] * frequency
    near = jnp.arange(fine).astype(F32)[None, :, None] * frequency
    sines = jnp.sin(far) * jnp.cos(near) - jnp.cos(far) * jnp.sin(near)
    cosines = jnp.cos(far) * jnp.cos(near) + jnp.sin(far) * jnp.sin(near)
    return jnp.concatenate([sines, cosines], 2).reshape(row_count, width_all)


def split_low(values):
    high = values.astype(BF).astype(F32)
    return high, values - high


def place(step, order_ref):
    last = jnp.minimum(step, NBLK - 1)
    block = order_ref[last]
    row = jnp.where(step < NBLK, block, NBLK) * BLOCK
    return block, pl.multiple_of(row, BLOCK), last


def row_terms(q_ref, kx_ref, par_ref, row):
    query = q_ref[pl.ds(row, BLOCK), :].astype(F32)
    marks = kx_ref[pl.ds(row, BLOCK), :].astype(F32)
    return query + par_ref[0:1, :], query + par_ref[1:2, :], query + par_ref[2:3, :], marks


def gather_keys(order_ref, from_ref, to_ref, lanes):
    to_ref[:MEM, lanes] = from_ref[MROW:, :]
    for at in range(NBLK):
        rows = pl.ds(pl.multiple_of(BLOCK * order_ref[at], BLOCK), BLOCK)
        to_ref[MEM + BLOCK * at : MEM + BLOCK * (at + 1), lanes] = from_ref[rows, :]


def key_spots(order_ref, block, count):
    spots = [(0, MEM, pl.multiple_of(REL_M - BLOCK * block, BLOCK), 0)]
    for at in range(count):
        rel_row = pl.multiple_of(REL_T + BLOCK * (order_ref[at] - block), LANES)
        spots.append((MEM + BLOCK * at, BLOCK, rel_row, SPAN_M + SPAN_T * at))
    return spots


def gather_spans(spots, rel_ref, span_ref):
    for _, key_count, rel_row, put in spots:
        span = key_count + BLOCK
        span_ref[put : put + span, :] = rel_ref[pl.ds(rel_row, span), :]


def forward_kernel(
    order_ref,
    q_ref,
    k_ref,
    v_ref,
    rel_ref,
    kx_ref,
    par_ref,
    att_ref,
    exp_ref,
    inv_ref,
    kcat_ref,
    vcat_ref,
    score_ref,
    lhs_ref,
    qr_ref,
    span_ref,
    sum_ref,
):
    step = pl.program_id(0)

    @pl.when(step == 0)
    def _():
        gather_keys(order_ref, k_ref, kcat_ref, slice(0, LANES))
        gather_keys(order_ref, kx_ref, kcat_ref, slice(LANES, 2 * LANES))
        gather_keys(order_ref, v_ref, vcat_ref, slice(0, LANES))
        vcat_ref[:, LANES:] = jnp.ones((KEYS, LANES), BF)

    block, row, last = place(step, order_ref)
    lane = lax.broadcasted_iota(jnp.int32, (BLOCK, LANES), 1)
    query_w, query_r, query_s, marks = row_terms(q_ref, kx_ref, par_ref, row)
    same, other = query_s * par_ref[3:4, :], query_s * par_ref[4:5, :]
    for head in range(2):
        mine = (lane < DH) == (head == 0)
        other_sum = jnp.sum(jnp.where(mine, other, 0.0), -1, keepdims=True)
        diff = jnp.sum(jnp.where(mine, same, 0.0), -1, keepdims=True) - other_sum
        diff_high, diff_low = split_low(diff)
        other_high, other_low = split_low(other_sum)
        extra = jnp.where(lane < 3, marks * diff_high, jnp.where(lane < 6, marks * diff_low, 0.0))
        extra = jnp.where(lane == 6, other_high, jnp.where(lane == 7, other_low, extra))
        extra = jnp.where(lane == 8, NEGATIVE, extra)
        lhs_ref[head, :, :LANES] = jnp.where(mine, query_w, 0.0).astype(BF)
        lhs_ref[head, :, LANES:] = extra.astype(BF)
        qr_ref[head] = jnp.where(mine, query_r, 0.0).astype(BF)

    across = lax.broadcasted_iota(jnp.int32, (BLOCK, BLOCK), 0) - lax.broadcasted_iota(
        jnp.int32, (BLOCK, BLOCK), 1
    )
    hidden_at = jnp.where(step < NBLK, BLOCK, 0)

    for count in range(NBLK):

        @pl.when(last == count)
        def _():
            spots = key_spots(order_ref, block, count + 1)
            keys = MEM + BLOCK * (count + 1)
            spans = SPAN_M + SPAN_T * (count + 1)
            gather_spans(spots, rel_ref, span_ref)
            for head in range(2):
                content = inner_rows(lhs_ref[head], kcat_ref[:keys, :])
                position = inner_rows(qr_ref[head], span_ref[:spans, :])
                top = None
                for at, key_count, _, put in spots:
                    span = key_count + BLOCK
                    moved = position[:, put : put + span]
                    moved = pltpu.roll(moved, span - BLOCK + 1, 1, stride=1, stride_axis=0)
                    tile = content[:, at : at + key_count] + moved[:, :key_count]
                    if at + key_count == keys:
                        tile = jnp.where(across == hidden_at, NEGATIVE, tile)
                    score_ref[head, :, at : at + key_count] = tile
                    for piece in range(0, key_count, LANES):
                        part = tile[:, piece : piece + LANES]
                        top = part if top is None else jnp.maximum(top, part)
                peak = jnp.max(top, -1, keepdims=True)
                low = jnp.exp2((score_ref[head, :, :keys] - peak) * EXP2_SCALE).astype(BF)
                exp_ref[head, :, :keys] = low
                sum_ref[head] = product(low, vcat_ref[:keys, :])

    sums = sum_ref[0], sum_ref[1]
    first = lane < DH
    inverse = 1.0 / jnp.where(first, sums[0][:, LANES:], sums[1][:, LANES:])
    total = jnp.where(first, sums[0][:, :LANES], sums[1][:, :LANES])
    att_ref[pl.ds(row, BLOCK), :] = (total * inverse).astype(BF)
    inv_ref[pl.ds(row, BLOCK), :] = inverse


def backward_kernel(
    order_ref,
    q_ref,
    k_ref,
    v_ref,
    rel_ref,
    kx_ref,
    par_ref,
    grad_ref,
    att_ref,
    inv_ref,
    exp_ref,
    dqkv_ref,
    drel_ref,
    dpar_ref,
    kcat_ref,
    vcat_ref,
    flip_ref,
    lhs_ref,
    qwt_ref,
    qrt_ref,
    gt_ref,
    dkt_ref,
    dvt_ref,
    drelt_ref,
    accw_ref,
    accr_ref,
    span_ref,
    moved_ref,
):
    step = pl.program_id(0)

    @pl.when(step == 0)
    def _():
        gather_keys(order_ref, k_ref, kcat_ref, slice(0, LANES))
        gather_keys(order_ref, kx_ref, kcat_ref, slice(LANES, 2 * LANES))
        gather_keys(order_ref, v_ref, vcat_ref, slice(0, LANES))
        vcat_ref[:, :LANES] = (vcat_ref[:, :LANES].astype(F32) * SCORE_SCALE).astype(BF)
        vcat_ref[:, LANES:] = jnp.full((KEYS, LANES), SCORE_SCALE, BF)
        up = lax.broadcasted_iota(jnp.int32, (BLOCK, BLOCK), 0)
        down = lax.broadcasted_iota(jnp.int32, (BLOCK, BLOCK), 1)
        flip_ref[...] = jnp.where(up + down == BLOCK - 1, 1.0, 0.0).astype(BF)
        dkt_ref[...] = jnp.zeros_like(dkt_ref)
        dvt_ref[...] = jnp.zeros_like(dvt_ref)
        drelt_ref[...] = jnp.zeros_like(drelt_ref)
        dpar_ref[...] = jnp.zeros_like(dpar_ref)

    block, row, last = place(step, order_ref)
    lane = lax.broadcasted_iota(jnp.int32, (BLOCK, LANES), 1)
    first = lane < DH
    flip = flip_ref[...]
    rows = pl.ds(row, BLOCK)
    grad_low = (grad_ref[rows, :].astype(F32) * inv_ref[rows, :]).astype(BF)
    query, marks = product(flip, q_ref[rows, :]), product(flip, kx_ref[rows, :])
    grad, att = product(flip, grad_low), product(flip, att_ref[rows, :])
    query_w = query + par_ref[0:1, :]
    query_r = query + par_ref[1:2, :]
    query_s = query + par_ref[2:3, :]
    dots = grad * att
    for head in range(2):
        mine = first == (head == 0)
        high, low = split_low(-jnp.sum(jnp.where(mine, dots, 0.0), -1, keepdims=True))
        extra = jnp.where(lane == 0, high, jnp.where(lane == 1, low, 0.0))
        lhs_ref[head, :, :LANES] = jnp.where(mine, grad, 0.0).astype(BF)
        lhs_ref[head, :, LANES:] = extra.astype(BF)
    qwt_ref[...] = query_w.astype(BF).astype(F32).T.astype(BF)
    qrt_ref[...] = query_r.astype(BF).astype(F32).T.astype(BF)
    gt_ref[...] = grad_low.astype(F32).T.astype(BF)

    for count in range(NBLK):

        @pl.when(last == count)
        def _():
            spots = key_spots(order_ref, block, count + 1)
            keys = MEM + BLOCK * (count + 1)
            spans = SPAN_M + SPAN_T * (count + 1)
            gather_spans(spots, rel_ref, span_ref)
            for head in range(2):
                own = slice(DH * head, DH * head + DH)
                probs = exp_ref[head, :, :keys]
                slope = inner_rows(lhs_ref[head], vcat_ref[:keys, :])
                scaled = (product(flip, probs) * slope).astype(BF)
                for at, key_count, _, put in spots:
                    span = key_count + BLOCK
                    moved = jnp.concatenate(
                        [scaled[:, at : at + key_count], jnp.zeros((BLOCK, BLOCK), BF)], 1
                    )
                    moved_ref[head, :, put : put + span] = pltpu.roll(
                        moved, 0, 1, stride=1, stride_axis=0
                    )
                dkt_ref[own, :keys] += product(qwt_ref[own, :], scaled)
                dvt_ref[own, :keys] += product(gt_ref[own, :], probs)
                accw_ref[head] = product(scaled, kcat_ref[:keys, :])
                accr_ref[head] = product(moved_ref[head, :, :spans], span_ref[:spans, :])
                drel = product(qrt_ref[own, :], moved_ref[head, :, :spans])
                for _, key_count, rel_row, put in spots:
                    span = key_count + BLOCK
                    drelt_ref[own, pl.ds(rel_row, span)] += drel[:, put : put + span]

    grad_w = jnp.where(first, accw_ref[0, :, :LANES], accw_ref[1, :, :LANES])
    grad_r = jnp.where(first, accr_ref[0], accr_ref[1])
    same_sums, other_sums = [], []
    for head in range(2):
        sums = accw_ref[head, :, LANES:]
        same_sums.append(jnp.sum(jnp.where(lane < 3, marks * sums, 0.0), -1, keepdims=True))
        total = jnp.sum(jnp.where(lane == 6, sums, 0.0), -1, keepdims=True)
        other_sums.append(total - same_sums[head])
    same = jnp.where(first, same_sums[0], same_sums[1])
    other = jnp.where(first, other_sums[0], other_sums[1])
    grad_s = same * par_ref[3:4, :] + other * par_ref[4:5, :]
    high, low = split_low(grad_w + grad_r + grad_s)
    dqkv_ref[rows, :LANES] = (
        product(flip, high.astype(BF)) + product(flip, low.astype(BF))
    ).astype(BF)
    for at, terms in enumerate((grad_w, grad_r, grad_s, same * query_s, other * query_s)):
        dpar_ref[at : at + 1, :] += jnp.sum(terms, 0, keepdims=True)

    @pl.when(step == STEPS - 1)
    def _():
        dqkv_ref[MROW:, :LANES] = jnp.zeros((MEM, LANES), BF)
        dqkv_ref[L:MROW, LANES:] = jnp.zeros((BLOCK, 2 * LANES), BF)
        for lanes, from_ref in ((1, dkt_ref), (2, dvt_ref)):
            lanes = slice(lanes * LANES, (lanes + 1) * LANES)
            dqkv_ref[MROW:, lanes] = from_ref[:, :MEM].T.astype(BF)
            for at in range(NBLK):
                rows_at = pl.ds(pl.multiple_of(BLOCK * order_ref[at], BLOCK), BLOCK)
                start = MEM + BLOCK * at
                dqkv_ref[rows_at, lanes] = from_ref[:, start : start + BLOCK].T.astype(BF)
        drel_ref[...] = drelt_ref[...].T.astype(BF)


def column(rows, at):
    return pl.BlockSpec((rows, LANES), lambda step, order: (0, at))


def attention_specs(pair, first):
    ins = [column(ROWS, first + at) for at in range(3)]
    ins += [column(REL_ROWS, pair), column(ROWS, 0), column(8, pair)]
    exps = pl.BlockSpec((None, 2, BLOCK, KEYS), lambda step, order: (step, 0, 0, 0))
    return ins, exps


def settings(passes):
    return dict(
        compiler_params=pltpu.CompilerParams(
            dimension_semantics=("arbitrary",), vmem_limit_bytes=40 * 1024 * 1024
        ),
        cost_estimate=pl.CostEstimate(
            flops=passes * 4 * MROW * KEYS * BLOCK,
            bytes_accessed=STEPS * 2 * BLOCK * KEYS * 2,
            transcendentals=2 * MROW * KEYS,
        ),
    )


def attention_forward(pair, first, order, qkv, rel, marks, par):
    ins, exps = attention_specs(pair, first)
    return pl.pallas_call(
        forward_kernel,
        grid_spec=pltpu.PrefetchScalarGridSpec(
            num_scalar_prefetch=1,
            grid=(STEPS,),
            in_specs=ins,
            out_specs=[column(MROW, 0), exps, column(MROW, 0)],
            scratch_shapes=[
                pltpu.VMEM((KEYS, 2 * LANES), BF),
                pltpu.VMEM((KEYS, 2 * LANES), BF),
                pltpu.VMEM((2, BLOCK, KEYS), F32),
                pltpu.VMEM((2, BLOCK, 2 * LANES), BF),
                pltpu.VMEM((2, BLOCK, LANES), BF),
                pltpu.VMEM((SPANS, LANES), BF),
                pltpu.VMEM((2, BLOCK, 2 * LANES), F32),
            ],
        ),
        out_shape=[
            jax.ShapeDtypeStruct((MROW, LANES), BF),
            pltpu.HBM((STEPS, 2, BLOCK, KEYS), BF),
            jax.ShapeDtypeStruct((MROW, LANES), F32),
        ],
        **settings(16),
    )(order, qkv, qkv, qkv, rel, marks, par)


def attention_backward(pair, first, order, qkv, rel, marks, par, grad, att, inverse, exps_in):
    ins, exps = attention_specs(pair, first)
    qkv, rel, exps_in = (
        pltpu.with_memory_space_constraint(t, pltpu.HBM) for t in (qkv, rel, exps_in)
    )
    return pl.pallas_call(
        backward_kernel,
        grid_spec=pltpu.PrefetchScalarGridSpec(
            num_scalar_prefetch=1,
            grid=(STEPS,),
            in_specs=ins + [column(MROW, 0)] * 3 + [exps],
            out_specs=[
                pl.BlockSpec((ROWS, 3 * LANES), lambda step, order: (0, 0)),
                column(REL_ROWS, 0),
                column(8, 0),
            ],
            scratch_shapes=[
                pltpu.VMEM((KEYS, 2 * LANES), BF),
                pltpu.VMEM((KEYS, 2 * LANES), BF),
                pltpu.VMEM((BLOCK, BLOCK), BF),
                pltpu.VMEM((2, BLOCK, 2 * LANES), BF),
                pltpu.VMEM((LANES, BLOCK), BF),
                pltpu.VMEM((LANES, BLOCK), BF),
                pltpu.VMEM((LANES, BLOCK), BF),
                pltpu.VMEM((LANES, KEYS), F32),
                pltpu.VMEM((LANES, KEYS), F32),
                pltpu.VMEM((LANES, REL_ROWS), F32),
                pltpu.VMEM((2, BLOCK, 2 * LANES), F32),
                pltpu.VMEM((2, BLOCK, LANES), F32),
                pltpu.VMEM((SPANS, LANES), BF),
                pltpu.VMEM((2, BLOCK, SPANS), BF),
            ],
        ),
        out_shape=[
            jax.ShapeDtypeStruct((ROWS, 3 * LANES), BF),
            jax.ShapeDtypeStruct((REL_ROWS, LANES), BF),
            jax.ShapeDtypeStruct((8, LANES), F32),
        ],
        **settings(24),
    )(order, qkv, qkv, qkv, rel, marks, par, grad, att, inverse, exps_in)


CHUNKS = 2


def norm_parts(values):
    center = values - jnp.mean(values, -1, keepdims=True)
    spread = jnp.mean(center * center, -1, keepdims=True)
    scale = lax.rsqrt(spread + EPSILON)
    return center * scale, scale


def norm_pull(grad, unit, scale, gain):
    grad = grad * gain
    mean = jnp.mean(grad, -1, keepdims=True)
    slope = jnp.mean(grad * unit, -1, keepdims=True)
    return (grad - mean - unit * slope) * scale


def dealt(values, groups):
    if groups is None:
        return values.astype(BF)
    share = values.shape[0] // (2 * groups)
    pieces = [
        values[(side * groups + at) * share :][:share] for at in range(groups) for side in range(2)
    ]
    return jnp.concatenate(pieces, 0).astype(BF)


def middle_kernel(
    groups,
    side_ref,
    attn_ref,
    hidden_ref,
    query_ref,
    grad_hidden_ref,
    grad_query_ref,
    weights_ref,
    inner_bias_ref,
    small_ref,
    result_ref,
    grad_sum_ref,
    grad_attn_ref,
    gw_ref,
    gb_inner_ref,
    g_small_ref,
    unit_ref,
    scale_ref,
    low_ref,
    low_t_ref,
    act_ref,
    slope_ref,
    sum_ref,
    grad_ref,
    grad_low_ref,
    back_ref,
    held_ref,
    arrived,
):
    step = pl.program_id(0)
    rows, width = attn_ref.shape
    tiles = act_ref.shape[1] // width
    half = hidden_ref.shape[0]
    cut = rows // CHUNKS
    gain_one, shift_one = small_ref[0:1, :], small_ref[1:2, :]
    gain_two, shift_two = small_ref[2:3, :], small_ref[3:4, :]
    parts = [slice(at * cut, at * cut + cut) for at in range(CHUNKS)]

    def fetch(at):
        columns = pl.ds(pl.multiple_of(at * width, width), width)
        return pltpu.make_async_copy(weights_ref.at[:, columns], held_ref.at[at], arrived.at[at])

    @pl.when(step == 0)
    def _():
        fetch(0).start()
        for at in range(tiles):
            fetch(1 + at).start()
            fetch(1 + tiles + at).start()
        fetch(0).wait()
        sum_ref[...] = product(attn_ref[...], held_ref[0])
        sum_ref[:half, :] += hidden_ref[...].astype(F32)
        sum_ref[half:, :] += query_ref[...].astype(F32)
        for part in parts:
            unit, scale = norm_parts(sum_ref[part, :])
            unit_ref[part, :] = unit
            scale_ref[part, :] = jnp.broadcast_to(scale, (cut, LANES))
            first = unit * gain_one + shift_one
            low_ref[part, :] = first.astype(BF)
            sum_ref[part, :] = first + small_ref[4:5, :]

    place_of = jnp.where(step < tiles, step, jnp.minimum(lax.div(step - tiles, 2), tiles - 1))
    columns = pl.ds(pl.multiple_of(place_of * width, width), width)

    w_inner, w_outer = held_ref.at[1 + place_of], held_ref.at[1 + tiles + place_of]

    @pl.when(step < tiles)
    def _():
        fetch(1 + step).wait()
        fetch(1 + tiles + step).wait()
        for part in parts:
            pre = product(low_ref[part, :], w_inner[...]) + inner_bias_ref[...]
            square = pre * pre
            bend = jnp.tanh(0.7978845608028654 * (pre + 0.044715 * square * pre))
            half_bend = 0.5 + 0.5 * bend
            wide = pre * half_bend
            act = wide.astype(BF)
            act_ref[part, columns] = act
            turn = 1.5957691216057308 + 0.2140644488 * square
            slope_ref[part, columns] = half_bend + wide * (1.0 - half_bend) * turn
            sum_ref[part, :] += product(act, w_outer[...])

    @pl.when(step == tiles - 1)
    def _():
        g_gain = g_shift = g_outer = 0.0
        grad_ref[:half, :] = grad_hidden_ref[...].astype(F32)
        grad_ref[half:, :] = grad_query_ref[...].astype(F32)
        for part in parts:
            unit, scale = norm_parts(sum_ref[part, :])
            result_ref[part, :] = (unit * gain_two + shift_two).astype(BF)
            grad = grad_ref[part, :]
            g_gain += jnp.sum(grad * unit, 0, keepdims=True)
            g_shift += jnp.sum(grad, 0, keepdims=True)
            grad = norm_pull(grad, unit, scale, gain_two)
            low = grad.astype(BF)
            grad_ref[part, :] = grad
            grad_low_ref[part, :] = low
            g_outer += jnp.sum(low.astype(F32), 0, keepdims=True)
        g_small_ref[...] = jnp.zeros_like(g_small_ref)
        g_small_ref[2:3, :] = g_gain
        g_small_ref[3:4, :] = g_shift
        g_small_ref[4:5, :] = g_outer
        low_t_ref[...] = low_ref[...].T

    turn_back = jnp.logical_and(step >= tiles, step < 3 * tiles)

    @pl.when(jnp.logical_and(turn_back, lax.rem(step - tiles, 2) == 0))
    def _():
        g_inner = 0.0
        for part in parts:
            back = inner_rows(grad_low_ref[part, :], w_outer[...])
            low = (back * slope_ref[part, columns]).astype(BF)
            back_ref[part, :] = low
            g_inner += jnp.sum(low.astype(F32), 0, keepdims=True)
            grad_ref[part, :] += inner_rows(low, w_inner[...])
        gb_inner_ref[...] = g_inner
        gw_ref[...] = dealt(product(low_t_ref[...], back_ref[...]), groups)

    @pl.when(jnp.logical_and(turn_back, lax.rem(step - tiles, 2) == 1))
    def _():
        gw_ref[...] = dealt(inner_cols(act_ref[:, columns], grad_low_ref[...]), groups)

    @pl.when(step == 3 * tiles)
    def _():
        g_gain = g_shift = 0.0
        for part in parts:
            unit, scale = unit_ref[part, :], scale_ref[part, 0:1]
            grad = grad_ref[part, :]
            g_gain += jnp.sum(grad * unit, 0, keepdims=True)
            g_shift += jnp.sum(grad, 0, keepdims=True)
            grad = norm_pull(grad, unit, scale, gain_one)
            grad_sum_ref[part, :] = grad
            grad_low_ref[part, :] = grad.astype(BF)
        g_small_ref[0:1, :] = g_gain
        g_small_ref[1:2, :] = g_shift
        gw_ref[...] = dealt(inner_cols(attn_ref[...], grad_low_ref[...]), groups)
        back = inner_rows(grad_low_ref[...], held_ref[0]).astype(BF)
        left = side_ref[0] == 0
        middle_at = width // 2
        for at in range(0, middle_at, LANES):
            near, far = back[:, at : at + LANES], back[:, middle_at + at :][:, :LANES]
            grad_attn_ref[0, at // LANES] = jnp.where(left, near, far)
            grad_attn_ref[1, at // LANES] = jnp.where(left, far, near)


def middle(groups, side, attn, hidden, query, grad_hidden, grad_query, weights, inner_bias, small):
    rows, width = attn.shape
    tiles = inner_bias.shape[1] // width

    def whole(array):
        return pl.BlockSpec(array.shape, lambda step, side: (0,) * array.ndim)

    def square(at):
        return pl.BlockSpec((width, width), lambda step, side: (0, at(step)))

    def back(step):
        return lax.min(lax.div(lax.max(step - tiles, 0), 2), tiles - 1)

    def tile(step):
        return lax.select(step < tiles, step, back(step))

    def written(step):
        odd = lax.rem(lax.max(step - tiles, 0), 2)
        return lax.select(step == 3 * tiles, 0, 1 + back(step) + tiles * odd)

    outs = [
        jax.ShapeDtypeStruct((rows, width), BF),
        jax.ShapeDtypeStruct((rows, width), F32),
        jax.ShapeDtypeStruct((2, width // 2 // LANES, rows, LANES), BF),
        jax.ShapeDtypeStruct((width, (1 + 2 * tiles) * width), BF),
        jax.ShapeDtypeStruct((1, tiles * width), F32),
        jax.ShapeDtypeStruct((8, width), F32),
    ]
    return pl.pallas_call(
        functools.partial(middle_kernel, groups),
        grid_spec=pltpu.PrefetchScalarGridSpec(
            num_scalar_prefetch=1,
            grid=(1 + 3 * tiles,),
            in_specs=[whole(t) for t in (attn, hidden, query, grad_hidden, grad_query)]
            + [
                pl.BlockSpec(memory_space=pl.ANY),
                pl.BlockSpec((1, width), lambda step, side: (0, tile(step))),
                whole(small),
            ],
            out_specs=[whole(t) for t in outs[:3]]
            + [
                square(written),
                pl.BlockSpec((1, width), lambda step, side: (0, back(step))),
                whole(outs[5]),
            ],
            scratch_shapes=[
                pltpu.VMEM((rows, width), F32),
                pltpu.VMEM((rows, LANES), F32),
                pltpu.VMEM((rows, width), BF),
                pltpu.VMEM((width, rows), BF),
                pltpu.VMEM((rows, tiles * width), BF),
                pltpu.VMEM((rows, tiles * width), F32),
                pltpu.VMEM((rows, width), F32),
                pltpu.VMEM((rows, width), F32),
                pltpu.VMEM((rows, width), BF),
                pltpu.VMEM((rows, width), BF),
                pltpu.VMEM((1 + 2 * tiles, width, width), BF),
                pltpu.SemaphoreType.DMA((1 + 2 * tiles,)),
            ],
        ),
        out_shape=outs,
        compiler_params=pltpu.CompilerParams(
            dimension_semantics=("arbitrary",), vmem_limit_bytes=VMEM_LIMIT
        ),
        cost_estimate=pl.CostEstimate(
            flops=12 * rows * width * width * tiles,
            bytes_accessed=20 * width * width * tiles,
            transcendentals=rows * width * tiles,
        ),
    )(side, attn, hidden, query, grad_hidden, grad_query, weights, inner_bias, small)


def swap(values):
    return lax.ppermute(values, "seq", [(0, 1), (1, 0)])


def bit_orders(groups):
    high = list(range(groups.bit_length() - 2, 0, -1))
    return high, high[-1:] + high[:-1]


def across(values, groups, bit):
    return lax.ppermute(values, "fsdp", [(i, i ^ (1 << bit)) for i in range(groups)])


def merged(values, theirs, place, held, bit):
    axis = sum(1 for other in held if other > bit)
    return jnp.where(
        (place >> bit) & 1 == 0,
        jnp.stack([values, theirs], axis),
        jnp.stack([theirs, values], axis),
    )


def gather_beside(one, two, groups, chunks, beside):
    place = lax.axis_index("fsdp")
    order_one, order_two = bit_orders(groups)
    order_one, order_two = order_one + [0], order_two + [0]
    swapped, late = [], []
    for at, (bit_one, bit_two) in enumerate(zip(order_one, order_two)):
        left = len(order_one) - at
        take = chunks[: -(-len(chunks) // left)] if len(chunks) >= left else []
        chunks = chunks[len(take) :]
        theirs = [across(one, groups, bit_one), across(two, groups, bit_two)]
        theirs += [swap(chunk) for chunk in take]
        if at == 1:
            theirs, beside = lax.optimization_barrier((theirs, beside))
        else:
            theirs = lax.optimization_barrier(theirs)
        if at == len(order_one) - 2:
            late = theirs[:2]
        one = merged(one, theirs[0], place, order_one[:at], bit_one)
        two = merged(two, theirs[1], place, order_two[:at], bit_two)
        swapped += theirs[2:]
    bits = len(order_one)
    return (
        one.reshape((-1,) + one.shape[bits + 1 :]),
        two.reshape((-1,) + two.shape[bits + 1 :]),
        swapped,
        beside,
        late,
    )


def shuffle(count, lanes):
    take = jnp.arange(count * lanes)[:, None]
    give = jnp.arange(count * lanes)[None, :]
    return ((take % lanes) * count + take // lanes == give).astype(BF)


def pad_to(values, count):
    return jnp.pad(values, (0, count - values.shape[0]))


def shards(
    hidden,
    query_in,
    memory,
    segment_ids,
    block_order,
    memory_valid,
    w_query,
    w_key,
    w_value,
    w_out,
    w_rel,
    rel_biases,
    seg_embed,
    w_inner,
    b_inner,
    w_outer,
    b_outer,
    norm_gains,
    norm_biases,
    grad_hidden_out,
    grad_query_out,
):
    side = lax.axis_index("seq")
    groups = lax.axis_size("fsdp")
    place_at = lax.axis_index("fsdp")
    half, width = hidden.shape[1:]
    target_half = query_in.shape[1]
    memory_half = memory.shape[1]
    head_width = w_rel.shape[1]
    shard_rows = w_query.shape[0]
    ffn_width = w_inner.shape[1]
    own_rows = half + target_half

    def by_side(own, other, axis):
        return jnp.where(
            side == 0,
            jnp.concatenate([own, other], axis),
            jnp.concatenate([other, own], axis),
        )

    pairs = head_width // LANES
    pair_width = 3 * LANES

    def head_columns(weight, pair):
        return lax.dynamic_slice_in_dim(weight, side * head_width + pair * LANES, LANES, 1)

    def pair_columns(pair):
        return [head_columns(weight, pair) for weight in (w_query, w_key, w_value)]

    order = block_order[0]
    segs = segment_ids[0]
    target_seg = lax.dynamic_slice_in_dim(segs, MEM + order[NBLK - 1] * BLOCK, BLOCK)
    seg_rows = jnp.concatenate([segs[MEM:], target_seg, segs[:MEM]])
    invalid = jnp.concatenate([jnp.zeros((MROW,), jnp.int32), (memory_valid[0] != 1).astype(jnp.int32)])
    lane = jnp.arange(LANES)[None, :]
    marks = jnp.where(lane < 6, seg_rows[:, None] == lane % 3, (lane == 6) | (lane == 7))
    marks = jnp.where(lane == 8, invalid[:, None] == 1, marks).astype(BF)

    pos_table = sinusoid(REL_ROWS, width, MEM + L - 1).astype(BF)
    few = jnp.concatenate([rel_biases, seg_embed], 0)
    few = jnp.pad(few, ((0, shard_rows - 5), (0, LANES - few.shape[1])))
    quarter = half // 2
    weights_one, weights_two, swapped, (pos_table, marks), late = gather_beside(
        jnp.concatenate(sum([pair_columns(pair) for pair in range(pairs - 1)], []), 1),
        jnp.concatenate(pair_columns(pairs - 1) + [w_rel, few], 1),
        groups,
        [hidden[0, :quarter], hidden[0, quarter:], memory[0], query_in[0]],
        (pos_table, marks),
    )
    rel_weight = weights_two[:, pair_width : pair_width + head_width]
    few_all = weights_two[:, pair_width + head_width :].reshape(groups, shard_rows, LANES)
    few_all = few_all[:, :5, : head_width // groups].astype(F32)
    few_all = few_all.transpose(1, 0, 2).reshape(5, head_width)

    blocks = ffn_width // width
    spots = shuffle(blocks, LANES)
    smalls = (b_inner, b_outer, norm_gains, norm_biases)
    small_flat = pad_to(jnp.concatenate([t.reshape(-1) for t in smalls]), shard_rows * LANES)
    inner_moved = lax.dot_general(
        w_inner.reshape(shard_rows, -1, blocks * LANES),
        spots,
        (((2,), (1,)), ((), ())),
        preferred_element_type=F32,
    ).astype(BF)
    inner_moved = inner_moved.reshape(shard_rows, -1, blocks, LANES).transpose(0, 2, 1, 3)
    mixed = jnp.concatenate(
        [
            w_out,
            inner_moved.reshape(shard_rows, ffn_width),
            w_outer.reshape(shard_rows, ffn_width),
            small_flat.reshape(shard_rows, LANES),
        ],
        1,
    )
    mixed, _ = lax.optimization_barrier((mixed, late))
    mixed = lax.all_gather(mixed, "fsdp", axis=0, tiled=True)
    small_all = mixed[:, width + 2 * ffn_width :].reshape(groups, shard_rows * LANES).astype(F32)

    def unpack():
        found, at = [], 0
        for small in smalls:
            piece = small_all[:, at : at + small.size].reshape((groups,) + small.shape)
            found.append(jnp.moveaxis(piece, 0, -2).reshape(small.shape[:-1] + (-1,)))
            at += small.size
        return found

    inner_bias, outer_bias, gains, shifts = unpack()

    cuts = ((0, half), (half, own_rows))
    far_hidden = jnp.concatenate(swapped[:2], 0)
    stacked = jnp.concatenate(
        [
            by_side(hidden[0], far_hidden, 0),
            by_side(query_in[0], swapped[3], 0),
            by_side(memory[0], swapped[2], 0),
        ],
        0,
    )

    qkv_one = product(stacked, weights_one).astype(BF)
    qkv_two = product(stacked, weights_two[:, :pair_width]).astype(BF)
    rel = product(pos_table, rel_weight).astype(BF)
    par = jnp.concatenate([few_all, jnp.zeros((3, head_width), F32)], 0)
    def rows_of(values, which):
        return jnp.concatenate(
            [
                lax.dynamic_slice_in_dim(values, which * half, half, 0),
                lax.dynamic_slice_in_dim(values, L + which * target_half, target_half, 0),
            ],
            0,
        )

    def pair_args(pair):
        last = pair == pairs - 1
        at = (0, qkv_two) if last else (3 * pair, qkv_one)
        return (pair, at[0], order, at[1], rel, marks, par)

    kept = []
    own_att, far_att = [], []
    for pair in range(pairs):
        att, exps, inverse = attention_forward(*pair_args(pair))
        kept.append((att, inverse, exps))
        own_att.append(rows_of(att, side))
        far_att.append(swap(rows_of(att, 1 - side)))
    attn_rows = by_side(jnp.concatenate(own_att, 1), jnp.concatenate(far_att, 1), 1)
    small = jnp.stack([gains[0], shifts[0], gains[1], shifts[1], outer_bias] + [outer_bias] * 3)
    devices = 2 * groups
    out_rows = width // devices
    dealt_rows = out_rows % 8 == 0
    result, grad_sum_one, grad_attn, grad_weights, grad_b_inner, grad_small = middle(
        groups if dealt_rows else None,
        side.astype(jnp.int32)[None],
        attn_rows,
        hidden[0],
        query_in[0],
        grad_hidden_out[0],
        grad_query_out[0],
        mixed,
        inner_bias.reshape(width, blocks).T.reshape(1, ffn_width),
        small,
    )

    if dealt_rows:
        token_sums = lax.psum_scatter(grad_weights, "fsdp", scatter_dimension=0, tiled=True)
        token_sums = token_sums.reshape(2, out_rows, -1)
        near_sums = lax.dynamic_index_in_dim(token_sums, side, 0, True)
        far_sums = swap(lax.dynamic_index_in_dim(token_sums, 1 - side, 0, True))
        token_sums = jnp.concatenate([near_sums, far_sums], 0)
    else:
        token_sums = lax.psum_scatter(
            grad_weights, ("seq", "fsdp"), scatter_dimension=0, tiled=True
        )[None]
    grad_b_inner = grad_b_inner.reshape(blocks, width).T.reshape(devices, -1)
    row_count = width // devices
    token_flat = jnp.concatenate(
        [
            grad_b_inner.reshape(devices, -1),
            grad_small[:5].reshape(5, devices, -1).transpose(1, 0, 2).reshape(devices, -1),
        ],
        1,
    )
    inner_count = ffn_width // devices

    weights_two = weights_two[:, :pair_width]
    weights_one, weights_two, attn_rows = lax.optimization_barrier(
        (weights_one, weights_two, attn_rows)
    )
    far_one, far_two = swap(weights_one), swap(weights_two)

    far_grads = [swap(grad_attn[1, pair]) for pair in range(pairs)]

    core = place_at % 2
    same_core = [[at for at in range(groups) if at % 2 == which] for which in range(2)]

    def core_pieces(parts, which):
        parts = [part.reshape((groups // 2, 2) + part.shape[1:]) for part in parts]
        parts = [lax.dynamic_index_in_dim(part, which, 1, False) for part in parts]
        message = jnp.concatenate(parts[:2], 2)
        return jnp.concatenate([message] + parts[2:], 1) if parts[2:] else message

    def core_message(parts):
        far = across(core_pieces(parts, 1 - core), groups, 0)
        near = core_pieces(parts, core)
        return (near.astype(F32) + far.astype(F32)).astype(BF)

    def sum_message(message):
        message = lax.all_to_all(
            message,
            "fsdp",
            split_axis=0,
            concat_axis=0,
            tiled=True,
            axis_index_groups=same_core,
        )
        return jnp.sum(message.astype(F32), 0)

    own_rows_grads, far_rows_grads, sums, few_grads = [], [], [], []
    for pair in range(pairs):
        own, far = grad_attn[0, pair], far_grads[pair]
        if pair:
            own, message, sums = lax.optimization_barrier((own, message, sums))
            sums.append(sum_message(message))
        head_grad = jnp.concatenate([by_side(own[a:b], far[a:b], 0) for a, b in cuts], 0)
        dqkv, drel, dpar = attention_backward(*pair_args(pair), head_grad, *kept[pair])
        if pair:
            dqkv, drel, sums = lax.optimization_barrier((dqkv, drel, sums))
        few_grads.append(dpar[:5])
        own_rows_grads.append(rows_of(dqkv, side))
        far_rows_grads.append(swap(rows_of(dqkv, 1 - side)))
        grad_pair = inner_cols(stacked, dqkv).astype(BF)
        grad_pair = grad_pair.reshape(2, groups, out_rows, pair_width).transpose(1, 0, 2, 3)
        parts = [
            grad_pair.reshape(groups, shard_rows, pair_width),
            inner_cols(pos_table, drel).astype(BF).reshape(groups, shard_rows, LANES),
        ]
        if pair == 0:
            token_flat = token_flat.reshape(2, groups, -1).transpose(1, 0, 2).astype(BF)
            extra = ((0, 0), (0, 6), (0, pair_width + LANES - token_flat.shape[2]))
            parts.append(jnp.pad(token_flat, extra))
        if pair == pairs - 1:
            few = jnp.concatenate(few_grads, 1).reshape(5, groups, head_width // groups)
            few = few.transpose(1, 0, 2).reshape(groups, 1, -1).astype(BF)
            few = jnp.pad(few, ((0, 0), (0, 7), (0, pair_width + LANES - few.shape[2])))
            parts.append(few)
        message = core_message(parts)
    sums.append(sum_message(message))
    sums, token_sums = lax.optimization_barrier((sums, token_sums))
    shares = token_sums.shape[0]
    plain = jnp.sum(token_sums.astype(F32), 0)
    out_out = plain[:, :width]
    out_outer = plain[:, width + ffn_width :].reshape(blocks * out_rows, width)
    inner_sums = token_sums[:, :, width : width + ffn_width]
    inner_sums = inner_sums.reshape(shares, out_rows, blocks, -1, LANES).transpose(1, 3, 0, 2, 4)
    out_inner = product(
        inner_sums.reshape(out_rows, -1, shares * blocks * LANES),
        jnp.concatenate([spots] * shares, 0),
    ).reshape(out_rows, ffn_width)

    early = slice(0, pairs - 1)
    grad_own = grad_sum_one + inner_rows(
        jnp.concatenate(own_rows_grads + far_rows_grads[early], 1),
        jnp.concatenate([weights_one, weights_two, far_one], 1),
    )
    grad_own = grad_own + inner_rows(far_rows_grads[-1], far_two)

    both_sums = jnp.concatenate([t[:shard_rows, :pair_width] for t in sums], 1)
    own_sum = lax.dynamic_slice_in_dim(both_sums, side * out_rows, out_rows, 0)
    far_sum = lax.dynamic_slice_in_dim(both_sums, (1 - side) * out_rows, out_rows, 0)
    far_sum = swap(far_sum.astype(BF)).astype(F32)
    small_sums = lax.dynamic_index_in_dim(sums[0], shard_rows + side, 0, False)
    small_sums += swap(
        lax.dynamic_index_in_dim(sums[0], shard_rows + 1 - side, 0, False).astype(BF)
    ).astype(F32)
    out_b_inner = small_sums[:inner_count]
    out_rest = small_sums[inner_count : inner_count + 5 * row_count].reshape(5, row_count)
    out_gains, out_shifts, out_b_outer = out_rest[0:4:2], out_rest[1:4:2], out_rest[4]

    def weight_rows(values, which):
        return [
            values[:, pair * pair_width + which * LANES :][:, :LANES] for pair in range(pairs)
        ]

    out_query, out_key, out_value = (
        by_side(
            jnp.concatenate(weight_rows(own_sum, which), 1),
            jnp.concatenate(weight_rows(far_sum, which), 1),
            1,
        )
        for which in range(3)
    )
    out_rel = jnp.concatenate([t[:shard_rows, pair_width:] for t in sums], 1)
    few_sum = sums[-1][shard_rows, : 5 * (head_width // groups)].reshape(5, -1)
    out_biases, out_seg = few_sum[:3], few_sum[3:]
    return (
        result[None, :half],
        result[None, half:],
        grad_own[None, :half],
        grad_own[None, half:],
        out_query,
        out_key,
        out_value,
        out_out,
        out_rel,
        out_biases,
        out_seg,
        out_inner,
        out_b_inner,
        out_outer,
        out_b_outer,
        out_gains,
        out_shifts,
    )


def solution(mesh):
    rows = P("fsdp", "seq", None)
    both = ("seq", "fsdp")
    in_specs = (
        (rows,) * 3
        + (P("fsdp", None),) * 7
        + (P("fsdp", "seq"), P(None, both), P(None, both))
        + (P("fsdp", None), P("fsdp"), P("fsdp", None), P("fsdp"))
        + (P(None, "fsdp"), P(None, "fsdp"))
        + (rows,) * 2
    )
    out_specs = (
        (rows,) * 4
        + (P(both, None),) * 4
        + (P("fsdp", "seq"), P(None, both), P(None, both))
        + (P(both, None), P(both), P(both, None), P(both))
        + (P(None, both), P(None, both))
    )
    return jax.shard_map(shards, mesh=mesh, in_specs=in_specs, out_specs=out_specs, check_vma=False)
```

```python
import functools

import jax
import jax.numpy as jnp
from jax import lax
from jax.experimental import pallas as pl
from jax.experimental.pallas import tpu as pltpu
from jax.sharding import PartitionSpec as P

DH = 64
BLOCK = 256
NBLK = 4
MEM = 384
L = 1024
LANES = 128

QROW = L
MROW = L + BLOCK
ROWS = L + BLOCK + MEM
KEYS = MEM + L
SPAN_M = MEM + BLOCK
SPAN_T = 2 * BLOCK
REL_M = L - BLOCK
REL_T = MEM + L - BLOCK
REL_ROWS = MEM + 2 * L
SPANS = SPAN_M + NBLK * SPAN_T

EPSILON = 1e-05
NEGATIVE = -1e30
SCORE_SCALE = 0.125
EXP2_SCALE = SCORE_SCALE * 1.4426950408889634
STEPS = NBLK + 1
VMEM_LIMIT = 60 * 1024 * 1024
BF = jnp.bfloat16
F32 = jnp.float32


def product(left, right):
    return jnp.dot(left, right, preferred_element_type=F32)


def inner_rows(left, right):
    return lax.dot_general(left, right, (((1,), (1,)), ((), ())), preferred_element_type=F32)


def inner_cols(left, right):
    return lax.dot_general(left, right, (((0,), (0,)), ((), ())), preferred_element_type=F32)


def sinusoid(row_count, width_all, farthest):
    fine = DH
    frequency = 10000.0 ** (-jnp.arange(0, width_all, 2).astype(F32) / width_all)
    starts = (farthest - fine * jnp.arange(row_count // fine)).astype(F32)
    far = starts[:, None, None] * frequency
    near = jnp.arange(fine).astype(F32)[None, :, None] * frequency
    sines = jnp.sin(far) * jnp.cos(near) - jnp.cos(far) * jnp.sin(near)
    cosines = jnp.cos(far) * jnp.cos(near) + jnp.sin(far) * jnp.sin(near)
    return jnp.concatenate([sines, cosines], 2).reshape(row_count, width_all)


def split_low(values):
    high = values.astype(BF).astype(F32)
    return high, values - high


def place(step, order_ref):
    last = jnp.minimum(step, NBLK - 1)
    block = order_ref[last]
    row = jnp.where(step < NBLK, block, NBLK) * BLOCK
    return block, pl.multiple_of(row, BLOCK), last


def row_terms(q_ref, kx_ref, par_ref, row):
    query = q_ref[pl.ds(row, BLOCK), :].astype(F32)
    marks = kx_ref[pl.ds(row, BLOCK), :].astype(F32)
    return query + par_ref[0:1, :], query + par_ref[1:2, :], query + par_ref[2:3, :], marks


def gather_keys(order_ref, from_ref, to_ref, lanes):
    to_ref[:MEM, lanes] = from_ref[MROW:, :]
    for at in range(NBLK):
        rows = pl.ds(pl.multiple_of(BLOCK * order_ref[at], BLOCK), BLOCK)
        to_ref[MEM + BLOCK * at : MEM + BLOCK * (at + 1), lanes] = from_ref[rows, :]


def key_spots(order_ref, block, count):
    spots = [(0, MEM, pl.multiple_of(REL_M - BLOCK * block, BLOCK), 0)]
    for at in range(count):
        rel_row = pl.multiple_of(REL_T + BLOCK * (order_ref[at] - block), LANES)
        spots.append((MEM + BLOCK * at, BLOCK, rel_row, SPAN_M + SPAN_T * at))
    return spots


def gather_spans(spots, rel_ref, span_ref):
    for _, key_count, rel_row, put in spots:
        span = key_count + BLOCK
        span_ref[put : put + span, :] = rel_ref[pl.ds(rel_row, span), :]


def forward_kernel(
    order_ref,
    q_ref,
    k_ref,
    v_ref,
    rel_ref,
    kx_ref,
    par_ref,
    att_ref,
    exp_ref,
    inv_ref,
    kcat_ref,
    vcat_ref,
    score_ref,
    lhs_ref,
    qr_ref,
    span_ref,
    sum_ref,
):
    step = pl.program_id(0)

    @pl.when(step == 0)
    def _():
        gather_keys(order_ref, k_ref, kcat_ref, slice(0, LANES))
        gather_keys(order_ref, kx_ref, kcat_ref, slice(LANES, 2 * LANES))
        gather_keys(order_ref, v_ref, vcat_ref, slice(0, LANES))
        vcat_ref[:, LANES:] = jnp.ones((KEYS, LANES), BF)

    block, row, last = place(step, order_ref)
    lane = lax.broadcasted_iota(jnp.int32, (BLOCK, LANES), 1)
    query_w, query_r, query_s, marks = row_terms(q_ref, kx_ref, par_ref, row)
    same, other = query_s * par_ref[3:4, :], query_s * par_ref[4:5, :]
    for head in range(2):
        mine = (lane < DH) == (head == 0)
        other_sum = jnp.sum(jnp.where(mine, other, 0.0), -1, keepdims=True)
        diff = jnp.sum(jnp.where(mine, same, 0.0), -1, keepdims=True) - other_sum
        diff_high, diff_low = split_low(diff)
        other_high, other_low = split_low(other_sum)
        extra = jnp.where(lane < 3, marks * diff_high, jnp.where(lane < 6, marks * diff_low, 0.0))
        extra = jnp.where(lane == 6, other_high, jnp.where(lane == 7, other_low, extra))
        extra = jnp.where(lane == 8, NEGATIVE, extra)
        lhs_ref[head, :, :LANES] = jnp.where(mine, query_w, 0.0).astype(BF)
        lhs_ref[head, :, LANES:] = extra.astype(BF)
        qr_ref[head] = jnp.where(mine, query_r, 0.0).astype(BF)

    across = lax.broadcasted_iota(jnp.int32, (BLOCK, BLOCK), 0) - lax.broadcasted_iota(
        jnp.int32, (BLOCK, BLOCK), 1
    )
    hidden_at = jnp.where(step < NBLK, BLOCK, 0)

    for count in range(NBLK):

        @pl.when(last == count)
        def _():
            spots = key_spots(order_ref, block, count + 1)
            keys = MEM + BLOCK * (count + 1)
            spans = SPAN_M + SPAN_T * (count + 1)
            gather_spans(spots, rel_ref, span_ref)
            for head in range(2):
                content = inner_rows(lhs_ref[head], kcat_ref[:keys, :])
                position = inner_rows(qr_ref[head], span_ref[:spans, :])
                top = None
                for at, key_count, _, put in spots:
                    span = key_count + BLOCK
                    moved = position[:, put : put + span]
                    moved = pltpu.roll(moved, span - BLOCK + 1, 1, stride=1, stride_axis=0)
                    tile = content[:, at : at + key_count] + moved[:, :key_count]
                    if at + key_count == keys:
                        tile = jnp.where(across == hidden_at, NEGATIVE, tile)
                    score_ref[head, :, at : at + key_count] = tile
                    for piece in range(0, key_count, LANES):
                        part = tile[:, piece : piece + LANES]
                        top = part if top is None else jnp.maximum(top, part)
                peak = jnp.max(top, -1, keepdims=True)
                low = jnp.exp2((score_ref[head, :, :keys] - peak) * EXP2_SCALE).astype(BF)
                exp_ref[head, :, :keys] = low
                sum_ref[head] = product(low, vcat_ref[:keys, :])

    sums = sum_ref[0], sum_ref[1]
    first = lane < DH
    inverse = 1.0 / jnp.where(first, sums[0][:, LANES:], sums[1][:, LANES:])
    total = jnp.where(first, sums[0][:, :LANES], sums[1][:, :LANES])
    att_ref[pl.ds(row, BLOCK), :] = (total * inverse).astype(BF)
    inv_ref[pl.ds(row, BLOCK), :] = inverse


def backward_kernel(
    order_ref,
    q_ref,
    k_ref,
    v_ref,
    rel_ref,
    kx_ref,
    par_ref,
    near_ref,
    far_ref,
    att_ref,
    inv_ref,
    exp_ref,
    dqkv_ref,
    drel_ref,
    dpar_ref,
    kcat_ref,
    vcat_ref,
    flip_ref,
    lhs_ref,
    qwt_ref,
    qrt_ref,
    gt_ref,
    dkt_ref,
    dvt_ref,
    drelt_ref,
    accw_ref,
    accr_ref,
    span_ref,
    moved_ref,
    grad_ref,
):
    step = pl.program_id(0)

    @pl.when(step == 0)
    def _():
        gather_keys(order_ref, k_ref, kcat_ref, slice(0, LANES))
        gather_keys(order_ref, kx_ref, kcat_ref, slice(LANES, 2 * LANES))
        gather_keys(order_ref, v_ref, vcat_ref, slice(0, LANES))
        vcat_ref[:, :LANES] = (vcat_ref[:, :LANES].astype(F32) * SCORE_SCALE).astype(BF)
        vcat_ref[:, LANES:] = jnp.full((KEYS, LANES), SCORE_SCALE, BF)
        half, part = L // 2, BLOCK // 2
        for from_ref, which in ((near_ref, order_ref[NBLK]), (far_ref, 1 - order_ref[NBLK])):
            rows_at = pl.multiple_of(which * half, half)
            grad_ref[pl.ds(rows_at, half), :] = from_ref[:half, :]
            rows_at = pl.multiple_of(QROW + which * part, part)
            grad_ref[pl.ds(rows_at, part), :] = from_ref[half:, :]
        up = lax.broadcasted_iota(jnp.int32, (BLOCK, BLOCK), 0)
        down = lax.broadcasted_iota(jnp.int32, (BLOCK, BLOCK), 1)
        flip_ref[...] = jnp.where(up + down == BLOCK - 1, 1.0, 0.0).astype(BF)
        dkt_ref[...] = jnp.zeros_like(dkt_ref)
        dvt_ref[...] = jnp.zeros_like(dvt_ref)
        drelt_ref[...] = jnp.zeros_like(drelt_ref)
        dpar_ref[...] = jnp.zeros_like(dpar_ref)

    block, row, last = place(step, order_ref)
    lane = lax.broadcasted_iota(jnp.int32, (BLOCK, LANES), 1)
    first = lane < DH
    flip = flip_ref[...]
    rows = pl.ds(row, BLOCK)
    grad_low = (grad_ref[rows, :].astype(F32) * inv_ref[rows, :]).astype(BF)
    query, marks = product(flip, q_ref[rows, :]), product(flip, kx_ref[rows, :])
    grad, att = product(flip, grad_low), product(flip, att_ref[rows, :])
    query_w = query + par_ref[0:1, :]
    query_r = query + par_ref[1:2, :]
    query_s = query + par_ref[2:3, :]
    dots = grad * att
    for head in range(2):
        mine = first == (head == 0)
        high, low = split_low(-jnp.sum(jnp.where(mine, dots, 0.0), -1, keepdims=True))
        extra = jnp.where(lane == 0, high, jnp.where(lane == 1, low, 0.0))
        lhs_ref[head, :, :LANES] = jnp.where(mine, grad, 0.0).astype(BF)
        lhs_ref[head, :, LANES:] = extra.astype(BF)
    qwt_ref[...] = query_w.astype(BF).astype(F32).T.astype(BF)
    qrt_ref[...] = query_r.astype(BF).astype(F32).T.astype(BF)
    gt_ref[...] = grad_low.astype(F32).T.astype(BF)

    for count in range(NBLK):

        @pl.when(last == count)
        def _():
            spots = key_spots(order_ref, block, count + 1)
            keys = MEM + BLOCK * (count + 1)
            spans = SPAN_M + SPAN_T * (count + 1)
            gather_spans(spots, rel_ref, span_ref)
            for head in range(2):
                own = slice(DH * head, DH * head + DH)
                probs = exp_ref[head, :, :keys]
                slope = inner_rows(lhs_ref[head], vcat_ref[:keys, :])
                scaled = (product(flip, probs) * slope).astype(BF)
                for at, key_count, _, put in spots:
                    span = key_count + BLOCK
                    moved = jnp.concatenate(
                        [scaled[:, at : at + key_count], jnp.zeros((BLOCK, BLOCK), BF)], 1
                    )
                    moved_ref[head, :, put : put + span] = pltpu.roll(
                        moved, 0, 1, stride=1, stride_axis=0
                    )
                dkt_ref[own, :keys] += product(qwt_ref[own, :], scaled)
                dvt_ref[own, :keys] += product(gt_ref[own, :], probs)
                accw_ref[head] = product(scaled, kcat_ref[:keys, :])
                accr_ref[head] = product(moved_ref[head, :, :spans], span_ref[:spans, :])
                drel = product(qrt_ref[own, :], moved_ref[head, :, :spans])
                for _, key_count, rel_row, put in spots:
                    span = key_count + BLOCK
                    drelt_ref[own, pl.ds(rel_row, span)] += drel[:, put : put + span]

    grad_w = jnp.where(first, accw_ref[0, :, :LANES], accw_ref[1, :, :LANES])
    grad_r = jnp.where(first, accr_ref[0], accr_ref[1])
    same_sums, other_sums = [], []
    for head in range(2):
        sums = accw_ref[head, :, LANES:]
        same_sums.append(jnp.sum(jnp.where(lane < 3, marks * sums, 0.0), -1, keepdims=True))
        total = jnp.sum(jnp.where(lane == 6, sums, 0.0), -1, keepdims=True)
        other_sums.append(total - same_sums[head])
    same = jnp.where(first, same_sums[0], same_sums[1])
    other = jnp.where(first, other_sums[0], other_sums[1])
    grad_s = same * par_ref[3:4, :] + other * par_ref[4:5, :]
    high, low = split_low(grad_w + grad_r + grad_s)
    dqkv_ref[rows, :LANES] = (
        product(flip, high.astype(BF)) + product(flip, low.astype(BF))
    ).astype(BF)
    for at, terms in enumerate((grad_w, grad_r, grad_s, same * query_s, other * query_s)):
        dpar_ref[at : at + 1, :] += jnp.sum(terms, 0, keepdims=True)

    @pl.when(step == STEPS - 1)
    def _():
        dqkv_ref[MROW:, :LANES] = jnp.zeros((MEM, LANES), BF)
        dqkv_ref[L:MROW, LANES:] = jnp.zeros((BLOCK, 2 * LANES), BF)
        for lanes, from_ref in ((1, dkt_ref), (2, dvt_ref)):
            lanes = slice(lanes * LANES, (lanes + 1) * LANES)
            dqkv_ref[MROW:, lanes] = from_ref[:, :MEM].T.astype(BF)
            for at in range(NBLK):
                rows_at = pl.ds(pl.multiple_of(BLOCK * order_ref[at], BLOCK), BLOCK)
                start = MEM + BLOCK * at
                dqkv_ref[rows_at, lanes] = from_ref[:, start : start + BLOCK].T.astype(BF)
        drel_ref[...] = drelt_ref[...].T.astype(BF)


def column(rows, at):
    return pl.BlockSpec((rows, LANES), lambda step, order: (0, at))


def attention_specs(pair, first):
    ins = [column(ROWS, first + at) for at in range(3)]
    ins += [column(REL_ROWS, pair), column(ROWS, 0), column(8, pair)]
    exps = pl.BlockSpec((None, 2, BLOCK, KEYS), lambda step, order: (step, 0, 0, 0))
    return ins, exps


def settings(passes):
    return dict(
        compiler_params=pltpu.CompilerParams(
            dimension_semantics=("arbitrary",), vmem_limit_bytes=40 * 1024 * 1024
        ),
        cost_estimate=pl.CostEstimate(
            flops=passes * 4 * MROW * KEYS * BLOCK,
            bytes_accessed=STEPS * 2 * BLOCK * KEYS * 2,
            transcendentals=2 * MROW * KEYS,
        ),
    )


def attention_forward(pair, first, order, qkv, rel, marks, par):
    ins, exps = attention_specs(pair, first)
    return pl.pallas_call(
        forward_kernel,
        grid_spec=pltpu.PrefetchScalarGridSpec(
            num_scalar_prefetch=1,
            grid=(STEPS,),
            in_specs=ins,
            out_specs=[column(MROW, 0), exps, column(MROW, 0)],
            scratch_shapes=[
                pltpu.VMEM((KEYS, 2 * LANES), BF),
                pltpu.VMEM((KEYS, 2 * LANES), BF),
                pltpu.VMEM((2, BLOCK, KEYS), F32),
                pltpu.VMEM((2, BLOCK, 2 * LANES), BF),
                pltpu.VMEM((2, BLOCK, LANES), BF),
                pltpu.VMEM((SPANS, LANES), BF),
                pltpu.VMEM((2, BLOCK, 2 * LANES), F32),
            ],
        ),
        out_shape=[
            jax.ShapeDtypeStruct((MROW, LANES), BF),
            pltpu.HBM((STEPS, 2, BLOCK, KEYS), BF),
            jax.ShapeDtypeStruct((MROW, LANES), F32),
        ],
        **settings(16),
    )(order, qkv, qkv, qkv, rel, marks, par)


def attention_backward(pair, first, order, qkv, rel, marks, par, side, near, far, att, inverse, exps_in):
    ins, exps = attention_specs(pair, first)
    order = jnp.concatenate([order, side.astype(order.dtype)[None]])
    qkv, rel, exps_in = (
        pltpu.with_memory_space_constraint(t, pltpu.HBM) for t in (qkv, rel, exps_in)
    )
    return pl.pallas_call(
        backward_kernel,
        grid_spec=pltpu.PrefetchScalarGridSpec(
            num_scalar_prefetch=1,
            grid=(STEPS,),
            in_specs=ins
            + [column(near.shape[0], 0)] * 2
            + [column(MROW, 0)] * 2
            + [exps],
            out_specs=[
                pl.BlockSpec((ROWS, 3 * LANES), lambda step, order: (0, 0)),
                column(REL_ROWS, 0),
                column(8, 0),
            ],
            scratch_shapes=[
                pltpu.VMEM((KEYS, 2 * LANES), BF),
                pltpu.VMEM((KEYS, 2 * LANES), BF),
                pltpu.VMEM((BLOCK, BLOCK), BF),
                pltpu.VMEM((2, BLOCK, 2 * LANES), BF),
                pltpu.VMEM((LANES, BLOCK), BF),
                pltpu.VMEM((LANES, BLOCK), BF),
                pltpu.VMEM((LANES, BLOCK), BF),
                pltpu.VMEM((LANES, KEYS), F32),
                pltpu.VMEM((LANES, KEYS), F32),
                pltpu.VMEM((LANES, REL_ROWS), F32),
                pltpu.VMEM((2, BLOCK, 2 * LANES), F32),
                pltpu.VMEM((2, BLOCK, LANES), F32),
                pltpu.VMEM((SPANS, LANES), BF),
                pltpu.VMEM((2, BLOCK, SPANS), BF),
                pltpu.VMEM((MROW, LANES), BF),
            ],
        ),
        out_shape=[
            jax.ShapeDtypeStruct((ROWS, 3 * LANES), BF),
            jax.ShapeDtypeStruct((REL_ROWS, LANES), BF),
            jax.ShapeDtypeStruct((8, LANES), F32),
        ],
        **settings(24),
    )(order, qkv, qkv, qkv, rel, marks, par, near, far, att, inverse, exps_in)


CHUNKS = 2


def norm_parts(values):
    center = values - jnp.mean(values, -1, keepdims=True)
    spread = jnp.mean(center * center, -1, keepdims=True)
    scale = lax.rsqrt(spread + EPSILON)
    return center * scale, scale


def norm_pull(grad, unit, scale, gain):
    grad = grad * gain
    mean = jnp.mean(grad, -1, keepdims=True)
    slope = jnp.mean(grad * unit, -1, keepdims=True)
    return (grad - mean - unit * slope) * scale


def dealt(values, groups):
    if groups is None:
        return values.astype(BF)
    share = values.shape[0] // (2 * groups)
    pieces = [
        values[(side * groups + at) * share :][:share] for at in range(groups) for side in range(2)
    ]
    return jnp.concatenate(pieces, 0).astype(BF)


def middle_kernel(
    groups,
    side_ref,
    attn_ref,
    hidden_ref,
    query_ref,
    grad_hidden_ref,
    grad_query_ref,
    weights_ref,
    inner_bias_ref,
    small_ref,
    result_ref,
    grad_sum_ref,
    gw_ref,
    gb_inner_ref,
    g_small_ref,
    *rest,
):
    pairs = attn_ref.shape[1] // (2 * LANES)
    near_refs, far_refs, rest = rest[:pairs], rest[pairs : 2 * pairs], rest[2 * pairs :]
    middle_steps(
        groups,
        side_ref,
        attn_ref,
        hidden_ref,
        query_ref,
        grad_hidden_ref,
        grad_query_ref,
        weights_ref,
        inner_bias_ref,
        small_ref,
        result_ref,
        grad_sum_ref,
        gw_ref,
        gb_inner_ref,
        g_small_ref,
        near_refs,
        far_refs,
        *rest,
    )


def middle_steps(
    groups,
    side_ref,
    attn_ref,
    hidden_ref,
    query_ref,
    grad_hidden_ref,
    grad_query_ref,
    weights_ref,
    inner_bias_ref,
    small_ref,
    result_ref,
    grad_sum_ref,
    gw_ref,
    gb_inner_ref,
    g_small_ref,
    near_refs,
    far_refs,
    unit_ref,
    scale_ref,
    low_ref,
    low_t_ref,
    act_ref,
    slope_ref,
    sum_ref,
    grad_ref,
    grad_low_ref,
    back_ref,
    held_ref,
    arrived,
):
    step = pl.program_id(0)
    rows, width = attn_ref.shape
    tiles = act_ref.shape[1] // width
    half = hidden_ref.shape[0]
    cut = rows // CHUNKS
    gain_one, shift_one = small_ref[0:1, :], small_ref[1:2, :]
    gain_two, shift_two = small_ref[2:3, :], small_ref[3:4, :]
    parts = [slice(at * cut, at * cut + cut) for at in range(CHUNKS)]

    def fetch(at):
        columns = pl.ds(pl.multiple_of(at * width, width), width)
        return pltpu.make_async_copy(weights_ref.at[:, columns], held_ref.at[at], arrived.at[at])

    @pl.when(step == 0)
    def _():
        fetch(0).start()
        for at in range(tiles):
            fetch(1 + at).start()
            fetch(1 + tiles + at).start()
        fetch(0).wait()
        sum_ref[...] = product(attn_ref[...], held_ref[0])
        sum_ref[:half, :] += hidden_ref[...].astype(F32)
        sum_ref[half:, :] += query_ref[...].astype(F32)
        for part in parts:
            unit, scale = norm_parts(sum_ref[part, :])
            unit_ref[part, :] = unit
            scale_ref[part, :] = jnp.broadcast_to(scale, (cut, LANES))
            first = unit * gain_one + shift_one
            low_ref[part, :] = first.astype(BF)
            sum_ref[part, :] = first + small_ref[4:5, :]

    place_of = jnp.where(step < tiles, step, jnp.minimum(lax.div(step - tiles, 2), tiles - 1))
    columns = pl.ds(pl.multiple_of(place_of * width, width), width)

    w_inner, w_outer = held_ref.at[1 + place_of], held_ref.at[1 + tiles + place_of]

    @pl.when(step < tiles)
    def _():
        fetch(1 + step).wait()
        fetch(1 + tiles + step).wait()
        for part in parts:
            pre = product(low_ref[part, :], w_inner[...]) + inner_bias_ref[...]
            square = pre * pre
            bend = jnp.tanh(0.7978845608028654 * (pre + 0.044715 * square * pre))
            half_bend = 0.5 + 0.5 * bend
            wide = pre * half_bend
            act = wide.astype(BF)
            act_ref[part, columns] = act
            turn = 1.5957691216057308 + 0.2140644488 * square
            slope_ref[part, columns] = half_bend + wide * (1.0 - half_bend) * turn
            sum_ref[part, :] += product(act, w_outer[...])

    @pl.when(step == tiles - 1)
    def _():
        g_gain = g_shift = g_outer = 0.0
        grad_ref[:half, :] = grad_hidden_ref[...].astype(F32)
        grad_ref[half:, :] = grad_query_ref[...].astype(F32)
        for part in parts:
            unit, scale = norm_parts(sum_ref[part, :])
            result_ref[part, :] = (unit * gain_two + shift_two).astype(BF)
            grad = grad_ref[part, :]
            g_gain += jnp.sum(grad * unit, 0, keepdims=True)
            g_shift += jnp.sum(grad, 0, keepdims=True)
            grad = norm_pull(grad, unit, scale, gain_two)
            low = grad.astype(BF)
            grad_ref[part, :] = grad
            grad_low_ref[part, :] = low
            g_outer += jnp.sum(low.astype(F32), 0, keepdims=True)
        g_small_ref[...] = jnp.zeros_like(g_small_ref)
        g_small_ref[2:3, :] = g_gain
        g_small_ref[3:4, :] = g_shift
        g_small_ref[4:5, :] = g_outer
        low_t_ref[...] = low_ref[...].T

    turn_back = jnp.logical_and(step >= tiles, step < 3 * tiles)

    @pl.when(jnp.logical_and(turn_back, lax.rem(step - tiles, 2) == 0))
    def _():
        g_inner = 0.0
        for part in parts:
            back = inner_rows(grad_low_ref[part, :], w_outer[...])
            low = (back * slope_ref[part, columns]).astype(BF)
            back_ref[part, :] = low
            g_inner += jnp.sum(low.astype(F32), 0, keepdims=True)
            grad_ref[part, :] += inner_rows(low, w_inner[...])
        gb_inner_ref[...] = g_inner
        gw_ref[...] = dealt(product(low_t_ref[...], back_ref[...]), groups)

    @pl.when(jnp.logical_and(turn_back, lax.rem(step - tiles, 2) == 1))
    def _():
        gw_ref[...] = dealt(inner_cols(act_ref[:, columns], grad_low_ref[...]), groups)

    @pl.when(step == 3 * tiles)
    def _():
        g_gain = g_shift = 0.0
        for part in parts:
            unit, scale = unit_ref[part, :], scale_ref[part, 0:1]
            grad = grad_ref[part, :]
            g_gain += jnp.sum(grad * unit, 0, keepdims=True)
            g_shift += jnp.sum(grad, 0, keepdims=True)
            grad = norm_pull(grad, unit, scale, gain_one)
            grad_sum_ref[part, :] = grad
            grad_low_ref[part, :] = grad.astype(BF)
        g_small_ref[0:1, :] = g_gain
        g_small_ref[1:2, :] = g_shift
        gw_ref[...] = dealt(inner_cols(attn_ref[...], grad_low_ref[...]), groups)
        back = inner_rows(grad_low_ref[...], held_ref[0]).astype(BF)
        left = side_ref[0] == 0
        middle_at = width // 2
        for at in range(0, middle_at, LANES):
            near, far = back[:, at : at + LANES], back[:, middle_at + at :][:, :LANES]
            near_refs[at // LANES][...] = jnp.where(left, near, far)
            far_refs[at // LANES][...] = jnp.where(left, far, near)


def middle(groups, side, attn, hidden, query, grad_hidden, grad_query, weights, inner_bias, small):
    rows, width = attn.shape
    tiles = inner_bias.shape[1] // width

    def whole(array):
        return pl.BlockSpec(array.shape, lambda step, side: (0,) * array.ndim)

    def square(at):
        return pl.BlockSpec((width, width), lambda step, side: (0, at(step)))

    def back(step):
        return lax.min(lax.div(lax.max(step - tiles, 0), 2), tiles - 1)

    def tile(step):
        return lax.select(step < tiles, step, back(step))

    def written(step):
        odd = lax.rem(lax.max(step - tiles, 0), 2)
        return lax.select(step == 3 * tiles, 0, 1 + back(step) + tiles * odd)

    outs = [
        jax.ShapeDtypeStruct((rows, width), BF),
        jax.ShapeDtypeStruct((rows, width), F32),
        jax.ShapeDtypeStruct((width, (1 + 2 * tiles) * width), BF),
        jax.ShapeDtypeStruct((1, tiles * width), F32),
        jax.ShapeDtypeStruct((8, width), F32),
    ] + [jax.ShapeDtypeStruct((rows, LANES), BF)] * (width // LANES)
    return pl.pallas_call(
        functools.partial(middle_kernel, groups),
        grid_spec=pltpu.PrefetchScalarGridSpec(
            num_scalar_prefetch=1,
            grid=(1 + 3 * tiles,),
            in_specs=[whole(t) for t in (attn, hidden, query, grad_hidden, grad_query)]
            + [
                pl.BlockSpec(memory_space=pl.ANY),
                pl.BlockSpec((1, width), lambda step, side: (0, tile(step))),
                whole(small),
            ],
            out_specs=[whole(t) for t in outs[:2]]
            + [
                square(written),
                pl.BlockSpec((1, width), lambda step, side: (0, back(step))),
                whole(outs[4]),
            ]
            + [whole(t) for t in outs[5:]],
            scratch_shapes=[
                pltpu.VMEM((rows, width), F32),
                pltpu.VMEM((rows, LANES), F32),
                pltpu.VMEM((rows, width), BF),
                pltpu.VMEM((width, rows), BF),
                pltpu.VMEM((rows, tiles * width), BF),
                pltpu.VMEM((rows, tiles * width), F32),
                pltpu.VMEM((rows, width), F32),
                pltpu.VMEM((rows, width), F32),
                pltpu.VMEM((rows, width), BF),
                pltpu.VMEM((rows, width), BF),
                pltpu.VMEM((1 + 2 * tiles, width, width), BF),
                pltpu.SemaphoreType.DMA((1 + 2 * tiles,)),
            ],
        ),
        out_shape=outs,
        compiler_params=pltpu.CompilerParams(
            dimension_semantics=("arbitrary",), vmem_limit_bytes=VMEM_LIMIT
        ),
        cost_estimate=pl.CostEstimate(
            flops=12 * rows * width * width * tiles,
            bytes_accessed=20 * width * width * tiles,
            transcendentals=rows * width * tiles,
        ),
    )(side, attn, hidden, query, grad_hidden, grad_query, weights, inner_bias, small)


def swap(values):
    return lax.ppermute(values, "seq", [(0, 1), (1, 0)])


def bit_orders(groups):
    high = list(range(groups.bit_length() - 2, 0, -1))
    return high, high[-1:] + high[:-1]


def across(values, groups, bit):
    return lax.ppermute(values, "fsdp", [(i, i ^ (1 << bit)) for i in range(groups)])


def merged(values, theirs, place, held, bit):
    axis = sum(1 for other in held if other > bit)
    return jnp.where(
        (place >> bit) & 1 == 0,
        jnp.stack([values, theirs], axis),
        jnp.stack([theirs, values], axis),
    )


def gather_beside(one, two, groups, chunks, beside):
    place = lax.axis_index("fsdp")
    order_one, order_two = bit_orders(groups)
    order_one, order_two = order_one + [0], order_two + [0]
    swapped, late = [], []
    for at, (bit_one, bit_two) in enumerate(zip(order_one, order_two)):
        left = len(order_one) - at
        take = chunks[: -(-len(chunks) // left)] if len(chunks) >= left else []
        chunks = chunks[len(take) :]
        theirs = [across(one, groups, bit_one), across(two, groups, bit_two)]
        theirs += [swap(chunk) for chunk in take]
        if at == 1:
            theirs, beside = lax.optimization_barrier((theirs, beside))
        else:
            theirs = lax.optimization_barrier(theirs)
        if at == len(order_one) - 2:
            late = theirs[:2]
        one = merged(one, theirs[0], place, order_one[:at], bit_one)
        two = merged(two, theirs[1], place, order_two[:at], bit_two)
        swapped += theirs[2:]
    bits = len(order_one)
    return (
        one.reshape((-1,) + one.shape[bits + 1 :]),
        two.reshape((-1,) + two.shape[bits + 1 :]),
        swapped,
        beside,
        late,
    )


def shuffle(count, lanes):
    take = jnp.arange(count * lanes)[:, None]
    give = jnp.arange(count * lanes)[None, :]
    return ((take % lanes) * count + take // lanes == give).astype(BF)


def pad_to(values, count):
    return jnp.pad(values, (0, count - values.shape[0]))


def shards(
    hidden,
    query_in,
    memory,
    segment_ids,
    block_order,
    memory_valid,
    w_query,
    w_key,
    w_value,
    w_out,
    w_rel,
    rel_biases,
    seg_embed,
    w_inner,
    b_inner,
    w_outer,
    b_outer,
    norm_gains,
    norm_biases,
    grad_hidden_out,
    grad_query_out,
):
    side = lax.axis_index("seq")
    groups = lax.axis_size("fsdp")
    place_at = lax.axis_index("fsdp")
    half, width = hidden.shape[1:]
    target_half = query_in.shape[1]
    memory_half = memory.shape[1]
    head_width = w_rel.shape[1]
    shard_rows = w_query.shape[0]
    ffn_width = w_inner.shape[1]
    own_rows = half + target_half

    def by_side(own, other, axis):
        return jnp.where(
            side == 0,
            jnp.concatenate([own, other], axis),
            jnp.concatenate([other, own], axis),
        )

    pairs = head_width // LANES
    pair_width = 3 * LANES

    def head_columns(weight, pair):
        return lax.dynamic_slice_in_dim(weight, side * head_width + pair * LANES, LANES, 1)

    def pair_columns(pair):
        return [head_columns(weight, pair) for weight in (w_query, w_key, w_value)]

    order = block_order[0]
    segs = segment_ids[0]
    target_seg = lax.dynamic_slice_in_dim(segs, MEM + order[NBLK - 1] * BLOCK, BLOCK)
    seg_rows = jnp.concatenate([segs[MEM:], target_seg, segs[:MEM]])
    invalid = jnp.concatenate([jnp.zeros((MROW,), jnp.int32), (memory_valid[0] != 1).astype(jnp.int32)])
    lane = jnp.arange(LANES)[None, :]
    marks = jnp.where(lane < 6, seg_rows[:, None] == lane % 3, (lane == 6) | (lane == 7))
    marks = jnp.where(lane == 8, invalid[:, None] == 1, marks).astype(BF)

    pos_table = sinusoid(REL_ROWS, width, MEM + L - 1).astype(BF)
    few = jnp.concatenate([rel_biases, seg_embed], 0)
    few = jnp.pad(few, ((0, shard_rows - 5), (0, LANES - few.shape[1])))
    quarter = half // 2
    weights_one, weights_two, swapped, (pos_table, marks), late = gather_beside(
        jnp.concatenate(sum([pair_columns(pair) for pair in range(pairs - 1)], []), 1),
        jnp.concatenate(pair_columns(pairs - 1) + [w_rel, few], 1),
        groups,
        [hidden[0, :quarter], hidden[0, quarter:], memory[0], query_in[0]],
        (pos_table, marks),
    )
    rel_weight = weights_two[:, pair_width : pair_width + head_width]
    few_all = weights_two[:, pair_width + head_width :].reshape(groups, shard_rows, LANES)
    few_all = few_all[:, :5, : head_width // groups].astype(F32)
    few_all = few_all.transpose(1, 0, 2).reshape(5, head_width)

    blocks = ffn_width // width
    spots = shuffle(blocks, LANES)
    smalls = (b_inner, b_outer, norm_gains, norm_biases)
    small_flat = pad_to(jnp.concatenate([t.reshape(-1) for t in smalls]), shard_rows * LANES)
    inner_moved = lax.dot_general(
        w_inner.reshape(shard_rows, -1, blocks * LANES),
        spots,
        (((2,), (1,)), ((), ())),
        preferred_element_type=F32,
    ).astype(BF)
    inner_moved = inner_moved.reshape(shard_rows, -1, blocks, LANES).transpose(0, 2, 1, 3)
    mixed = jnp.concatenate(
        [
            w_out,
            inner_moved.reshape(shard_rows, ffn_width),
            w_outer.reshape(shard_rows, ffn_width),
            small_flat.reshape(shard_rows, LANES),
        ],
        1,
    )
    mixed, _ = lax.optimization_barrier((mixed, late))
    mixed = lax.all_gather(mixed, "fsdp", axis=0, tiled=True)
    small_all = mixed[:, width + 2 * ffn_width :].reshape(groups, shard_rows * LANES).astype(F32)

    def unpack():
        found, at = [], 0
        for small in smalls:
            piece = small_all[:, at : at + small.size].reshape((groups,) + small.shape)
            found.append(jnp.moveaxis(piece, 0, -2).reshape(small.shape[:-1] + (-1,)))
            at += small.size
        return found

    inner_bias, outer_bias, gains, shifts = unpack()

    cuts = ((0, half), (half, own_rows))
    far_hidden = jnp.concatenate(swapped[:2], 0)
    stacked = jnp.concatenate(
        [
            by_side(hidden[0], far_hidden, 0),
            by_side(query_in[0], swapped[3], 0),
            by_side(memory[0], swapped[2], 0),
        ],
        0,
    )

    qkv_one = product(stacked, weights_one).astype(BF)
    qkv_two = product(stacked, weights_two[:, :pair_width]).astype(BF)
    rel = product(pos_table, rel_weight).astype(BF)
    par = jnp.concatenate([few_all, jnp.zeros((3, head_width), F32)], 0)
    def rows_of(values, which):
        return jnp.concatenate(
            [
                lax.dynamic_slice_in_dim(values, which * half, half, 0),
                lax.dynamic_slice_in_dim(values, L + which * target_half, target_half, 0),
            ],
            0,
        )

    def pair_args(pair):
        last = pair == pairs - 1
        at = (0, qkv_two) if last else (3 * pair, qkv_one)
        return (pair, at[0], order, at[1], rel, marks, par)

    kept = []
    own_att, far_att = [], []
    for pair in range(pairs):
        att, exps, inverse = attention_forward(*pair_args(pair))
        kept.append((att, inverse, exps))
        own_att.append(rows_of(att, side))
        far_att.append(swap(rows_of(att, 1 - side)))
    attn_rows = by_side(jnp.concatenate(own_att, 1), jnp.concatenate(far_att, 1), 1)
    small = jnp.stack([gains[0], shifts[0], gains[1], shifts[1], outer_bias] + [outer_bias] * 3)
    devices = 2 * groups
    out_rows = width // devices
    dealt_rows = out_rows % 8 == 0
    result, grad_sum_one, grad_weights, grad_b_inner, grad_small, *grad_attn = middle(
        groups if dealt_rows else None,
        side.astype(jnp.int32)[None],
        attn_rows,
        hidden[0],
        query_in[0],
        grad_hidden_out[0],
        grad_query_out[0],
        mixed,
        inner_bias.reshape(width, blocks).T.reshape(1, ffn_width),
        small,
    )

    if dealt_rows:
        token_sums = lax.psum_scatter(grad_weights, "fsdp", scatter_dimension=0, tiled=True)
        token_sums = token_sums.reshape(2, out_rows, -1)
        near_sums = lax.dynamic_index_in_dim(token_sums, side, 0, True)
        far_sums = swap(lax.dynamic_index_in_dim(token_sums, 1 - side, 0, True))
        token_sums = jnp.concatenate([near_sums, far_sums], 0)
    else:
        token_sums = lax.psum_scatter(
            grad_weights, ("seq", "fsdp"), scatter_dimension=0, tiled=True
        )[None]
    grad_b_inner = grad_b_inner.reshape(blocks, width).T.reshape(devices, -1)
    row_count = width // devices
    token_flat = jnp.concatenate(
        [
            grad_b_inner.reshape(devices, -1),
            grad_small[:5].reshape(5, devices, -1).transpose(1, 0, 2).reshape(devices, -1),
        ],
        1,
    )
    inner_count = ffn_width // devices

    weights_two = weights_two[:, :pair_width]
    weights_one, weights_two, attn_rows = lax.optimization_barrier(
        (weights_one, weights_two, attn_rows)
    )
    far_one, far_two = swap(weights_one), swap(weights_two)

    far_grads = [swap(grad_attn[pairs + pair]) for pair in range(pairs)]

    core = place_at % 2
    same_core = [[at for at in range(groups) if at % 2 == which] for which in range(2)]

    def core_pieces(parts, which):
        parts = [part.reshape((groups // 2, 2) + part.shape[1:]) for part in parts]
        parts = [lax.dynamic_index_in_dim(part, which, 1, False) for part in parts]
        message = jnp.concatenate(parts[:2], 2)
        return jnp.concatenate([message] + parts[2:], 1) if parts[2:] else message

    def core_message(parts):
        far = across(core_pieces(parts, 1 - core), groups, 0)
        near = core_pieces(parts, core)
        return (near.astype(F32) + far.astype(F32)).astype(BF)

    def sum_message(message):
        message = lax.all_to_all(
            message,
            "fsdp",
            split_axis=0,
            concat_axis=0,
            tiled=True,
            axis_index_groups=same_core,
        )
        return jnp.sum(message.astype(F32), 0)

    own_rows_grads, far_rows_grads, sums, few_grads = [], [], [], []
    for pair in range(pairs):
        own, far = grad_attn[pair], far_grads[pair]
        if pair:
            own, message, sums = lax.optimization_barrier((own, message, sums))
            sums.append(sum_message(message))
        dqkv, drel, dpar = attention_backward(*pair_args(pair), side, own, far, *kept[pair])
        if pair:
            dqkv, drel, sums = lax.optimization_barrier((dqkv, drel, sums))
        few_grads.append(dpar[:5])
        own_rows_grads.append(rows_of(dqkv, side))
        far_rows_grads.append(swap(rows_of(dqkv, 1 - side)))
        grad_pair = inner_cols(stacked, dqkv).astype(BF)
        grad_pair = grad_pair.reshape(2, groups, out_rows, pair_width).transpose(1, 0, 2, 3)
        parts = [
            grad_pair.reshape(groups, shard_rows, pair_width),
            inner_cols(pos_table, drel).astype(BF).reshape(groups, shard_rows, LANES),
        ]
        if pair == 0:
            token_flat = token_flat.reshape(2, groups, -1).transpose(1, 0, 2).astype(BF)
            extra = ((0, 0), (0, 6), (0, pair_width + LANES - token_flat.shape[2]))
            parts.append(jnp.pad(token_flat, extra))
        if pair == pairs - 1:
            few = jnp.concatenate(few_grads, 1).reshape(5, groups, head_width // groups)
            few = few.transpose(1, 0, 2).reshape(groups, 1, -1).astype(BF)
            few = jnp.pad(few, ((0, 0), (0, 7), (0, pair_width + LANES - few.shape[2])))
            parts.append(few)
        message = core_message(parts)
    sums.append(sum_message(message))
    sums, token_sums = lax.optimization_barrier((sums, token_sums))
    shares = token_sums.shape[0]
    plain = jnp.sum(token_sums.astype(F32), 0)
    out_out = plain[:, :width]
    out_outer = plain[:, width + ffn_width :].reshape(blocks * out_rows, width)
    inner_sums = token_sums[:, :, width : width + ffn_width]
    inner_sums = inner_sums.reshape(shares, out_rows, blocks, -1, LANES).transpose(1, 3, 0, 2, 4)
    out_inner = product(
        inner_sums.reshape(out_rows, -1, shares * blocks * LANES),
        jnp.concatenate([spots] * shares, 0),
    ).reshape(out_rows, ffn_width)

    early = slice(0, pairs - 1)
    grad_own = grad_sum_one + inner_rows(
        jnp.concatenate(own_rows_grads + far_rows_grads[early], 1),
        jnp.concatenate([weights_one, weights_two, far_one], 1),
    )
    grad_own = grad_own + inner_rows(far_rows_grads[-1], far_two)

    both_sums = jnp.concatenate([t[:shard_rows, :pair_width] for t in sums], 1)
    own_sum = lax.dynamic_slice_in_dim(both_sums, side * out_rows, out_rows, 0)
    far_sum = lax.dynamic_slice_in_dim(both_sums, (1 - side) * out_rows, out_rows, 0)
    far_sum = swap(far_sum.astype(BF)).astype(F32)
    small_sums = lax.dynamic_index_in_dim(sums[0], shard_rows + side, 0, False)
    small_sums += swap(
        lax.dynamic_index_in_dim(sums[0], shard_rows + 1 - side, 0, False).astype(BF)
    ).astype(F32)
    out_b_inner = small_sums[:inner_count]
    out_rest = small_sums[inner_count : inner_count + 5 * row_count].reshape(5, row_count)
    out_gains, out_shifts, out_b_outer = out_rest[0:4:2], out_rest[1:4:2], out_rest[4]

    def weight_rows(values, which):
        return [
            values[:, pair * pair_width + which * LANES :][:, :LANES] for pair in range(pairs)
        ]

    out_query, out_key, out_value = (
        by_side(
            jnp.concatenate(weight_rows(own_sum, which), 1),
            jnp.concatenate(weight_rows(far_sum, which), 1),
            1,
        )
        for which in range(3)
    )
    out_rel = jnp.concatenate([t[:shard_rows, pair_width:] for t in sums], 1)
    few_sum = sums[-1][shard_rows, : 5 * (head_width // groups)].reshape(5, -1)
    out_biases, out_seg = few_sum[:3], few_sum[3:]
    return (
        result[None, :half],
        result[None, half:],
        grad_own[None, :half],
        grad_own[None, half:],
        out_query,
        out_key,
        out_value,
        out_out,
        out_rel,
        out_biases,
        out_seg,
        out_inner,
        out_b_inner,
        out_outer,
        out_b_outer,
        out_gains,
        out_shifts,
    )


def solution(mesh):
    rows = P("fsdp", "seq", None)
    both = ("seq", "fsdp")
    in_specs = (
        (rows,) * 3
        + (P("fsdp", None),) * 7
        + (P("fsdp", "seq"), P(None, both), P(None, both))
        + (P("fsdp", None), P("fsdp"), P("fsdp", None), P("fsdp"))
        + (P(None, "fsdp"), P(None, "fsdp"))
        + (rows,) * 2
    )
    out_specs = (
        (rows,) * 4
        + (P(both, None),) * 4
        + (P("fsdp", "seq"), P(None, both), P(None, both))
        + (P(both, None), P(both), P(both, None), P(both))
        + (P(None, both), P(None, both))
    )
    return jax.shard_map(shards, mesh=mesh, in_specs=in_specs, out_specs=out_specs, check_vma=False)
```

```python
import functools

import jax
import jax.numpy as jnp
from jax import lax
from jax.experimental import pallas as pl
from jax.experimental.pallas import tpu as pltpu
from jax.sharding import PartitionSpec as P

DH = 64
BLOCK = 256
NBLK = 4
MEM = 384
L = 1024
LANES = 128

QROW = L
MROW = L + BLOCK
ROWS = L + BLOCK + MEM
KEYS = MEM + L
SPAN_M = MEM + BLOCK
SPAN_T = 2 * BLOCK
REL_M = L - BLOCK
REL_T = MEM + L - BLOCK
REL_ROWS = MEM + 2 * L
SPANS = SPAN_M + NBLK * SPAN_T

EPSILON = 1e-05
NEGATIVE = -1e30
SCORE_SCALE = 0.125
EXP2_SCALE = SCORE_SCALE * 1.4426950408889634
STEPS = NBLK + 1
VMEM_LIMIT = 60 * 1024 * 1024
BF = jnp.bfloat16
F32 = jnp.float32


def product(left, right):
    return jnp.dot(left, right, preferred_element_type=F32)


def inner_rows(left, right):
    return lax.dot_general(left, right, (((1,), (1,)), ((), ())), preferred_element_type=F32)


def inner_cols(left, right):
    return lax.dot_general(left, right, (((0,), (0,)), ((), ())), preferred_element_type=F32)


def sinusoid(row_count, width_all, farthest):
    fine = DH
    frequency = 10000.0 ** (-jnp.arange(0, width_all, 2).astype(F32) / width_all)
    starts = (farthest - fine * jnp.arange(row_count // fine)).astype(F32)
    far = starts[:, None, None] * frequency
    near = jnp.arange(fine).astype(F32)[None, :, None] * frequency
    sines = jnp.sin(far) * jnp.cos(near) - jnp.cos(far) * jnp.sin(near)
    cosines = jnp.cos(far) * jnp.cos(near) + jnp.sin(far) * jnp.sin(near)
    return jnp.concatenate([sines, cosines], 2).reshape(row_count, width_all)


def split_low(values):
    high = values.astype(BF).astype(F32)
    return high, values - high


def place(step, order_ref):
    last = jnp.minimum(step, NBLK - 1)
    block = order_ref[last]
    row = jnp.where(step < NBLK, block, NBLK) * BLOCK
    return block, pl.multiple_of(row, BLOCK), last


def row_terms(q_ref, kx_ref, par_ref, row):
    query = q_ref[pl.ds(row, BLOCK), :].astype(F32)
    marks = kx_ref[pl.ds(row, BLOCK), :].astype(F32)
    return query + par_ref[0:1, :], query + par_ref[1:2, :], query + par_ref[2:3, :], marks


def gather_keys(order_ref, from_ref, to_ref, lanes):
    to_ref[:MEM, lanes] = from_ref[MROW:, :]
    for at in range(NBLK):
        rows = pl.ds(pl.multiple_of(BLOCK * order_ref[at], BLOCK), BLOCK)
        to_ref[MEM + BLOCK * at : MEM + BLOCK * (at + 1), lanes] = from_ref[rows, :]


def key_spots(order_ref, block, count):
    spots = [(0, MEM, pl.multiple_of(REL_M - BLOCK * block, BLOCK), 0)]
    for at in range(count):
        rel_row = pl.multiple_of(REL_T + BLOCK * (order_ref[at] - block), LANES)
        spots.append((MEM + BLOCK * at, BLOCK, rel_row, SPAN_M + SPAN_T * at))
    return spots


def gather_spans(spots, rel_ref, span_ref):
    for _, key_count, rel_row, put in spots:
        span = key_count + BLOCK
        span_ref[put : put + span, :] = rel_ref[pl.ds(rel_row, span), :]


def forward_kernel(
    order_ref,
    q_ref,
    k_ref,
    v_ref,
    rel_ref,
    kx_ref,
    par_ref,
    att_ref,
    exp_ref,
    inv_ref,
    kcat_ref,
    vcat_ref,
    score_ref,
    lhs_ref,
    qr_ref,
    span_ref,
    sum_ref,
):
    step = pl.program_id(0)

    @pl.when(step == 0)
    def _():
        gather_keys(order_ref, k_ref, kcat_ref, slice(0, LANES))
        gather_keys(order_ref, kx_ref, kcat_ref, slice(LANES, 2 * LANES))
        gather_keys(order_ref, v_ref, vcat_ref, slice(0, LANES))
        vcat_ref[:, LANES:] = jnp.ones((KEYS, LANES), BF)

    block, row, last = place(step, order_ref)
    lane = lax.broadcasted_iota(jnp.int32, (BLOCK, LANES), 1)
    query_w, query_r, query_s, marks = row_terms(q_ref, kx_ref, par_ref, row)
    same, other = query_s * par_ref[3:4, :], query_s * par_ref[4:5, :]
    for head in range(2):
        mine = (lane < DH) == (head == 0)
        other_sum = jnp.sum(jnp.where(mine, other, 0.0), -1, keepdims=True)
        diff = jnp.sum(jnp.where(mine, same, 0.0), -1, keepdims=True) - other_sum
        diff_high, diff_low = split_low(diff)
        other_high, other_low = split_low(other_sum)
        extra = jnp.where(lane < 3, marks * diff_high, jnp.where(lane < 6, marks * diff_low, 0.0))
        extra = jnp.where(lane == 6, other_high, jnp.where(lane == 7, other_low, extra))
        extra = jnp.where(lane == 8, NEGATIVE, extra)
        lhs_ref[head, :, :LANES] = jnp.where(mine, query_w, 0.0).astype(BF)
        lhs_ref[head, :, LANES:] = extra.astype(BF)
        qr_ref[head] = jnp.where(mine, query_r, 0.0).astype(BF)

    across = lax.broadcasted_iota(jnp.int32, (BLOCK, BLOCK), 0) - lax.broadcasted_iota(
        jnp.int32, (BLOCK, BLOCK), 1
    )
    hidden_at = jnp.where(step < NBLK, BLOCK, 0)

    for count in range(NBLK):

        @pl.when(last == count)
        def _():
            spots = key_spots(order_ref, block, count + 1)
            keys = MEM + BLOCK * (count + 1)
            spans = SPAN_M + SPAN_T * (count + 1)
            gather_spans(spots, rel_ref, span_ref)
            for head in range(2):
                content = inner_rows(lhs_ref[head], kcat_ref[:keys, :])
                position = inner_rows(qr_ref[head], span_ref[:spans, :])
                top = None
                for at, key_count, _, put in spots:
                    span = key_count + BLOCK
                    moved = position[:, put : put + span]
                    moved = pltpu.roll(moved, span - BLOCK + 1, 1, stride=1, stride_axis=0)
                    tile = content[:, at : at + key_count] + moved[:, :key_count]
                    if at + key_count == keys:
                        tile = jnp.where(across == hidden_at, NEGATIVE, tile)
                    score_ref[head, :, at : at + key_count] = tile
                    for piece in range(0, key_count, LANES):
                        part = tile[:, piece : piece + LANES]
                        top = part if top is None else jnp.maximum(top, part)
                peak = jnp.max(top, -1, keepdims=True)
                low = jnp.exp2((score_ref[head, :, :keys] - peak) * EXP2_SCALE).astype(BF)
                exp_ref[head, :, :keys] = low
                sum_ref[head] = product(low, vcat_ref[:keys, :])

    sums = sum_ref[0], sum_ref[1]
    first = lane < DH
    inverse = 1.0 / jnp.where(first, sums[0][:, LANES:], sums[1][:, LANES:])
    total = jnp.where(first, sums[0][:, :LANES], sums[1][:, :LANES])
    att_ref[pl.ds(row, BLOCK), :] = (total * inverse).astype(BF)
    inv_ref[pl.ds(row, BLOCK), :] = inverse


def backward_kernel(
    order_ref,
    q_ref,
    k_ref,
    v_ref,
    rel_ref,
    kx_ref,
    par_ref,
    near_ref,
    far_ref,
    att_ref,
    inv_ref,
    exp_ref,
    dqkv_ref,
    drel_ref,
    dpar_ref,
    kcat_ref,
    vcat_ref,
    flip_ref,
    lhs_ref,
    qwt_ref,
    qrt_ref,
    gt_ref,
    dkt_ref,
    dvt_ref,
    drelt_ref,
    accw_ref,
    accr_ref,
    span_ref,
    moved_ref,
    grad_ref,
):
    step = pl.program_id(0)

    @pl.when(step == 0)
    def _():
        gather_keys(order_ref, k_ref, kcat_ref, slice(0, LANES))
        gather_keys(order_ref, kx_ref, kcat_ref, slice(LANES, 2 * LANES))
        gather_keys(order_ref, v_ref, vcat_ref, slice(0, LANES))
        vcat_ref[:, :LANES] = (vcat_ref[:, :LANES].astype(F32) * SCORE_SCALE).astype(BF)
        vcat_ref[:, LANES:] = jnp.full((KEYS, LANES), SCORE_SCALE, BF)
        half, part = L // 2, BLOCK // 2
        for from_ref, which in ((near_ref, order_ref[NBLK]), (far_ref, 1 - order_ref[NBLK])):
            rows_at = pl.multiple_of(which * half, half)
            grad_ref[pl.ds(rows_at, half), :] = from_ref[:half, :]
            rows_at = pl.multiple_of(QROW + which * part, part)
            grad_ref[pl.ds(rows_at, part), :] = from_ref[half:, :]
        up = lax.broadcasted_iota(jnp.int32, (BLOCK, BLOCK), 0)
        down = lax.broadcasted_iota(jnp.int32, (BLOCK, BLOCK), 1)
        flip_ref[...] = jnp.where(up + down == BLOCK - 1, 1.0, 0.0).astype(BF)
        dkt_ref[...] = jnp.zeros_like(dkt_ref)
        dvt_ref[...] = jnp.zeros_like(dvt_ref)
        drelt_ref[...] = jnp.zeros_like(drelt_ref)
        dpar_ref[...] = jnp.zeros_like(dpar_ref)

    block, row, last = place(step, order_ref)
    lane = lax.broadcasted_iota(jnp.int32, (BLOCK, LANES), 1)
    first = lane < DH
    flip = flip_ref[...]
    rows = pl.ds(row, BLOCK)
    grad_low = (grad_ref[rows, :].astype(F32) * inv_ref[rows, :]).astype(BF)
    query, marks = product(flip, q_ref[rows, :]), product(flip, kx_ref[rows, :])
    grad, att = product(flip, grad_low), product(flip, att_ref[rows, :])
    query_w = query + par_ref[0:1, :]
    query_r = query + par_ref[1:2, :]
    query_s = query + par_ref[2:3, :]
    dots = grad * att
    for head in range(2):
        mine = first == (head == 0)
        high, low = split_low(-jnp.sum(jnp.where(mine, dots, 0.0), -1, keepdims=True))
        extra = jnp.where(lane == 0, high, jnp.where(lane == 1, low, 0.0))
        lhs_ref[head, :, :LANES] = jnp.where(mine, grad, 0.0).astype(BF)
        lhs_ref[head, :, LANES:] = extra.astype(BF)
    qwt_ref[...] = query_w.astype(BF).astype(F32).T.astype(BF)
    qrt_ref[...] = query_r.astype(BF).astype(F32).T.astype(BF)
    gt_ref[...] = grad_low.astype(F32).T.astype(BF)

    for count in range(NBLK):

        @pl.when(last == count)
        def _():
            spots = key_spots(order_ref, block, count + 1)
            keys = MEM + BLOCK * (count + 1)
            spans = SPAN_M + SPAN_T * (count + 1)
            gather_spans(spots, rel_ref, span_ref)
            for head in range(2):
                own = slice(DH * head, DH * head + DH)
                probs = exp_ref[head, :, :keys]
                slope = inner_rows(lhs_ref[head], vcat_ref[:keys, :])
                scaled = (product(flip, probs) * slope).astype(BF)
                for at, key_count, _, put in spots:
                    span = key_count + BLOCK
                    moved = jnp.concatenate(
                        [scaled[:, at : at + key_count], jnp.zeros((BLOCK, BLOCK), BF)], 1
                    )
                    moved_ref[head, :, put : put + span] = pltpu.roll(
                        moved, 0, 1, stride=1, stride_axis=0
                    )
                dkt_ref[own, :keys] += product(qwt_ref[own, :], scaled)
                dvt_ref[own, :keys] += product(gt_ref[own, :], probs)
                accw_ref[head] = product(scaled, kcat_ref[:keys, :])
                accr_ref[head] = product(moved_ref[head, :, :spans], span_ref[:spans, :])
                drel = product(qrt_ref[own, :], moved_ref[head, :, :spans])
                for _, key_count, rel_row, put in spots:
                    span = key_count + BLOCK
                    drelt_ref[own, pl.ds(rel_row, span)] += drel[:, put : put + span]

    grad_w = jnp.where(first, accw_ref[0, :, :LANES], accw_ref[1, :, :LANES])
    grad_r = jnp.where(first, accr_ref[0], accr_ref[1])
    same_sums, other_sums = [], []
    for head in range(2):
        sums = accw_ref[head, :, LANES:]
        same_sums.append(jnp.sum(jnp.where(lane < 3, marks * sums, 0.0), -1, keepdims=True))
        total = jnp.sum(jnp.where(lane == 6, sums, 0.0), -1, keepdims=True)
        other_sums.append(total - same_sums[head])
    same = jnp.where(first, same_sums[0], same_sums[1])
    other = jnp.where(first, other_sums[0], other_sums[1])
    grad_s = same * par_ref[3:4, :] + other * par_ref[4:5, :]
    high, low = split_low(grad_w + grad_r + grad_s)
    dqkv_ref[rows, :LANES] = (
        product(flip, high.astype(BF)) + product(flip, low.astype(BF))
    ).astype(BF)
    for at, terms in enumerate((grad_w, grad_r, grad_s, same * query_s, other * query_s)):
        dpar_ref[at : at + 1, :] += jnp.sum(terms, 0, keepdims=True)

    @pl.when(step == STEPS - 1)
    def _():
        dqkv_ref[MROW:, :LANES] = jnp.zeros((MEM, LANES), BF)
        dqkv_ref[L:MROW, LANES:] = jnp.zeros((BLOCK, 2 * LANES), BF)
        for lanes, from_ref in ((1, dkt_ref), (2, dvt_ref)):
            lanes = slice(lanes * LANES, (lanes + 1) * LANES)
            dqkv_ref[MROW:, lanes] = from_ref[:, :MEM].T.astype(BF)
            for at in range(NBLK):
                rows_at = pl.ds(pl.multiple_of(BLOCK * order_ref[at], BLOCK), BLOCK)
                start = MEM + BLOCK * at
                dqkv_ref[rows_at, lanes] = from_ref[:, start : start + BLOCK].T.astype(BF)
        drel_ref[...] = drelt_ref[...].T.astype(BF)


def column(rows, at):
    return pl.BlockSpec((rows, LANES), lambda step, order: (0, at))


def attention_specs(pair, first):
    ins = [column(ROWS, first + at) for at in range(3)]
    ins += [column(REL_ROWS, pair), column(ROWS, 0), column(8, pair)]
    exps = pl.BlockSpec((None, 2, BLOCK, KEYS), lambda step, order: (step, 0, 0, 0))
    return ins, exps


def settings(passes):
    return dict(
        compiler_params=pltpu.CompilerParams(
            dimension_semantics=("arbitrary",), vmem_limit_bytes=40 * 1024 * 1024
        ),
        cost_estimate=pl.CostEstimate(
            flops=passes * 4 * MROW * KEYS * BLOCK,
            bytes_accessed=STEPS * 2 * BLOCK * KEYS * 2,
            transcendentals=2 * MROW * KEYS,
        ),
    )


def attention_forward(pair, first, order, qkv, rel, marks, par):
    ins, exps = attention_specs(pair, first)
    qkv, rel = (pltpu.with_memory_space_constraint(t, pltpu.HBM) for t in (qkv, rel))
    return pl.pallas_call(
        forward_kernel,
        grid_spec=pltpu.PrefetchScalarGridSpec(
            num_scalar_prefetch=1,
            grid=(STEPS,),
            in_specs=ins,
            out_specs=[column(MROW, 0), exps, column(MROW, 0)],
            scratch_shapes=[
                pltpu.VMEM((KEYS, 2 * LANES), BF),
                pltpu.VMEM((KEYS, 2 * LANES), BF),
                pltpu.VMEM((2, BLOCK, KEYS), F32),
                pltpu.VMEM((2, BLOCK, 2 * LANES), BF),
                pltpu.VMEM((2, BLOCK, LANES), BF),
                pltpu.VMEM((SPANS, LANES), BF),
                pltpu.VMEM((2, BLOCK, 2 * LANES), F32),
            ],
        ),
        out_shape=[
            jax.ShapeDtypeStruct((MROW, LANES), BF),
            pltpu.HBM((STEPS, 2, BLOCK, KEYS), BF),
            jax.ShapeDtypeStruct((MROW, LANES), F32),
        ],
        **settings(16),
    )(order, qkv, qkv, qkv, rel, marks, par)


def attention_backward(pair, first, order, qkv, rel, marks, par, side, near, far, att, inverse, exps_in):
    ins, exps = attention_specs(pair, first)
    order = jnp.concatenate([order, side.astype(order.dtype)[None]])
    qkv, rel, exps_in = (
        pltpu.with_memory_space_constraint(t, pltpu.HBM) for t in (qkv, rel, exps_in)
    )
    return pl.pallas_call(
        backward_kernel,
        grid_spec=pltpu.PrefetchScalarGridSpec(
            num_scalar_prefetch=1,
            grid=(STEPS,),
            in_specs=ins
            + [column(near.shape[0], 0)] * 2
            + [column(MROW, 0)] * 2
            + [exps],
            out_specs=[
                pl.BlockSpec((ROWS, 3 * LANES), lambda step, order: (0, 0)),
                column(REL_ROWS, 0),
                column(8, 0),
            ],
            scratch_shapes=[
                pltpu.VMEM((KEYS, 2 * LANES), BF),
                pltpu.VMEM((KEYS, 2 * LANES), BF),
                pltpu.VMEM((BLOCK, BLOCK), BF),
                pltpu.VMEM((2, BLOCK, 2 * LANES), BF),
                pltpu.VMEM((LANES, BLOCK), BF),
                pltpu.VMEM((LANES, BLOCK), BF),
                pltpu.VMEM((LANES, BLOCK), BF),
                pltpu.VMEM((LANES, KEYS), F32),
                pltpu.VMEM((LANES, KEYS), F32),
                pltpu.VMEM((LANES, REL_ROWS), F32),
                pltpu.VMEM((2, BLOCK, 2 * LANES), F32),
                pltpu.VMEM((2, BLOCK, LANES), F32),
                pltpu.VMEM((SPANS, LANES), BF),
                pltpu.VMEM((2, BLOCK, SPANS), BF),
                pltpu.VMEM((MROW, LANES), BF),
            ],
        ),
        out_shape=[
            jax.ShapeDtypeStruct((ROWS, 3 * LANES), BF),
            jax.ShapeDtypeStruct((REL_ROWS, LANES), BF),
            jax.ShapeDtypeStruct((8, LANES), F32),
        ],
        **settings(24),
    )(order, qkv, qkv, qkv, rel, marks, par, near, far, att, inverse, exps_in)


CHUNKS = 2


def norm_parts(values):
    center = values - jnp.mean(values, -1, keepdims=True)
    spread = jnp.mean(center * center, -1, keepdims=True)
    scale = lax.rsqrt(spread + EPSILON)
    return center * scale, scale


def norm_pull(grad, unit, scale, gain):
    grad = grad * gain
    mean = jnp.mean(grad, -1, keepdims=True)
    slope = jnp.mean(grad * unit, -1, keepdims=True)
    return (grad - mean - unit * slope) * scale


def dealt(values, groups):
    if groups is None:
        return values.astype(BF)
    share = values.shape[0] // (2 * groups)
    pieces = [
        values[(side * groups + at) * share :][:share] for at in range(groups) for side in range(2)
    ]
    return jnp.concatenate(pieces, 0).astype(BF)


def middle_kernel(
    groups,
    side_ref,
    attn_ref,
    hidden_ref,
    query_ref,
    grad_hidden_ref,
    grad_query_ref,
    weights_ref,
    inner_bias_ref,
    small_ref,
    result_ref,
    grad_sum_ref,
    gw_ref,
    gb_inner_ref,
    g_small_ref,
    *rest,
):
    pairs = attn_ref.shape[1] // (2 * LANES)
    near_refs, far_refs, rest = rest[:pairs], rest[pairs : 2 * pairs], rest[2 * pairs :]
    middle_steps(
        groups,
        side_ref,
        attn_ref,
        hidden_ref,
        query_ref,
        grad_hidden_ref,
        grad_query_ref,
        weights_ref,
        inner_bias_ref,
        small_ref,
        result_ref,
        grad_sum_ref,
        gw_ref,
        gb_inner_ref,
        g_small_ref,
        near_refs,
        far_refs,
        *rest,
    )


def middle_steps(
    groups,
    side_ref,
    attn_ref,
    hidden_ref,
    query_ref,
    grad_hidden_ref,
    grad_query_ref,
    weights_ref,
    inner_bias_ref,
    small_ref,
    result_ref,
    grad_sum_ref,
    gw_ref,
    gb_inner_ref,
    g_small_ref,
    near_refs,
    far_refs,
    unit_ref,
    scale_ref,
    low_ref,
    low_t_ref,
    act_ref,
    slope_ref,
    sum_ref,
    grad_ref,
    grad_low_ref,
    back_ref,
    held_ref,
    arrived,
):
    step = pl.program_id(0)
    rows, width = attn_ref.shape
    tiles = act_ref.shape[1] // width
    half = hidden_ref.shape[0]
    cut = rows // CHUNKS
    gain_one, shift_one = small_ref[0:1, :], small_ref[1:2, :]
    gain_two, shift_two = small_ref[2:3, :], small_ref[3:4, :]
    parts = [slice(at * cut, at * cut + cut) for at in range(CHUNKS)]

    def fetch(at):
        columns = pl.ds(pl.multiple_of(at * width, width), width)
        return pltpu.make_async_copy(weights_ref.at[:, columns], held_ref.at[at], arrived.at[at])

    @pl.when(step == 0)
    def _():
        fetch(0).start()
        for at in range(tiles):
            fetch(1 + at).start()
            fetch(1 + tiles + at).start()
        fetch(0).wait()
        sum_ref[...] = product(attn_ref[...], held_ref[0])
        sum_ref[:half, :] += hidden_ref[...].astype(F32)
        sum_ref[half:, :] += query_ref[...].astype(F32)
        for part in parts:
            unit, scale = norm_parts(sum_ref[part, :])
            unit_ref[part, :] = unit
            scale_ref[part, :] = jnp.broadcast_to(scale, (cut, LANES))
            first = unit * gain_one + shift_one
            low_ref[part, :] = first.astype(BF)
            sum_ref[part, :] = first + small_ref[4:5, :]

    place_of = jnp.where(step < tiles, step, jnp.minimum(lax.div(step - tiles, 2), tiles - 1))
    columns = pl.ds(pl.multiple_of(place_of * width, width), width)

    w_inner, w_outer = held_ref.at[1 + place_of], held_ref.at[1 + tiles + place_of]

    @pl.when(step < tiles)
    def _():
        fetch(1 + step).wait()
        fetch(1 + tiles + step).wait()
        for part in parts:
            pre = product(low_ref[part, :], w_inner[...]) + inner_bias_ref[...]
            square = pre * pre
            bend = jnp.tanh(0.7978845608028654 * (pre + 0.044715 * square * pre))
            half_bend = 0.5 + 0.5 * bend
            wide = pre * half_bend
            act = wide.astype(BF)
            act_ref[part, columns] = act
            turn = 1.5957691216057308 + 0.2140644488 * square
            slope_ref[part, columns] = half_bend + wide * (1.0 - half_bend) * turn
            sum_ref[part, :] += product(act, w_outer[...])

    @pl.when(step == tiles - 1)
    def _():
        g_gain = g_shift = g_outer = 0.0
        grad_ref[:half, :] = grad_hidden_ref[...].astype(F32)
        grad_ref[half:, :] = grad_query_ref[...].astype(F32)
        for part in parts:
            unit, scale = norm_parts(sum_ref[part, :])
            result_ref[part, :] = (unit * gain_two + shift_two).astype(BF)
            grad = grad_ref[part, :]
            g_gain += jnp.sum(grad * unit, 0, keepdims=True)
            g_shift += jnp.sum(grad, 0, keepdims=True)
            grad = norm_pull(grad, unit, scale, gain_two)
            low = grad.astype(BF)
            grad_ref[part, :] = grad
            grad_low_ref[part, :] = low
            g_outer += jnp.sum(low.astype(F32), 0, keepdims=True)
        g_small_ref[...] = jnp.zeros_like(g_small_ref)
        g_small_ref[2:3, :] = g_gain
        g_small_ref[3:4, :] = g_shift
        g_small_ref[4:5, :] = g_outer
        low_t_ref[...] = low_ref[...].T

    turn_back = jnp.logical_and(step >= tiles, step < 3 * tiles)

    @pl.when(jnp.logical_and(turn_back, lax.rem(step - tiles, 2) == 0))
    def _():
        g_inner = 0.0
        for part in parts:
            back = inner_rows(grad_low_ref[part, :], w_outer[...])
            low = (back * slope_ref[part, columns]).astype(BF)
            back_ref[part, :] = low
            g_inner += jnp.sum(low.astype(F32), 0, keepdims=True)
            grad_ref[part, :] += inner_rows(low, w_inner[...])
        gb_inner_ref[...] = g_inner
        gw_ref[...] = dealt(product(low_t_ref[...], back_ref[...]), groups)

    @pl.when(jnp.logical_and(turn_back, lax.rem(step - tiles, 2) == 1))
    def _():
        gw_ref[...] = dealt(inner_cols(act_ref[:, columns], grad_low_ref[...]), groups)

    @pl.when(step == 3 * tiles)
    def _():
        g_gain = g_shift = 0.0
        for part in parts:
            unit, scale = unit_ref[part, :], scale_ref[part, 0:1]
            grad = grad_ref[part, :]
            g_gain += jnp.sum(grad * unit, 0, keepdims=True)
            g_shift += jnp.sum(grad, 0, keepdims=True)
            grad = norm_pull(grad, unit, scale, gain_one)
            grad_sum_ref[part, :] = grad
            grad_low_ref[part, :] = grad.astype(BF)
        g_small_ref[0:1, :] = g_gain
        g_small_ref[1:2, :] = g_shift
        gw_ref[...] = dealt(inner_cols(attn_ref[...], grad_low_ref[...]), groups)
        back = inner_rows(grad_low_ref[...], held_ref[0]).astype(BF)
        left = side_ref[0] == 0
        middle_at = width // 2
        for at in range(0, middle_at, LANES):
            near, far = back[:, at : at + LANES], back[:, middle_at + at :][:, :LANES]
            near_refs[at // LANES][...] = jnp.where(left, near, far)
            far_refs[at // LANES][...] = jnp.where(left, far, near)


def middle(groups, side, attn, hidden, query, grad_hidden, grad_query, weights, inner_bias, small):
    rows, width = attn.shape
    tiles = inner_bias.shape[1] // width

    def whole(array):
        return pl.BlockSpec(array.shape, lambda step, side: (0,) * array.ndim)

    def square(at):
        return pl.BlockSpec((width, width), lambda step, side: (0, at(step)))

    def back(step):
        return lax.min(lax.div(lax.max(step - tiles, 0), 2), tiles - 1)

    def tile(step):
        return lax.select(step < tiles, step, back(step))

    def written(step):
        odd = lax.rem(lax.max(step - tiles, 0), 2)
        return lax.select(step == 3 * tiles, 0, 1 + back(step) + tiles * odd)

    outs = [
        jax.ShapeDtypeStruct((rows, width), BF),
        jax.ShapeDtypeStruct((rows, width), F32),
        jax.ShapeDtypeStruct((width, (1 + 2 * tiles) * width), BF),
        jax.ShapeDtypeStruct((1, tiles * width), F32),
        jax.ShapeDtypeStruct((8, width), F32),
    ] + [jax.ShapeDtypeStruct((rows, LANES), BF)] * (width // LANES)
    return pl.pallas_call(
        functools.partial(middle_kernel, groups),
        grid_spec=pltpu.PrefetchScalarGridSpec(
            num_scalar_prefetch=1,
            grid=(1 + 3 * tiles,),
            in_specs=[whole(t) for t in (attn, hidden, query, grad_hidden, grad_query)]
            + [
                pl.BlockSpec(memory_space=pl.ANY),
                pl.BlockSpec((1, width), lambda step, side: (0, tile(step))),
                whole(small),
            ],
            out_specs=[whole(t) for t in outs[:2]]
            + [
                square(written),
                pl.BlockSpec((1, width), lambda step, side: (0, back(step))),
                whole(outs[4]),
            ]
            + [whole(t) for t in outs[5:]],
            scratch_shapes=[
                pltpu.VMEM((rows, width), F32),
                pltpu.VMEM((rows, LANES), F32),
                pltpu.VMEM((rows, width), BF),
                pltpu.VMEM((width, rows), BF),
                pltpu.VMEM((rows, tiles * width), BF),
                pltpu.VMEM((rows, tiles * width), F32),
                pltpu.VMEM((rows, width), F32),
                pltpu.VMEM((rows, width), F32),
                pltpu.VMEM((rows, width), BF),
                pltpu.VMEM((rows, width), BF),
                pltpu.VMEM((1 + 2 * tiles, width, width), BF),
                pltpu.SemaphoreType.DMA((1 + 2 * tiles,)),
            ],
        ),
        out_shape=outs,
        compiler_params=pltpu.CompilerParams(
            dimension_semantics=("arbitrary",), vmem_limit_bytes=VMEM_LIMIT
        ),
        cost_estimate=pl.CostEstimate(
            flops=12 * rows * width * width * tiles,
            bytes_accessed=20 * width * width * tiles,
            transcendentals=rows * width * tiles,
        ),
    )(side, attn, hidden, query, grad_hidden, grad_query, weights, inner_bias, small)


def swap(values):
    return lax.ppermute(values, "seq", [(0, 1), (1, 0)])


def bit_orders(groups):
    high = list(range(groups.bit_length() - 2, 0, -1))
    return high, high[-1:] + high[:-1]


def across(values, groups, bit):
    return lax.ppermute(values, "fsdp", [(i, i ^ (1 << bit)) for i in range(groups)])


def merged(values, theirs, place, held, bit):
    axis = sum(1 for other in held if other > bit)
    return jnp.where(
        (place >> bit) & 1 == 0,
        jnp.stack([values, theirs], axis),
        jnp.stack([theirs, values], axis),
    )


def gather_beside(one, two, groups, chunks, beside):
    place = lax.axis_index("fsdp")
    order_one, order_two = bit_orders(groups)
    order_one, order_two = order_one + [0], order_two + [0]
    swapped, late = [], []
    for at, (bit_one, bit_two) in enumerate(zip(order_one, order_two)):
        left = len(order_one) - at
        take = chunks[: -(-len(chunks) // left)] if len(chunks) >= left else []
        chunks = chunks[len(take) :]
        theirs = [across(one, groups, bit_one), across(two, groups, bit_two)]
        theirs += [swap(chunk) for chunk in take]
        if at == 1:
            theirs, beside = lax.optimization_barrier((theirs, beside))
        else:
            theirs = lax.optimization_barrier(theirs)
        if at == len(order_one) - 2:
            late = theirs[:2]
        one = merged(one, theirs[0], place, order_one[:at], bit_one)
        two = merged(two, theirs[1], place, order_two[:at], bit_two)
        swapped += theirs[2:]
    bits = len(order_one)
    return (
        one.reshape((-1,) + one.shape[bits + 1 :]),
        two.reshape((-1,) + two.shape[bits + 1 :]),
        swapped,
        beside,
        late,
    )


def shuffle(count, lanes):
    take = jnp.arange(count * lanes)[:, None]
    give = jnp.arange(count * lanes)[None, :]
    return ((take % lanes) * count + take // lanes == give).astype(BF)


def pad_to(values, count):
    return jnp.pad(values, (0, count - values.shape[0]))


def shards(
    hidden,
    query_in,
    memory,
    segment_ids,
    block_order,
    memory_valid,
    w_query,
    w_key,
    w_value,
    w_out,
    w_rel,
    rel_biases,
    seg_embed,
    w_inner,
    b_inner,
    w_outer,
    b_outer,
    norm_gains,
    norm_biases,
    grad_hidden_out,
    grad_query_out,
):
    side = lax.axis_index("seq")
    groups = lax.axis_size("fsdp")
    place_at = lax.axis_index("fsdp")
    half, width = hidden.shape[1:]
    target_half = query_in.shape[1]
    memory_half = memory.shape[1]
    head_width = w_rel.shape[1]
    shard_rows = w_query.shape[0]
    ffn_width = w_inner.shape[1]
    own_rows = half + target_half

    def by_side(own, other, axis):
        return jnp.where(
            side == 0,
            jnp.concatenate([own, other], axis),
            jnp.concatenate([other, own], axis),
        )

    pairs = head_width // LANES
    pair_width = 3 * LANES

    def head_columns(weight, pair):
        return lax.dynamic_slice_in_dim(weight, side * head_width + pair * LANES, LANES, 1)

    def pair_columns(pair):
        return [head_columns(weight, pair) for weight in (w_query, w_key, w_value)]

    order = block_order[0]
    segs = segment_ids[0]
    target_seg = lax.dynamic_slice_in_dim(segs, MEM + order[NBLK - 1] * BLOCK, BLOCK)
    seg_rows = jnp.concatenate([segs[MEM:], target_seg, segs[:MEM]])
    invalid = jnp.concatenate([jnp.zeros((MROW,), jnp.int32), (memory_valid[0] != 1).astype(jnp.int32)])
    lane = jnp.arange(LANES)[None, :]
    marks = jnp.where(lane < 6, seg_rows[:, None] == lane % 3, (lane == 6) | (lane == 7))
    marks = jnp.where(lane == 8, invalid[:, None] == 1, marks).astype(BF)

    pos_table = sinusoid(REL_ROWS, width, MEM + L - 1).astype(BF)
    few = jnp.concatenate([rel_biases, seg_embed], 0)
    few = jnp.pad(few, ((0, shard_rows - 5), (0, LANES - few.shape[1])))
    quarter = half // 2
    weights_one, weights_two, swapped, (pos_table, marks), late = gather_beside(
        jnp.concatenate(sum([pair_columns(pair) for pair in range(pairs - 1)], []), 1),
        jnp.concatenate(pair_columns(pairs - 1) + [w_rel, few], 1),
        groups,
        [hidden[0, :quarter], hidden[0, quarter:], memory[0], query_in[0]],
        (pos_table, marks),
    )
    rel_weight = weights_two[:, pair_width : pair_width + head_width]
    few_all = weights_two[:, pair_width + head_width :].reshape(groups, shard_rows, LANES)
    few_all = few_all[:, :5, : head_width // groups].astype(F32)
    few_all = few_all.transpose(1, 0, 2).reshape(5, head_width)

    blocks = ffn_width // width
    spots = shuffle(blocks, LANES)
    smalls = (b_inner, b_outer, norm_gains, norm_biases)
    small_flat = pad_to(jnp.concatenate([t.reshape(-1) for t in smalls]), shard_rows * LANES)
    inner_moved = lax.dot_general(
        w_inner.reshape(shard_rows, -1, blocks * LANES),
        spots,
        (((2,), (1,)), ((), ())),
        preferred_element_type=F32,
    ).astype(BF)
    inner_moved = inner_moved.reshape(shard_rows, -1, blocks, LANES).transpose(0, 2, 1, 3)
    mixed = jnp.concatenate(
        [
            w_out,
            inner_moved.reshape(shard_rows, ffn_width),
            w_outer.reshape(shard_rows, ffn_width),
            small_flat.reshape(shard_rows, LANES),
        ],
        1,
    )
    mixed, _ = lax.optimization_barrier((mixed, late))
    mixed = lax.all_gather(mixed, "fsdp", axis=0, tiled=True)
    small_all = mixed[:, width + 2 * ffn_width :].reshape(groups, shard_rows * LANES).astype(F32)

    def unpack():
        found, at = [], 0
        for small in smalls:
            piece = small_all[:, at : at + small.size].reshape((groups,) + small.shape)
            found.append(jnp.moveaxis(piece, 0, -2).reshape(small.shape[:-1] + (-1,)))
            at += small.size
        return found

    inner_bias, outer_bias, gains, shifts = unpack()

    cuts = ((0, half), (half, own_rows))
    far_hidden = jnp.concatenate(swapped[:2], 0)
    stacked = jnp.concatenate(
        [
            by_side(hidden[0], far_hidden, 0),
            by_side(query_in[0], swapped[3], 0),
            by_side(memory[0], swapped[2], 0),
        ],
        0,
    )

    qkv_one = product(stacked, weights_one).astype(BF)
    qkv_two = product(stacked, weights_two[:, :pair_width]).astype(BF)
    rel = product(pos_table, rel_weight).astype(BF)
    par = jnp.concatenate([few_all, jnp.zeros((3, head_width), F32)], 0)
    def rows_of(values, which):
        return jnp.concatenate(
            [
                lax.dynamic_slice_in_dim(values, which * half, half, 0),
                lax.dynamic_slice_in_dim(values, L + which * target_half, target_half, 0),
            ],
            0,
        )

    def pair_args(pair):
        last = pair == pairs - 1
        at = (0, qkv_two) if last else (3 * pair, qkv_one)
        return (pair, at[0], order, at[1], rel, marks, par)

    kept = []
    own_att, far_att = [], []
    for pair in range(pairs):
        att, exps, inverse = attention_forward(*pair_args(pair))
        kept.append((att, inverse, exps))
        own_att.append(rows_of(att, side))
        far_att.append(swap(rows_of(att, 1 - side)))
    attn_rows = by_side(jnp.concatenate(own_att, 1), jnp.concatenate(far_att, 1), 1)
    small = jnp.stack([gains[0], shifts[0], gains[1], shifts[1], outer_bias] + [outer_bias] * 3)
    devices = 2 * groups
    out_rows = width // devices
    dealt_rows = out_rows % 8 == 0
    result, grad_sum_one, grad_weights, grad_b_inner, grad_small, *grad_attn = middle(
        groups if dealt_rows else None,
        side.astype(jnp.int32)[None],
        attn_rows,
        hidden[0],
        query_in[0],
        grad_hidden_out[0],
        grad_query_out[0],
        mixed,
        inner_bias.reshape(width, blocks).T.reshape(1, ffn_width),
        small,
    )

    if dealt_rows:
        token_sums = lax.psum_scatter(grad_weights, "fsdp", scatter_dimension=0, tiled=True)
        token_sums = token_sums.reshape(2, out_rows, -1)
        near_sums = lax.dynamic_index_in_dim(token_sums, side, 0, True)
        far_sums = swap(lax.dynamic_index_in_dim(token_sums, 1 - side, 0, True))
        token_sums = jnp.concatenate([near_sums, far_sums], 0)
    else:
        token_sums = lax.psum_scatter(
            grad_weights, ("seq", "fsdp"), scatter_dimension=0, tiled=True
        )[None]
    inner_count = ffn_width // devices

    weights_two = weights_two[:, :pair_width]
    weights_one, weights_two, attn_rows = lax.optimization_barrier(
        (weights_one, weights_two, attn_rows)
    )
    far_one, far_two = swap(weights_one), swap(weights_two)

    far_grads = [swap(grad_attn[pairs + pair]) for pair in range(pairs)]

    core = place_at % 2
    same_core = [[at for at in range(groups) if at % 2 == which] for which in range(2)]

    def core_pieces(parts, which):
        parts = [part.reshape((groups // 2, 2) + part.shape[1:]) for part in parts]
        parts = [lax.dynamic_index_in_dim(part, which, 1, False) for part in parts]
        message = jnp.concatenate(parts[:2], 2)
        return jnp.concatenate([message] + parts[2:], 1) if parts[2:] else message

    def core_message(parts):
        far = across(core_pieces(parts, 1 - core), groups, 0)
        near = core_pieces(parts, core)
        return (near.astype(F32) + far.astype(F32)).astype(BF)

    def sum_message(message):
        message = lax.all_to_all(
            message,
            "fsdp",
            split_axis=0,
            concat_axis=0,
            tiled=True,
            axis_index_groups=same_core,
        )
        return jnp.sum(message.astype(F32), 0)

    own_rows_grads, far_rows_grads, sums, few_grads = [], [], [], []
    for pair in range(pairs):
        own, far = grad_attn[pair], far_grads[pair]
        if pair:
            own, message, sums = lax.optimization_barrier((own, message, sums))
            sums.append(sum_message(message))
        dqkv, drel, dpar = attention_backward(*pair_args(pair), side, own, far, *kept[pair])
        if pair:
            dqkv, drel, sums = lax.optimization_barrier((dqkv, drel, sums))
        few_grads.append(dpar[:5])
        own_rows_grads.append(rows_of(dqkv, side))
        far_rows_grads.append(swap(rows_of(dqkv, 1 - side)))
        grad_pair = inner_cols(stacked, dqkv).astype(BF)
        grad_pair = grad_pair.reshape(2, groups, out_rows, pair_width).transpose(1, 0, 2, 3)
        parts = [
            grad_pair.reshape(groups, shard_rows, pair_width),
            inner_cols(pos_table, drel).astype(BF).reshape(groups, shard_rows, LANES),
        ]
        if pair == 0:
            drel, grad_b_inner, grad_small = lax.optimization_barrier(
                (drel, grad_b_inner, grad_small)
            )
            grad_b_inner = grad_b_inner.reshape(blocks, width).T.reshape(devices, -1)
            row_count = width // devices
            token_flat = jnp.concatenate(
                [
                    grad_b_inner.reshape(devices, -1),
                    grad_small[:5].reshape(5, devices, -1).transpose(1, 0, 2).reshape(devices, -1),
                ],
                1,
            )
            token_flat = token_flat.reshape(2, groups, -1).transpose(1, 0, 2).astype(BF)
            extra = ((0, 0), (0, 6), (0, pair_width + LANES - token_flat.shape[2]))
            parts.append(jnp.pad(token_flat, extra))
        if pair == pairs - 1:
            few = jnp.concatenate(few_grads, 1).reshape(5, groups, head_width // groups)
            few = few.transpose(1, 0, 2).reshape(groups, 1, -1).astype(BF)
            few = jnp.pad(few, ((0, 0), (0, 7), (0, pair_width + LANES - few.shape[2])))
            parts.append(few)
        message = core_message(parts)
    sums.append(sum_message(message))
    sums, token_sums = lax.optimization_barrier((sums, token_sums))
    shares = token_sums.shape[0]
    plain = jnp.sum(token_sums.astype(F32), 0)
    out_out = plain[:, :width]
    out_outer = plain[:, width + ffn_width :].reshape(blocks * out_rows, width)
    inner_sums = token_sums[:, :, width : width + ffn_width]
    inner_sums = inner_sums.reshape(shares, out_rows, blocks, -1, LANES).transpose(1, 3, 0, 2, 4)
    out_inner = product(
        inner_sums.reshape(out_rows, -1, shares * blocks * LANES),
        jnp.concatenate([spots] * shares, 0),
    ).reshape(out_rows, ffn_width)

    early = slice(0, pairs - 1)
    grad_own = grad_sum_one + inner_rows(
        jnp.concatenate(own_rows_grads + far_rows_grads[early], 1),
        jnp.concatenate([weights_one, weights_two, far_one], 1),
    )
    grad_own = grad_own + inner_rows(far_rows_grads[-1], far_two)

    both_sums = jnp.concatenate([t[:shard_rows, :pair_width] for t in sums], 1)
    own_sum = lax.dynamic_slice_in_dim(both_sums, side * out_rows, out_rows, 0)
    far_sum = lax.dynamic_slice_in_dim(both_sums, (1 - side) * out_rows, out_rows, 0)
    far_sum = swap(far_sum.astype(BF)).astype(F32)
    small_sums = lax.dynamic_index_in_dim(sums[0], shard_rows + side, 0, False)
    small_sums += swap(
        lax.dynamic_index_in_dim(sums[0], shard_rows + 1 - side, 0, False).astype(BF)
    ).astype(F32)
    out_b_inner = small_sums[:inner_count]
    out_rest = small_sums[inner_count : inner_count + 5 * row_count].reshape(5, row_count)
    out_gains, out_shifts, out_b_outer = out_rest[0:4:2], out_rest[1:4:2], out_rest[4]

    def weight_rows(values, which):
        return [
            values[:, pair * pair_width + which * LANES :][:, :LANES] for pair in range(pairs)
        ]

    out_query, out_key, out_value = (
        by_side(
            jnp.concatenate(weight_rows(own_sum, which), 1),
            jnp.concatenate(weight_rows(far_sum, which), 1),
            1,
        )
        for which in range(3)
    )
    out_rel = jnp.concatenate([t[:shard_rows, pair_width:] for t in sums], 1)
    few_sum = sums[-1][shard_rows, : 5 * (head_width // groups)].reshape(5, -1)
    out_biases, out_seg = few_sum[:3], few_sum[3:]
    return (
        result[None, :half],
        result[None, half:],
        grad_own[None, :half],
        grad_own[None, half:],
        out_query,
        out_key,
        out_value,
        out_out,
        out_rel,
        out_biases,
        out_seg,
        out_inner,
        out_b_inner,
        out_outer,
        out_b_outer,
        out_gains,
        out_shifts,
    )


def solution(mesh):
    rows = P("fsdp", "seq", None)
    both = ("seq", "fsdp")
    in_specs = (
        (rows,) * 3
        + (P("fsdp", None),) * 7
        + (P("fsdp", "seq"), P(None, both), P(None, both))
        + (P("fsdp", None), P("fsdp"), P("fsdp", None), P("fsdp"))
        + (P(None, "fsdp"), P(None, "fsdp"))
        + (rows,) * 2
    )
    out_specs = (
        (rows,) * 4
        + (P(both, None),) * 4
        + (P("fsdp", "seq"), P(None, both), P(None, both))
        + (P(both, None), P(both), P(both, None), P(both))
        + (P(None, both), P(None, both))
    )
    return jax.shard_map(shards, mesh=mesh, in_specs=in_specs, out_specs=out_specs, check_vma=False)
```
